128 devices in a mesh: row: 16 (over z, y_hi, core), col: 8 (over y_lo, x).
Axes of the slice: x: 4, y: 4 (y_hi: 2, y_lo: 2; y = y_hi * 2 + y_lo), z: 4, core: 2. Of those that a mesh axis runs over, the one named last changes fastest.
Arguments:
- tokens: bfloat16 [32, 1024, 768], P('row', 'col'), may hold values from -6 to 6
- grad_out: bfloat16 [32, 1024, 768], P('row', 'col'), may hold values from -6 to 6
- w_qkv: bfloat16 [768, 2304], replicated, may hold values from -0.21875 to 0.21875
- w_out: bfloat16 [768, 768], replicated, may hold values from -0.21875 to 0.21875
- gain: float32 [768], replicated, may hold values from 0.5 to 1.5
- log_decay_rows: bfloat16 [2, 12, 32, 1024], P(None, None, 'row', 'col'), may hold values from -1 to 0, as said below
- log_decay_cols: bfloat16 [2, 12, 1024, 32], P(None, None, ('col', 'row')), may hold values from -1 to 0, as said below
- border_cols: int32 [1024], replicated, may hold values 0 or 1
- border_rows: int32 [32], replicated, may hold values 0 or 1
Outputs:
- grad_tokens: bfloat16 [32, 1024, 768], P('row', 'col')
- grad_qkv_weight: float32 [768, 2304], P(('row', 'col'))
- grad_out_weight: float32 [768, 768], P(('row', 'col'))
- grad_gain: float32 [768], P(('row', 'col'))
- grad_decay_rows: bfloat16 [2, 12, 32, 1024], P(None, None, 'row', 'col')
- grad_decay_cols: bfloat16 [2, 12, 1024, 32], P(None, None, ('col', 'row'))
The draws below stay inside these ranges and needn't reach their ends.
Inputs may be any that keep to these rules, and one draw needn't show every extreme that they name: `log_decay_rows`: negative log decay of one scan step. `log_decay_cols`: negative log decay of one scan step. `border_cols`: tile border flags. `border_rows`: tile border flags.
All inputs are finite; a program needn't handle non-finite values.
Results may differ from the reference program's by a relative error of at most 0.014.
Values may be sent and summed in bfloat16 or wider, within the bound.
No kernel may reach another device: no remote copies, remote signals or barrier semaphores. Data moves between devices by JAX's collectives and lax.ppermute only.
A program may use at most 192 MiB of HBM per device.

```python
import functools
import jax
import jax.numpy as jnp
from jax import lax

HEADS = 12
HEAD_DIM = 64
D = 768
ROWS_DEV = 2
COLS_DEV = 128
GRID_H = 32
GRID_W = 1024
TOKENS = 32768


def decay_table(key, line_count, sequence_length, line_block, length_block, slow_share):
    random_subkeys = jax.random.split(key, 7)
    complete_shape = (2, HEADS, line_count, sequence_length)
    head_shape = (2, HEADS, 1, 1)
    slow_heads = jax.random.uniform(random_subkeys[0], head_shape) < slow_share
    slow_rate = jnp.exp(jax.random.uniform(random_subkeys[1], head_shape, minval=jnp.log(0.1), maxval=jnp.log(0.5))) / sequence_length
    fast_rate = jax.random.uniform(random_subkeys[2], head_shape, minval=1.0 / 50.0, maxval=1.0 / 30.0)
    stride_rate = jnp.where(slow_heads, slow_rate, fast_rate)
    uniform_pick = jax.random.uniform(random_subkeys[3], complete_shape)
    patch_factor = 0.5 * 4.0 ** uniform_pick
    window_factor = 0.5 * 4.0 ** jax.random.uniform(random_subkeys[4], (2, HEADS, line_count // line_block, sequence_length // length_block))
    window_factor = jnp.repeat(jnp.repeat(window_factor, line_block, axis=2), length_block, axis=3)
    surge_mask = jax.random.uniform(random_subkeys[5], complete_shape) < 2.0 / sequence_length
    surge_loss = jnp.log(jax.random.uniform(random_subkeys[6], complete_shape, minval=0.5, maxval=0.8))
    return -stride_rate * patch_factor * window_factor + jnp.where(surge_mask, surge_loss, 0.0)


def draw_log_decay_rows(key, part):
    key = jax.random.fold_in(key, 11)
    log_table = decay_table(key, GRID_H, GRID_W, ROWS_DEV, COLS_DEV, 0.5)
    return log_table.astype(jnp.bfloat16)


def draw_log_decay_cols(key, part):
    key = jax.random.fold_in(key, 13)
    log_table = decay_table(key, GRID_W, GRID_H, COLS_DEV, ROWS_DEV, 0.5)
    return log_table.astype(jnp.bfloat16)


def touch_ends(values, stream_key, low, top_value):
    longest = values.shape.index(max(values.shape))
    spots = []
    for shift in (0, 1):
        where = [jax.random.randint(jax.random.fold_in(stream_key, axis), (), 0, length) for axis, length in enumerate(values.shape)]
        where[longest] = (where[longest] + shift) % values.shape[longest]
        spots.append(tuple(where))
    return values.at[spots[0]].set(low).at[spots[1]].set(top_value)


def spiked(array, key, source, target, blocks, factor):
    def block_of(axis_at):
        return (jnp.arange(array.shape[axis_at]) // (array.shape[axis_at] // blocks)).reshape((-1,) + (1,) * (array.ndim - 1 - axis_at))

    near = jax.random.permutation(key, blocks)[block_of(target)]
    second = (block_of(target) + blocks // 2) % blocks
    return jnp.where((block_of(source) == near) | (block_of(source) == second), factor * array, array)


def levels(key, extent, cuts, smallest, top_value):
    factor_of = 1.0
    for axis_at, shards_of in cuts:
        steps = jax.random.uniform(jax.random.fold_in(jax.random.fold_in(key, 6), axis_at), (shards_of,), jnp.float32, smallest / len(cuts), top_value / len(cuts))
        factor_of = factor_of * jnp.repeat(jnp.exp(steps), extent[axis_at] // shards_of).reshape((-1,) + (1,) * (len(extent) - 1 - axis_at))
    return factor_of


def noise(key, extent, scale, reach, shards=(), held_as=jnp.bfloat16):
    values = scale * jax.random.normal(key, extent, jnp.float32)
    if shards:
        values = values * levels(key, extent, shards, -0.22, 0.18)
    return jnp.clip(values, -reach, reach).astype(held_as)


def heavy_noise(rng, dims, width, limit, cuts, heavy, held_as=jnp.bfloat16):
    array = width * jax.random.normal(rng, dims, jnp.float32)
    if cuts:
        array = array * levels(rng, dims, cuts, -0.22, 0.18)
    return jnp.clip(spiked(array, jax.random.fold_in(rng, 3), *heavy), -limit, limit).astype(held_as)


def setup_inputs(seed: int = 0) -> dict:
    key_of = jax.random.split(jax.random.key(seed), 10)
    tokens = heavy_noise(key_of[0], (GRID_H, GRID_W, D), 1.0, 6.0, ((0, 16), (1, 8)), (0, 2, 16, 2.0))
    grad_out = noise(key_of[1], (GRID_H, GRID_W, D), 1.0, 6.0, ((0, 16), (1, 8)))
    w_qkv = noise(key_of[2], (D, 3 * D), D ** -0.5, 0.21875)
    w_out = noise(key_of[3], (D, D), D ** -0.5, 0.21875)
    gain = jnp.clip(1.0 + 0.1 * jax.random.normal(key_of[4], (D,), jnp.float32), 0.5, 1.5)
    log_decay_rows = draw_log_decay_rows(jax.random.fold_in(key_of[9], 71), 0)
    log_decay_cols = draw_log_decay_cols(jax.random.fold_in(key_of[9], 71), 0)
    border_cols = touch_ends((jax.random.randint(key_of[7], (GRID_W,), 0, 2 * COLS_DEV) < 1).astype(jnp.int32), jax.random.fold_in(key_of[7], 1), 0, 1)
    border_rows = touch_ends((jax.random.randint(key_of[8], (GRID_H,), 0, 4 * ROWS_DEV) < 1).astype(jnp.int32), jax.random.fold_in(key_of[8], 1), 0, 1)
    return {"tokens": tokens, "grad_out": grad_out, "w_qkv": w_qkv, "w_out": w_out, "gain": gain, "log_decay_rows": log_decay_rows, "log_decay_cols": log_decay_cols, "border_cols": border_cols, "border_rows": border_rows}


EPSILON = 1e-05
HIGHEST = lax.Precision.HIGHEST

def heads_of(packed, head_count):
    leading = packed.shape[:-1]
    model_width = packed.shape[-1] // 3
    pieces = packed.reshape(leading + (3, head_count, model_width // head_count))
    return (pieces[..., 0, :, :], pieces[..., 1, :, :], pieces[..., 2, :, :])

def reversed_borders(borders):
    return jnp.concatenate([borders[1:], jnp.zeros((1,), jnp.int32)])

def decay_factors(decays, resets):
    log_sums = jnp.cumsum(decays.astype(jnp.float32), axis=-1)
    segment = jnp.cumsum(resets, dtype=jnp.int32)
    entries = jnp.where(segment == 0, jnp.exp(log_sums), 0.0)
    tail_weight = jnp.where(segment == segment[-1], jnp.exp(log_sums[..., -1:] - log_sums), 0.0)
    return (log_sums, segment, entries, tail_weight)

def carry_term(query_wide, entries, carry_in, scaling):
    product = jnp.einsum('lthd,lhde->lthe', query_wide, carry_in, precision=HIGHEST)
    return product * (jnp.swapaxes(entries, 1, 2)[..., None] * scaling)

def state_update(key_wide, value_wide, tail_weight):
    weighted = key_wide * jnp.swapaxes(tail_weight, 1, 2)[..., None]
    return jnp.einsum('lshd,lshe->lhde', weighted, value_wide, precision=HIGHEST)

def block_scan(queries, key_heads, values, decays, resets, carry_in):
    scaling = queries.shape[-1] ** (-0.5)
    log_sums, segment, entries, tail_weight = decay_factors(decays, resets)
    positions = jnp.arange(resets.shape[0], dtype=jnp.int32)
    same_part = (segment[:, None] == segment[None, :]) & (positions[:, None] >= positions[None, :])
    spread = log_sums[..., :, None] - log_sums[..., None, :]
    weights = jnp.where(same_part, jnp.exp(jnp.where(same_part, spread, 0.0)), 0.0)
    query_wide = queries.astype(jnp.float32)
    key_wide = key_heads.astype(jnp.float32)
    value_wide = values.astype(jnp.float32)
    scores = jnp.einsum('lthd,lshd->lhts', query_wide, key_wide, precision=HIGHEST)
    within_block = jnp.einsum('lhts,lshd->lthd', scores * weights * scaling, value_wide, precision=HIGHEST)
    carried = carry_term(query_wide, entries, carry_in, scaling)
    leaving = entries[..., -1][..., None, None] * carry_in + state_update(key_wide, value_wide, tail_weight)
    return (within_block + carried, leaving)

def down_up(projected, planes, border_rows):
    head_count = planes.shape[1]
    queries, key_heads, values = heads_of(jnp.swapaxes(projected, 0, 1), head_count)
    head_dim = queries.shape[-1]
    zero_state = jnp.zeros((queries.shape[0], head_count, head_dim, head_dim), jnp.float32)
    downward, _ = block_scan(queries, key_heads, values, jnp.swapaxes(planes[0], 0, 1), border_rows, zero_state)
    upward, _ = block_scan(queries[:, ::-1], key_heads[:, ::-1], values[:, ::-1], jnp.swapaxes(planes[1], 0, 1)[..., ::-1], reversed_borders(border_rows)[::-1], zero_state)
    combined = downward + upward[:, ::-1]
    combined = combined.reshape(combined.shape[0], combined.shape[1], -1)
    return jnp.swapaxes(combined, 0, 1).astype(jnp.bfloat16)

def norm_part(mixed, gain):
    power = lax.optimization_barrier(jnp.mean(mixed * mixed, axis=-1, keepdims=True))
    return mixed * lax.rsqrt(power + EPSILON) * gain

def sweep(queries, key_heads, values, decays, resets):
    line_count = queries.shape[0]

    def advance(carry_in, index):
        begin = index * COLS_DEV
        result, carry_out = jax.checkpoint(block_scan)(lax.dynamic_slice_in_dim(queries, begin, COLS_DEV, 1), lax.dynamic_slice_in_dim(key_heads, begin, COLS_DEV, 1), lax.dynamic_slice_in_dim(values, begin, COLS_DEV, 1), lax.dynamic_slice_in_dim(decays, begin, COLS_DEV, 2), lax.dynamic_slice_in_dim(resets, begin, COLS_DEV, 0), carry_in)
        return (carry_out, result)
    start_state = jnp.zeros((line_count, HEADS, HEAD_DIM, HEAD_DIM), jnp.float32)
    _, results = lax.scan(advance, start_state, jnp.arange(GRID_W // COLS_DEV, dtype=jnp.int32))
    return jnp.moveaxis(results, 0, 1).reshape(line_count, GRID_W, HEADS, HEAD_DIM)

def across_rows(projected, planes, border_cols):
    queries, key_heads, values = heads_of(projected, HEADS)
    rightward = sweep(queries, key_heads, values, jnp.swapaxes(planes[0], 0, 1), border_cols)
    leftward = sweep(queries[:, ::-1], key_heads[:, ::-1], values[:, ::-1], jnp.swapaxes(planes[1], 0, 1)[..., ::-1], reversed_borders(border_cols)[::-1])
    combined = rightward + leftward[:, ::-1]
    return combined.reshape(GRID_H, GRID_W, D)

def down_up_all(projected, planes, border_rows):
    groups = GRID_W // COLS_DEV
    grouped = jnp.swapaxes(projected.reshape(GRID_H, groups, COLS_DEV, 3 * D), 0, 1)
    plane_groups = jnp.moveaxis(planes.reshape(2, HEADS, groups, COLS_DEV, GRID_H), 2, 0)

    def one_group(group_pair):
        return down_up(group_pair[0], group_pair[1], border_rows)
    result = lax.map(one_group, (grouped, plane_groups))
    return jnp.swapaxes(result, 0, 1).reshape(GRID_H, GRID_W, D)

def reference(tokens, grad_out, w_qkv, w_out, gain, log_decay_rows, log_decay_cols, border_cols, border_rows):
    flat_tokens = tokens.reshape(TOKENS, D)
    projected = jnp.dot(flat_tokens, w_qkv, preferred_element_type=jnp.float32).astype(jnp.bfloat16)
    projected = projected.reshape(GRID_H, GRID_W, 3 * D)
    row_out, row_pull = jax.vjp(functools.partial(across_rows, border_cols=border_cols), projected, log_decay_rows)
    col_out, col_pull = jax.vjp(functools.partial(down_up_all, border_rows=border_rows), projected, log_decay_cols)
    mixed = row_out + lax.optimization_barrier(col_out).astype(jnp.float32)
    normed_value, norm_pull = jax.vjp(norm_part, mixed, gain)
    normed = normed_value.astype(jnp.bfloat16)
    flat_grad = grad_out.reshape(TOKENS, D)
    d_normed = jnp.dot(flat_grad, w_out.T, preferred_element_type=jnp.float32).astype(jnp.bfloat16)
    d_normed = lax.optimization_barrier(d_normed).astype(jnp.float32)
    d_mixed, d_gain = norm_pull(d_normed.reshape(GRID_H, GRID_W, D))
    d_out_weight = jnp.dot(normed.reshape(TOKENS, D).T, flat_grad, preferred_element_type=jnp.float32)
    row_qkv, row_decay = row_pull(d_mixed)
    col_qkv, col_decay = col_pull(d_mixed.astype(jnp.bfloat16))
    row_flat = row_qkv.reshape(TOKENS, 3 * D)
    col_flat = col_qkv.reshape(TOKENS, 3 * D)
    col_tokens = jnp.dot(col_flat, w_qkv.T, preferred_element_type=jnp.float32).astype(jnp.bfloat16)
    col_tokens = lax.optimization_barrier(col_tokens).astype(jnp.float32)
    grad_tokens = jnp.dot(row_flat, w_qkv.T, preferred_element_type=jnp.float32) + col_tokens
    grad_tokens = grad_tokens.astype(jnp.bfloat16).reshape(GRID_H, GRID_W, D)
    d_qkv_weight = jnp.dot(flat_tokens.T, row_flat, preferred_element_type=jnp.float32) + jnp.dot(flat_tokens.T, col_flat, preferred_element_type=jnp.float32)
    scaling = TOKENS ** (-0.5)
    return (grad_tokens, d_qkv_weight * scaling, d_out_weight * scaling, d_gain * scaling, row_decay, col_decay)
```

```python
import functools

import jax
import jax.numpy as jnp
from jax import lax
from jax.experimental import pallas as pl
from jax.experimental.pallas import tpu as pltpu
from jax.sharding import PartitionSpec as P

EPSILON = 1e-05
HEADS = 12
HEAD_DIM = 64
PAIRS = HEADS // 2
D = 768
F = 3 * D
ROWS = 2
COLS = 128
TOK = ROWS * COLS
GRID_H = 32
CD = 8
SCALE = HEAD_DIM ** (-0.5)
WIDE = F + D + 128
F32 = jnp.float32
BF = jnp.bfloat16
EVEN_ODD = [list(range(0, 16, 2)), list(range(1, 16, 2))]
CORE_SWAP = [(i, i ^ 1) for i in range(16)]


def call(body, outs, *args, smem=()):
    specs = [
        pl.BlockSpec(memory_space=pltpu.SMEM if n in smem else pltpu.VMEM) for n in range(len(args))
    ]
    return pl.pallas_call(
        body,
        out_shape=[jax.ShapeDtypeStruct(s, t) for s, t in outs],
        in_specs=specs,
        out_specs=[pl.BlockSpec(memory_space=pltpu.VMEM)] * len(outs),
        compiler_params=pltpu.CompilerParams(vmem_limit_bytes=56 * 1024 * 1024),
    )(*args)


def iota(shape, dim):
    return lax.broadcasted_iota(jnp.int32, shape, dim)


def nn(a, b):
    return lax.dot_general(a, b, (((1,), (0,)), ((), ())), preferred_element_type=F32)


def nt(a, b):
    return lax.dot_general(a, b, (((1,), (1,)), ((), ())), preferred_element_type=F32)


def tn(a, b):
    return lax.dot_general(a, b, (((0,), (0,)), ((), ())), preferred_element_type=F32)


def left_half(shape):
    return iota(shape, len(shape) - 1) < HEAD_DIM


def split_heads(x):
    mask = left_half(x.shape)
    zero = jnp.zeros_like(x)
    return jnp.concatenate([jnp.where(mask, x, zero), jnp.where(mask, zero, x)], axis=0)


def side(x):
    half = x.shape[0] // 2
    return jnp.concatenate([x[:half], x[half:]], axis=1)


def lanes_of(fac, p):
    shape = (fac.shape[0], 128)
    return jnp.where(left_half(shape), fac[:, 2 * p : 2 * p + 1], fac[:, 2 * p + 1 : 2 * p + 2])


def compact(m):
    return jnp.where(left_half((HEAD_DIM, 128)), m[:HEAD_DIM], m[HEAD_DIM:])


def block_of(ref, direction, r, p):
    n = direction * ROWS * PAIRS + r * PAIRS + p
    return n // 3, (n % 3) * HEAD_DIM


def weights(col_r, row_r, col_l, row_l, lower, mask):
    return jnp.exp(jnp.where(lower, col_r - row_r, col_l - row_l)) * mask


def prep_kernel(ldr_ref, ldc_ref, bc_ref, br_ref, wr_ref, wc_ref, fac_ref, th_ref):
    i0, i1 = iota((COLS, COLS), 0), iota((COLS, COLS), 1)
    le, ge = (i0 <= i1).astype(BF), (i0 >= i1).astype(BF)
    lower = i0 >= i1
    b = bc_ref[...].astype(F32)
    b8 = jnp.broadcast_to(b[0:1], (8, COLS)).astype(BF)
    seg_row = nn(b8, le)[0:1]
    seg_col = nt(ge, b8)[:, 0:1]
    first, last = seg_row[:, 0:1], seg_row[:, COLS - 1 : COLS]
    after = last + b[1:2, 0:1]
    mask = jnp.where(seg_col == seg_row, jnp.where(i0 == i1, 2.0 * SCALE, SCALE), 0.0)
    th_ref[...] = jnp.zeros_like(th_ref)
    for r in range(ROWS):
        lr, ll = ldr_ref[r, 0], ldr_ref[r, 1]
        row_r, row_l = nn(lr, le), nn(ll, ge)
        col_r, col_l = nt(ge, lr), nt(le, ll)
        for h in range(HEADS):
            w = weights(col_r[:, h : h + 1], row_r[h : h + 1], col_l[:, h : h + 1], row_l[h : h + 1], lower, mask)
            wr_ref[r * PAIRS + h // 2, (h % 2) * COLS : (h % 2 + 1) * COLS, :] = w
        fac_ref[0, r] = jnp.where(seg_col == 0.0, jnp.exp(col_r), 0.0) * SCALE
        fac_ref[1, r] = jnp.where(seg_col == after, jnp.exp(col_l), 0.0) * SCALE
        fac_ref[2, r] = jnp.where(seg_col == last, jnp.exp(col_r[COLS - 1 : COLS] - col_r), 0.0)
        fac_ref[3, r] = jnp.where(seg_col == first, jnp.exp(col_l[0:1] - col_l), 0.0)
        th_r = jnp.where(last == 0.0, jnp.exp(row_r[:, COLS - 1 : COLS]), 0.0)
        th_l = jnp.where(after == first, jnp.exp(row_l[:, 0:1]), 0.0)
        for direction, th in enumerate((th_r, th_l)):
            for p in range(PAIRS):
                n = direction * ROWS * PAIRS + r * PAIRS + p
                both = jnp.where(left_half((1, 128)), th[2 * p : 2 * p + 1], th[2 * p + 1 : 2 * p + 2])
                th_ref[n // 3, n % 3 : n % 3 + 1, :] = both
    j0, j1 = iota((TOK, TOK), 0), iota((TOK, TOK), 1)
    same = (j0 & 7) == (j1 & 7)
    below = (j0 >> 3) >= (j1 >> 3)
    cle = (same & ((j0 >> 3) <= (j1 >> 3))).astype(BF)
    cge = (same & below).astype(BF)
    r8 = jnp.broadcast_to(br_ref[...].astype(F32), (8, TOK)).astype(BF)
    seg_row = nn(r8, cle)[0:1]
    seg_col = nt(cge, r8)[:, 0:1]
    mask = jnp.where(same & (seg_col == seg_row), jnp.where(j0 == j1, 2.0 * SCALE, SCALE), 0.0)
    lr, ll = ldc_ref[0], ldc_ref[1]
    row_r, row_l = nn(lr, cle), nn(ll, cge)
    col_r, col_l = nt(cge, lr), nt(cle, ll)
    for h in range(HEADS):
        w = weights(col_r[:, h : h + 1], row_r[h : h + 1], col_l[:, h : h + 1], row_l[h : h + 1], below, mask)
        wc_ref[h // 2, (h % 2) * TOK : (h % 2 + 1) * TOK, :] = w


def project_kernel(x_ref, g_ref, w_ref, wo_ref, fac_ref, th_ref, qkv_ref, dn_ref, u_ref):
    qkv_ref[...] = nn(x_ref[...], w_ref[...]).astype(BF)
    for r in range(ROWS):
        rows = slice(r * COLS, (r + 1) * COLS)
        for p in range(PAIRS):
            k = qkv_ref[rows, D + p * 128 : D + (p + 1) * 128]
            v = qkv_ref[rows, 2 * D + p * 128 : 2 * D + (p + 1) * 128].astype(F32)
            for direction in range(2):
                tv = (lanes_of(fac_ref[2 + direction, r], p) * v).astype(BF)
                a, off = block_of(u_ref, direction, r, p)
                u_ref[a, off : off + HEAD_DIM, :] = compact(tn(k, tv)).astype(BF)
    u_ref[:, 192:208, :] = th_ref[...].astype(BF)
    dn_ref[...] = nt(g_ref[...], wo_ref[...]).astype(BF)


def chain_kernel(adjoint, rev_ref, th_ref, x_ref, out_ref):
    rev = rev_ref[0]
    state = jnp.zeros((192, 128), F32)
    for n in range(8):
        up, down = n, 7 - n
        if adjoint:
            up, down = down, up
        src = jnp.where(rev == 1, down, up)
        out_ref[src] = state.astype(BF)
        if n < 7:
            th = th_ref[src, 192:208, :].astype(F32)
            th = jnp.concatenate([jnp.broadcast_to(th[m : m + 1], (HEAD_DIM, 128)) for m in range(3)], axis=0)
            state = th * state + x_ref[src, 0:192, :].astype(F32)


def col_forward_kernel(rx_ref, w_ref, wo_ref, wc_ref, qkv_ref, dn_ref, out_ref):
    x = rx_ref[:, 0:16, :].reshape(TOK, D)
    g = rx_ref[:, 16:32, :].reshape(TOK, D)
    qkv_ref[...] = nn(x, w_ref[...]).astype(BF)
    for p in range(PAIRS):
        q = qkv_ref[:, p * 128 : (p + 1) * 128]
        k = qkv_ref[:, D + p * 128 : D + (p + 1) * 128]
        v = qkv_ref[:, 2 * D + p * 128 : 2 * D + (p + 1) * 128]
        probs = (nt(split_heads(q), k) * wc_ref[p]).astype(BF)
        out_ref[:, p * 128 : (p + 1) * 128] = nn(side(probs), split_heads(v)).astype(BF)
    dn_ref[...] = nt(g, wo_ref[...]).astype(BF)


def state_of(s_ref, direction, r, p):
    a, off = block_of(s_ref, direction, r, p)
    return s_ref[a, off : off + HEAD_DIM, :]


def both_states(s_ref, r, p):
    return jnp.concatenate([split_heads(state_of(s_ref, d, r, p)) for d in range(2)], axis=1)


def row_forward_kernel(qkv_ref, s_ref, wr_ref, fac_ref, col_ref, out_ref, xch_ref):
    for r in range(ROWS):
        rows = slice(r * COLS, (r + 1) * COLS)
        for p in range(PAIRS):
            q = qkv_ref[rows, p * 128 : (p + 1) * 128]
            k = qkv_ref[rows, D + p * 128 : D + (p + 1) * 128]
            v = qkv_ref[rows, 2 * D + p * 128 : 2 * D + (p + 1) * 128]
            probs = (nt(split_heads(q), k) * wr_ref[r * PAIRS + p]).astype(BF)
            carried = nn(q, both_states(s_ref, r, p))
            out = nn(side(probs), split_heads(v))
            out = out + lanes_of(fac_ref[0, r], p) * carried[:, :128]
            out = out + lanes_of(fac_ref[1, r], p) * carried[:, 128:]
            out_ref[rows, p * 128 : (p + 1) * 128] = out
    xch_ref[:, 0:16, :] = col_ref[...].reshape(16, 16, D)
    slab = out_ref[...].reshape(2, 16, 8, D).swapaxes(0, 1).reshape(16, 16, D)
    xch_ref[:, 16:32, :] = slab.astype(BF)


def norm_backward(mixed, dn, gain):
    inv = lax.rsqrt(jnp.mean(mixed * mixed, axis=-1, keepdims=True) + EPSILON)
    unit = mixed * inv
    scaled = dn * gain
    d_mixed = inv * (scaled - unit * jnp.mean(scaled * unit, axis=-1, keepdims=True))
    return unit, d_mixed


def from_slab(x):
    return x.astype(F32).reshape(16, 2, 8, D).swapaxes(0, 1).reshape(TOK, D)


def row_middle_kernel(rx_ref, row_ref, dn_ref, gain_ref, qkv_ref, fac_ref, dm_ref, normed_ref, gt_ref, g_ref):
    mixed = row_ref[...] + from_slab(rx_ref[:, 0:16, :])
    dn = dn_ref[...].astype(F32)
    gain = gain_ref[...]
    unit, d_mixed = norm_backward(mixed, dn, gain)
    dm_ref[...] = d_mixed.astype(BF)
    normed_ref[...] = (unit * gain).astype(BF)
    gt_ref[...] = (dn * unit).astype(BF)
    for r in range(ROWS):
        rows = slice(r * COLS, (r + 1) * COLS)
        for p in range(PAIRS):
            q = qkv_ref[rows, p * 128 : (p + 1) * 128]
            do = dm_ref[rows, p * 128 : (p + 1) * 128].astype(F32)
            for direction in range(2):
                eo = (lanes_of(fac_ref[direction, r], p) * do).astype(BF)
                a, off = block_of(g_ref, direction, r, p)
                g_ref[a, off : off + HEAD_DIM, :] = compact(tn(q, eo)).astype(BF)


def local_backward(q, k, v, do, w):
    q2, do2 = split_heads(q), split_heads(do)
    scores = nt(q2, k)
    dw = nt(do2, v) * w
    probs = (scores * w).astype(BF)
    both = (scores * dw).astype(BF)
    dw = dw.astype(BF)
    dq = nn(side(dw), split_heads(k))
    dk = tn(dw, q2)
    dv = tn(probs, do2)
    return dq, dk, dv, both


def col_backward_kernel(rx_ref, col_ref, dn_ref, gain_ref, qkv_ref, wc_ref, w_ref, dqkv_ref, gd_ref, tok_ref):
    mixed = rx_ref[:, 16:32, :].reshape(TOK, D).astype(F32) + col_ref[...].astype(F32)
    _, d_mixed = norm_backward(mixed, dn_ref[...].astype(F32), gain_ref[...])
    d_mixed = d_mixed.astype(BF)
    j0, j1 = iota((TOK, TOK), 0), iota((TOK, TOK), 1)
    same = (j0 & 7) == (j1 & 7)
    k0, k1 = j0 >> 3, j1 >> 3
    before, behind = (same & (k0 < k1)).astype(BF), (same & (k0 > k1)).astype(BF)
    table = jnp.concatenate([before, behind], axis=1)
    for p in range(PAIRS):
        lanes = slice(p * 128, (p + 1) * 128)
        q = qkv_ref[:, p * 128 : (p + 1) * 128]
        k = qkv_ref[:, D + p * 128 : D + (p + 1) * 128]
        v = qkv_ref[:, 2 * D + p * 128 : 2 * D + (p + 1) * 128]
        dq, dk, dv, both = local_backward(q, k, v, d_mixed[:, lanes], wc_ref[p])
        dqkv_ref[:, p * 128 : (p + 1) * 128] = dq.astype(BF)
        dqkv_ref[:, D + p * 128 : D + (p + 1) * 128] = dk.astype(BF)
        dqkv_ref[:, 2 * D + p * 128 : 2 * D + (p + 1) * 128] = dv.astype(BF)
        sums = nn(both, table)
        for half in range(2):
            part = sums[half * TOK : (half + 1) * TOK]
            h = 2 * p + half
            gd_ref[0, h : h + 1, :] = jnp.sum(jnp.where(k0 >= k1, part[:, :TOK], 0.0), axis=0, keepdims=True)
            gd_ref[1, h : h + 1, :] = jnp.sum(jnp.where(k0 <= k1, part[:, TOK:], 0.0), axis=0, keepdims=True)
    tok_ref[...] = nt(dqkv_ref[...], w_ref[...]).astype(BF)


def row_backward_kernel(qkv_ref, dm_ref, s_ref, a_ref, wr_ref, fac_ref, th_ref, dqkv_ref, gd_ref):
    i0, i1 = iota((COLS, COLS), 0), iota((COLS, COLS), 1)
    table = jnp.concatenate([(i0 < i1).astype(BF), (i0 > i1).astype(BF)], axis=1)
    left = left_half((COLS, 128))
    for r in range(ROWS):
        rows = slice(r * COLS, (r + 1) * COLS)
        for p in range(PAIRS):
            lanes = slice(p * 128, (p + 1) * 128)
            q = qkv_ref[rows, p * 128 : (p + 1) * 128]
            k = qkv_ref[rows, D + p * 128 : D + (p + 1) * 128]
            v = qkv_ref[rows, 2 * D + p * 128 : 2 * D + (p + 1) * 128]
            do = dm_ref[rows, lanes]
            dq, dk, dv, both = local_backward(q, k, v, do, wr_ref[r * PAIRS + p])
            states, adjoints = both_states(s_ref, r, p), both_states(a_ref, r, p)
            wide_do, wide_v = do.astype(F32), v.astype(F32)
            enter = [lanes_of(fac_ref[d, r], p) for d in range(2)]
            tail = [lanes_of(fac_ref[2 + d, r], p) for d in range(2)]
            eo = [e * wide_do for e in enter]
            tv = [t * wide_v for t in tail]
            dq = dq + nt(jnp.concatenate(eo, axis=1).astype(BF), states)
            dk = dk + nt(jnp.concatenate(tv, axis=1).astype(BF), adjoints)
            carried = nn(q, states)
            leaving = nn(k, adjoints)
            dv = dv + tail[0] * leaving[:, :128] + tail[1] * leaving[:, 128:]
            dqkv_ref[rows, p * 128 : (p + 1) * 128] = dq.astype(BF)
            dqkv_ref[rows, D + p * 128 : D + (p + 1) * 128] = dk.astype(BF)
            dqkv_ref[rows, 2 * D + p * 128 : 2 * D + (p + 1) * 128] = dv.astype(BF)
            sums = nn(both, table)
            for direction in range(2):
                e_all = carried[:, direction * 128 : (direction + 1) * 128] * eo[direction]
                g_all = leaving[:, direction * 128 : (direction + 1) * 128] * tv[direction]
                n = direction * ROWS * PAIRS + r * PAIRS + p
                through = th_ref[n // 3, n % 3 : n % 3 + 1, :]
                prod = state_of(s_ref, direction, r, p).astype(F32) * state_of(a_ref, direction, r, p).astype(F32)
                prod = through * jnp.sum(prod, axis=0, keepdims=True)
                keep = (i0 >= i1) if direction == 0 else (i0 <= i1)
                for half in range(2):
                    pick = left if half == 0 else ~left
                    e = jnp.sum(jnp.where(pick, e_all, 0.0), axis=1, keepdims=True)
                    g = jnp.sum(jnp.where(pick, g_all, 0.0), axis=1, keepdims=True)
                    c = jnp.sum(jnp.where(pick[0:1], prod, 0.0), axis=1, keepdims=True)
                    part = sums[half * COLS : (half + 1) * COLS, direction * COLS : (direction + 1) * COLS]
                    grad = jnp.sum(jnp.where(keep, part + e, g), axis=0, keepdims=True) + c
                    gd_ref[direction, 2 * p + half, r : r + 1, :] = grad


def weight_kernel(x_ref, rx_ref, dr_ref, dc_ref, normed_ref, g_ref, gt_ref, out_ref):
    x = jnp.concatenate([x_ref[...], rx_ref[:, 0:16, :].reshape(TOK, D)], axis=0)

    def put(value, start):
        width = value.shape[1]
        for c in range(2):
            for n in range(8):
                at = (2 * n + c) * 48
                out_ref[c, n, :, start : start + width] = value[at : at + 48].astype(BF)

    for start in range(0, F, 384):
        d = jnp.concatenate([dr_ref[:, start : start + 384], dc_ref[:, start : start + 384]], axis=0)
        put(tn(x, d), start)
    for start in range(0, D, 384):
        put(tn(normed_ref[...], g_ref[:, start : start + 384]), F + start)
    put(tn(gt_ref[...], jnp.ones((TOK, 128), BF)), F + D)


def token_kernel(dr_ref, w_ref, rx_ref, out_ref):
    out_ref[...] = (nt(dr_ref[...], w_ref[...]) + from_slab(rx_ref[...])).astype(BF)


def exchange(x, axis, groups=None):
    return lax.all_to_all(x, axis, 0, 0, tiled=True, axis_index_groups=groups)


def per_device(
    tokens, grad_out, w_qkv, w_out, gain, log_decay_rows, log_decay_cols, border_cols, border_rows
):
    place = lax.axis_index("col")
    core = lax.axis_index("row") % 2
    rev = (place >= 4).astype(jnp.int32).reshape(1)
    x = tokens.reshape(TOK, D)
    g = grad_out.reshape(TOK, D)
    gain = gain.reshape(1, D)

    def slab(a):
        return a.reshape(ROWS, 16, CD, D).swapaxes(0, 1).reshape(16, ROWS * CD, D)

    rx = exchange(jnp.concatenate([slab(tokens), slab(grad_out)], axis=1), "row")

    ldr = log_decay_rows.transpose(2, 0, 1, 3)
    ldc = log_decay_cols.swapaxes(2, 3).reshape(2, HEADS, TOK)
    tiles = jnp.concatenate([border_cols, jnp.zeros((COLS,), jnp.int32)]).reshape(9, COLS)
    bc = lax.dynamic_slice_in_dim(tiles, place, 2)
    br = jnp.broadcast_to(border_rows[:, None], (GRID_H, CD)).reshape(1, TOK)
    wr, wc, fac, th = call(
        prep_kernel,
        [
            ((ROWS * PAIRS, 2 * COLS, COLS), F32),
            ((PAIRS, 2 * TOK, TOK), F32),
            ((4, ROWS, COLS, HEADS), F32),
            ((8, 16, 128), F32),
        ],
        ldr, ldc, bc, br,
    )
    qkv, dn, update = call(
        project_kernel,
        [((TOK, F), BF), ((TOK, D), BF), ((8, 208, 128), BF)],
        x, g, w_qkv, w_out, fac, th,
    )
    update = exchange(update, "col")
    (entering,) = call(
        functools.partial(chain_kernel, False), [((8, 192, 128), BF)], rev, update, update, smem=(0,)
    )
    entering = exchange(entering, "col")
    qkv_c, dn_c, col_out = call(
        col_forward_kernel,
        [((TOK, F), BF), ((TOK, D), BF), ((TOK, D), BF)],
        rx, w_qkv, w_out, wc,
    )
    row_out, swap = call(
        row_forward_kernel,
        [((TOK, D), F32), ((16, 32, D), BF)],
        qkv, entering, wr, fac, col_out,
    )
    rx2 = exchange(swap, "row")
    dm, normed, gt, adj = call(
        row_middle_kernel,
        [((TOK, D), BF), ((TOK, D), BF), ((TOK, D), BF), ((8, 192, 128), BF)],
        rx2, row_out, dn, gain, qkv, fac,
    )
    adj = exchange(adj, "col")
    (leaving,) = call(
        functools.partial(chain_kernel, True), [((8, 192, 128), BF)], rev, update, adj, smem=(0,)
    )
    leaving = exchange(leaving, "col")
    dqkv_c, gdc, tok_c = call(
        col_backward_kernel,
        [((TOK, F), BF), ((2, HEADS, TOK), F32), ((TOK, D), BF)],
        rx2, col_out, dn_c, gain, qkv_c, wc, w_qkv,
    )
    rx3 = exchange(tok_c.reshape(16, 16, D), "row")
    dqkv, gdr = call(
        row_backward_kernel,
        [((TOK, F), BF), ((2, HEADS, ROWS, COLS), F32)],
        qkv, dm, entering, leaving, wr, fac, th,
    )
    (wg,) = call(
        weight_kernel, [((2, 8, 48, WIDE), BF)], x, rx, dqkv, dqkv_c, normed, g, gt
    )
    other = lax.ppermute(lax.dynamic_index_in_dim(wg, 1 - core, 0, False), "row", CORE_SWAP)
    mine = lax.dynamic_index_in_dim(wg, core, 0, False)
    wg = (mine.astype(F32) + other.astype(F32)).astype(BF)
    wg = exchange(wg, "row", EVEN_ODD)
    wg = jnp.sum(wg.astype(F32), axis=0).astype(BF).reshape(8, 6, WIDE)
    wg = exchange(wg, "col")
    wg = jnp.sum(wg.astype(F32), axis=0) * (32768.0 ** (-0.5))
    (grad_tokens,) = call(token_kernel, [((TOK, D), BF)], dqkv, w_qkv, rx3)
    return (
        grad_tokens.reshape(ROWS, COLS, D),
        wg[:, :F],
        wg[:, F : F + D],
        wg[:, F + D],
        gdr.astype(BF),
        gdc.astype(BF).reshape(2, HEADS, GRID_H, CD).swapaxes(2, 3),
    )


def solution(mesh):
    in_specs = (
        P("row", "col", None),
        P("row", "col", None),
        P(),
        P(),
        P(),
        P(None, None, "row", "col"),
        P(None, None, ("col", "row"), None),
        P(),
        P(),
    )
    out_specs = (
        P("row", "col", None),
        P(("row", "col"), None),
        P(("row", "col"), None),
        P(("row", "col")),
        P(None, None, "row", "col"),
        P(None, None, ("col", "row"), None),
    )
    return jax.shard_map(
        per_device, mesh=mesh, in_specs=in_specs, out_specs=out_specs, check_vma=False
    )
```

```python
import jax
import jax.numpy as jnp
from jax import lax
from jax.experimental import pallas as pl
from jax.experimental.pallas import tpu as pltpu
from jax.sharding import PartitionSpec as P

EPSILON = 1e-05
HEADS = 12
HEAD_DIM = 64
PAIRS = HEADS // 2
D = 768
F = 3 * D
ROWS = 2
COLS = 128
TOK = ROWS * COLS
GRID_H = 32
CD = 8
SCALE = HEAD_DIM ** (-0.5)
WIDE = F + D + 128
F32 = jnp.float32
BF = jnp.bfloat16
EVEN_ODD = [list(range(0, 16, 2)), list(range(1, 16, 2))]
CORE_SWAP = [(i, i ^ 1) for i in range(16)]


UNITS = ROWS * PAIRS
STATE = UNITS * HEAD_DIM
LOAD = STATE + 16


def call(body, us, outs, *args, smem=(), scratch=()):
    specs = [
        pl.BlockSpec(memory_space=pltpu.SMEM if n in smem else pltpu.VMEM) for n in range(len(args))
    ]
    return pl.pallas_call(
        body,
        out_shape=[jax.ShapeDtypeStruct(s, t) for s, t in outs],
        in_specs=specs,
        out_specs=[pl.BlockSpec(memory_space=pltpu.VMEM)] * len(outs),
        scratch_shapes=list(scratch),
        cost_estimate=pl.CostEstimate(
            flops=int(us * 1.1e9), bytes_accessed=int(us * 3.6e6), transcendentals=0
        ),
        compiler_params=pltpu.CompilerParams(vmem_limit_bytes=56 * 1024 * 1024),
    )(*args)


def iota(shape, dim):
    return lax.broadcasted_iota(jnp.int32, shape, dim)


def nn(a, b):
    return lax.dot_general(a, b, (((1,), (0,)), ((), ())), preferred_element_type=F32)


def nt(a, b):
    return lax.dot_general(a, b, (((1,), (1,)), ((), ())), preferred_element_type=F32)


def tn(a, b):
    return lax.dot_general(a, b, (((0,), (0,)), ((), ())), preferred_element_type=F32)


def left_half(shape):
    return iota(shape, len(shape) - 1) < HEAD_DIM


def split_heads(x):
    mask = left_half(x.shape)
    zero = jnp.zeros_like(x)
    return jnp.concatenate([jnp.where(mask, x, zero), jnp.where(mask, zero, x)], axis=0)


def side(x):
    half = x.shape[0] // 2
    return jnp.concatenate([x[:half], x[half:]], axis=1)


def lanes_of(fac, p):
    shape = (fac.shape[0], 128)
    return jnp.where(left_half(shape), fac[:, 2 * p : 2 * p + 1], fac[:, 2 * p + 1 : 2 * p + 2])


def compact(m):
    return jnp.where(left_half((HEAD_DIM, 128)), m[:HEAD_DIM], m[HEAD_DIM:])


def unit_rows(r, p):
    u = r * PAIRS + p
    return slice(u * HEAD_DIM, (u + 1) * HEAD_DIM)


def spread(both_ref, place, toward_right, out_ref):
    for d in range(8):
        side_of = d > place if toward_right else d < place
        out_ref[d] = both_ref[jnp.where(side_of, 0, 1)]


def gather_states(place, rx_ref, from_left, state_ref):
    state_ref[...] = jnp.zeros_like(state_ref)

    def step(direction, source):
        for u in range(UNITS):
            rows = slice(u * HEAD_DIM, (u + 1) * HEAD_DIM)
            th = rx_ref[source, STATE:LOAD, :].astype(F32)[u : u + 1]
            state_ref[direction, rows, :] = th * state_ref[direction, rows, :] + rx_ref[source, rows, :].astype(F32)

    lax.fori_loop(0, place, lambda n, c: (step(0 if from_left else 1, n), c)[1], 0)
    lax.fori_loop(0, 7 - place, lambda n, c: (step(1 if from_left else 0, 7 - n), c)[1], 0)


def pick_rows(core):
    m, f = iota((D // 2, D), 0), iota((D // 2, D), 1)
    n = (m * 683) >> 15
    return (f == m + 48 * (n + core)).astype(BF)


def per_head(shape):
    return (iota(shape, 0) == (iota(shape, 1) >> 6)).astype(BF)


def weights(col_r, row_r, col_l, row_l, lower, mask):
    return jnp.exp(jnp.where(lower, col_r - row_r, col_l - row_l)) * mask


def row_masks(bc_ref):
    i0, i1 = iota((COLS, COLS), 0), iota((COLS, COLS), 1)
    le, ge = (i0 <= i1).astype(BF), (i0 >= i1).astype(BF)
    b = bc_ref[...].astype(F32)
    b8 = jnp.broadcast_to(b[0:1], (8, COLS)).astype(BF)
    seg_row = nn(b8, le)[0:1]
    seg_col = nt(ge, b8)[:, 0:1]
    return i0, i1, le, ge, seg_row, seg_col, b[1:2, 0:1]


def summary_kernel(place_ref, ldr_ref, bc_ref, x_ref, w_ref, fac_ref, th_ref, kv_ref, u_ref, both_ref):
    i0, i1, le, ge, seg_row, seg_col, following = row_masks(bc_ref)
    first, last = seg_row[:, 0:1], seg_row[:, COLS - 1 : COLS]
    after = last + following
    th_ref[...] = jnp.zeros_like(th_ref)
    for r in range(ROWS):
        lr, ll = ldr_ref[r, 0], ldr_ref[r, 1]
        row_r, row_l = nn(lr, le), nn(ll, ge)
        col_r, col_l = nt(ge, lr), nt(le, ll)
        fac_ref[0, r] = jnp.where(seg_col == 0.0, jnp.exp(col_r), 0.0) * SCALE
        fac_ref[1, r] = jnp.where(seg_col == after, jnp.exp(col_l), 0.0) * SCALE
        fac_ref[2, r] = jnp.where(seg_col == last, jnp.exp(col_r[COLS - 1 : COLS] - col_r), 0.0)
        fac_ref[3, r] = jnp.where(seg_col == first, jnp.exp(col_l[0:1] - col_l), 0.0)
        th_r = jnp.where(last == 0.0, jnp.exp(row_r[:, COLS - 1 : COLS]), 0.0)
        th_l = jnp.where(after == first, jnp.exp(row_l[:, 0:1]), 0.0)
        for direction, th in enumerate((th_r, th_l)):
            for p in range(PAIRS):
                n = r * PAIRS + p
                both = jnp.where(left_half((1, 128)), th[2 * p : 2 * p + 1], th[2 * p + 1 : 2 * p + 2])
                th_ref[direction, n : n + 1, :] = both
    kv_ref[...] = nn(x_ref[...], w_ref[:, D:]).astype(BF)
    for r in range(ROWS):
        rows = slice(r * COLS, (r + 1) * COLS)
        for p in range(PAIRS):
            k = kv_ref[rows, p * 128 : (p + 1) * 128]
            v = kv_ref[rows, D + p * 128 : D + (p + 1) * 128].astype(F32)
            for direction in range(2):
                tv = (lanes_of(fac_ref[2 + direction, r], p) * v).astype(BF)
                both_ref[direction, unit_rows(r, p), :] = compact(tn(k, tv)).astype(BF)
    both_ref[:, STATE:LOAD, :] = th_ref[...].astype(BF)
    spread(both_ref, place_ref[0], True, u_ref)


def mask_kernel(ldr_ref, ldc_ref, bc_ref, br_ref, dep_ref, wr_ref, wc_ref):
    i0, i1, le, ge, seg_row, seg_col, _ = row_masks(bc_ref)
    lower = i0 >= i1
    mask = jnp.where(seg_col == seg_row, jnp.where(i0 == i1, 2.0 * SCALE, SCALE), 0.0)
    for r in range(ROWS):
        lr, ll = ldr_ref[r, 0], ldr_ref[r, 1]
        row_r, row_l = nn(lr, le), nn(ll, ge)
        col_r, col_l = nt(ge, lr), nt(le, ll)
        for h in range(HEADS):
            w = weights(col_r[:, h : h + 1], row_r[h : h + 1], col_l[:, h : h + 1], row_l[h : h + 1], lower, mask)
            wr_ref[r * PAIRS + h // 2, (h % 2) * COLS : (h % 2 + 1) * COLS, :] = w.astype(BF)
    j0, j1 = iota((TOK, TOK), 0), iota((TOK, TOK), 1)
    same = (j0 & 7) == (j1 & 7)
    below = (j0 >> 3) >= (j1 >> 3)
    cle = (same & ((j0 >> 3) <= (j1 >> 3))).astype(BF)
    cge = (same & below).astype(BF)
    r8 = jnp.broadcast_to(br_ref[...].astype(F32), (8, TOK)).astype(BF)
    seg_row = nn(r8, cle)[0:1]
    seg_col = nt(cge, r8)[:, 0:1]
    mask = jnp.where(same & (seg_col == seg_row), jnp.where(j0 == j1, 2.0 * SCALE, SCALE), 0.0)
    lr, ll = ldc_ref[0], ldc_ref[1]
    row_r, row_l = nn(lr, cle), nn(ll, cge)
    col_r, col_l = nt(cge, lr), nt(cle, ll)
    for h in range(HEADS):
        w = weights(col_r[:, h : h + 1], row_r[h : h + 1], col_l[:, h : h + 1], row_l[h : h + 1], below, mask)
        wc_ref[h // 2, (h % 2) * TOK : (h % 2 + 1) * TOK, :] = w.astype(BF)


def row_inside_kernel(
    core_ref, x_ref, g_ref, w_ref, wo_ref, kv_ref, wr_ref, q_ref, dn_ref, keep_ref, send_ref, out_ref, probs_ref
):
    core = core_ref[0]
    send_ref[...] = nt(pick_rows(1 - core), x_ref[...]).astype(BF)
    keep_ref[...] = nt(pick_rows(core), x_ref[...]).astype(BF)
    q_ref[...] = nn(x_ref[...], w_ref[:, :D]).astype(BF)
    dn_ref[...] = nt(g_ref[...], wo_ref[...]).astype(BF)
    for r in range(ROWS):
        rows = slice(r * COLS, (r + 1) * COLS)
        for p in range(PAIRS):
            lanes = slice(p * 128, (p + 1) * 128)
            k = kv_ref[rows, lanes]
            v = kv_ref[rows, D + p * 128 : D + (p + 1) * 128]
            n = r * PAIRS + p
            probs = (nt(split_heads(q_ref[rows, lanes]), k) * wr_ref[n].astype(F32)).astype(BF)
            probs_ref[n] = probs
            out_ref[rows, lanes] = nn(side(probs), split_heads(v))


def col_forward_kernel(
    core_ref, rx_ref, w_ref, wo_ref, wc_ref, qkv_ref, dn_ref, out_ref, probs_ref, keep_ref, send_ref
):
    x = rx_ref[:, 0:16, :].reshape(TOK, D)
    g = rx_ref[:, 16:32, :].reshape(TOK, D)
    qkv_ref[...] = nn(x, w_ref[...]).astype(BF)
    for p in range(PAIRS):
        q = qkv_ref[:, p * 128 : (p + 1) * 128]
        k = qkv_ref[:, D + p * 128 : D + (p + 1) * 128]
        v = qkv_ref[:, 2 * D + p * 128 : 2 * D + (p + 1) * 128]
        probs = (nt(split_heads(q), k) * wc_ref[p].astype(F32)).astype(BF)
        probs_ref[p] = probs
        out_ref[:, p * 128 : (p + 1) * 128] = nn(side(probs), split_heads(v)).astype(BF)
    dn_ref[...] = nt(g, wo_ref[...]).astype(BF)
    core = core_ref[0]
    keep_ref[...] = nt(pick_rows(core), x).astype(BF)
    send_ref[...] = nt(pick_rows(1 - core), x).astype(BF)


def state_of(s_ref, direction, r, p):
    return s_ref[direction, unit_rows(r, p), :]


def both_states(s_ref, r, p):
    return jnp.concatenate([split_heads(state_of(s_ref, d, r, p)) for d in range(2)], axis=1)


def row_join_kernel(place_ref, q_ref, rs_ref, fac_ref, inside_ref, col_ref, out_ref, xch_ref, s_ref, wide_ref):
    gather_states(place_ref[0], rs_ref, True, wide_ref)
    s_ref[...] = wide_ref[...].astype(BF)
    xch_ref[:, 0:16, :] = col_ref[...].reshape(16, 16, D)
    for r in range(ROWS):
        rows = slice(r * COLS, (r + 1) * COLS)
        for p in range(PAIRS):
            lanes = slice(p * 128, (p + 1) * 128)
            carried = nn(q_ref[rows, lanes], both_states(s_ref, r, p))
            out = inside_ref[rows, lanes]
            out = out + lanes_of(fac_ref[0, r], p) * carried[:, :128]
            out = out + lanes_of(fac_ref[1, r], p) * carried[:, 128:]
            out_ref[rows, lanes] = out
    slab = out_ref[...].reshape(2, 16, 8, D).swapaxes(0, 1).reshape(16, 16, D)
    xch_ref[:, 16:32, :] = slab.astype(BF)


def norm_backward(mixed, dn, gain):
    inv = lax.rsqrt(jnp.mean(mixed * mixed, axis=-1, keepdims=True) + EPSILON)
    unit = mixed * inv
    scaled = dn * gain
    d_mixed = inv * (scaled - unit * jnp.mean(scaled * unit, axis=-1, keepdims=True))
    return unit, d_mixed


def from_slab(x):
    return x.astype(F32).reshape(16, 2, 8, D).swapaxes(0, 1).reshape(TOK, D)


def row_middle_kernel(
    place_ref, rx_ref, row_ref, dn_ref, gain_ref, q_ref, fac_ref, th_ref, dm_ref, g_ref, both_ref
):
    mixed = row_ref[...] + from_slab(rx_ref[:, 0:16, :])
    _, d_mixed = norm_backward(mixed, dn_ref[...].astype(F32), gain_ref[...])
    dm_ref[...] = d_mixed.astype(BF)
    for r in range(ROWS):
        rows = slice(r * COLS, (r + 1) * COLS)
        for p in range(PAIRS):
            q = q_ref[rows, p * 128 : (p + 1) * 128]
            do = d_mixed[rows, p * 128 : (p + 1) * 128]
            for direction in range(2):
                eo = (lanes_of(fac_ref[direction, r], p) * do).astype(BF)
                both_ref[direction, unit_rows(r, p), :] = compact(tn(q, eo)).astype(BF)
    both_ref[:, STATE:LOAD, :] = th_ref[...].astype(BF)
    spread(both_ref, place_ref[0], False, g_ref)


def local_backward(q, k, v, do, w, probs):
    q2, do2 = split_heads(q), split_heads(do)
    dp = nt(do2, v)
    dw = (dp * w.astype(F32)).astype(BF)
    both = (dp * probs.astype(F32)).astype(BF)
    dq = nn(side(dw), split_heads(k))
    dk = tn(dw, q2)
    dv = tn(probs, do2)
    return dq, dk, dv, both


def col_backward_kernel(
    rx_ref, col_ref, dn_ref, gain_ref, qkv_ref, wc_ref, probs_ref, w_ref, dqkv_ref, gd_ref, tok_ref
):
    mixed = rx_ref[:, 16:32, :].reshape(TOK, D).astype(F32) + col_ref[...].astype(F32)
    _, d_mixed = norm_backward(mixed, dn_ref[...].astype(F32), gain_ref[...])
    d_mixed = d_mixed.astype(BF)
    j0, j1 = iota((TOK, TOK), 0), iota((TOK, TOK), 1)
    same = (j0 & 7) == (j1 & 7)
    k0, k1 = j0 >> 3, j1 >> 3
    before, behind = (same & (k0 < k1)).astype(BF), (same & (k0 > k1)).astype(BF)
    table = jnp.concatenate([before, behind], axis=1)
    for p in range(PAIRS):
        lanes = slice(p * 128, (p + 1) * 128)
        q = qkv_ref[:, p * 128 : (p + 1) * 128]
        k = qkv_ref[:, D + p * 128 : D + (p + 1) * 128]
        v = qkv_ref[:, 2 * D + p * 128 : 2 * D + (p + 1) * 128]
        dq, dk, dv, both = local_backward(q, k, v, d_mixed[:, lanes], wc_ref[p], probs_ref[p])
        dqkv_ref[:, p * 128 : (p + 1) * 128] = dq.astype(BF)
        dqkv_ref[:, D + p * 128 : D + (p + 1) * 128] = dk.astype(BF)
        dqkv_ref[:, 2 * D + p * 128 : 2 * D + (p + 1) * 128] = dv.astype(BF)
        sums = nn(both, table)
        for half in range(2):
            part = sums[half * TOK : (half + 1) * TOK]
            h = 2 * p + half
            gd_ref[0, h : h + 1, :] = jnp.sum(jnp.where(k0 >= k1, part[:, :TOK], 0.0), axis=0, keepdims=True)
            gd_ref[1, h : h + 1, :] = jnp.sum(jnp.where(k0 <= k1, part[:, TOK:], 0.0), axis=0, keepdims=True)
    tok_ref[...] = nt(dqkv_ref[...], w_ref[...]).astype(BF)


def row_local_kernel(
    core_ref, rx_ref, row_ref, dn_ref, gain_ref, q_ref, kv_ref, dm_ref, s_ref, wr_ref, probs_ref, fac_ref,
    dq_ref, part_ref, gd_ref, keep_ref, send_ref,
):
    mixed = row_ref[...] + from_slab(rx_ref[:, 0:16, :])
    unit = mixed * lax.rsqrt(jnp.mean(mixed * mixed, axis=-1, keepdims=True) + EPSILON)
    normed = (unit * gain_ref[...]).astype(BF)
    gain_terms = (dn_ref[...].astype(F32) * unit).astype(BF)
    core = core_ref[0]
    for ref, c in ((keep_ref, core), (send_ref, 1 - core)):
        pick = pick_rows(c)
        ref[0 : D // 2, :] = nt(pick, normed).astype(BF)
        ref[D // 2 : D, :] = nt(pick, gain_terms).astype(BF)
    i0, i1 = iota((COLS, COLS), 0), iota((COLS, COLS), 1)
    table = jnp.concatenate([(i0 < i1).astype(BF), (i0 > i1).astype(BF)], axis=1)
    entries = [[], []]
    for r in range(ROWS):
        rows = slice(r * COLS, (r + 1) * COLS)
        for p in range(PAIRS):
            lanes = slice(p * 128, (p + 1) * 128)
            q = q_ref[rows, lanes]
            k = kv_ref[rows, lanes]
            v = kv_ref[rows, D + p * 128 : D + (p + 1) * 128]
            do = dm_ref[rows, lanes]
            n = r * PAIRS + p
            dq, dk, dv, both = local_backward(q, k, v, do, wr_ref[n], probs_ref[n])
            states = both_states(s_ref, r, p)
            wide_do = do.astype(F32)
            eo = [lanes_of(fac_ref[d, r], p) * wide_do for d in range(2)]
            dq = dq + nt(jnp.concatenate(eo, axis=1).astype(BF), states)
            carried = nn(q, states)
            dq_ref[rows, lanes] = dq.astype(BF)
            part_ref[rows, lanes] = dk
            part_ref[rows, D + p * 128 : D + (p + 1) * 128] = dv
            sums = nn(both, table)
            for direction in range(2):
                entries[direction].append(
                    (carried[:, direction * 128 : (direction + 1) * 128] * eo[direction]).astype(BF)
                )
                keep = (i0 >= i1) if direction == 0 else (i0 <= i1)
                for half in range(2):
                    piece = sums[half * COLS : (half + 1) * COLS, direction * COLS : (direction + 1) * COLS]
                    n = r * HEADS + 2 * p + half
                    gd_ref[direction, n : n + 1, :] = jnp.sum(jnp.where(keep, piece, 0.0), axis=0, keepdims=True)
    heads = per_head((32, 2 * D))
    for direction in range(2):
        keep = ((i0 >= i1) if direction == 0 else (i0 <= i1)).astype(BF)
        total = nt(heads, jnp.concatenate(entries[direction], axis=1))
        gd_ref[direction] += nn(total.astype(BF), keep)[: 2 * HEADS]


def row_finish_kernel(
    place_ref, kv_ref, s_ref, ra_ref, fac_ref, th_ref, part_ref, gdp_ref, dkv_ref, gd_ref, wide_ref, a_ref
):
    gather_states(place_ref[0], ra_ref, False, wide_ref)
    a_ref[...] = wide_ref[...].astype(BF)
    i0, i1 = iota((COLS, COLS), 0), iota((COLS, COLS), 1)
    tails, throughs = [[], []], [[], []]
    for r in range(ROWS):
        rows = slice(r * COLS, (r + 1) * COLS)
        for p in range(PAIRS):
            lanes = slice(p * 128, (p + 1) * 128)
            far = slice(D + p * 128, D + (p + 1) * 128)
            k = kv_ref[rows, lanes]
            v = kv_ref[rows, far].astype(F32)
            adjoints = both_states(a_ref, r, p)
            tail = [lanes_of(fac_ref[2 + d, r], p) for d in range(2)]
            tv = [t * v for t in tail]
            dk = part_ref[rows, lanes] + nt(jnp.concatenate(tv, axis=1).astype(BF), adjoints)
            leaving = nn(k, adjoints)
            dv = part_ref[rows, far] + tail[0] * leaving[:, :128] + tail[1] * leaving[:, 128:]
            dkv_ref[rows, lanes] = dk.astype(BF)
            dkv_ref[rows, far] = dv.astype(BF)
            for d in range(2):
                tails[d].append((leaving[:, d * 128 : (d + 1) * 128] * tv[d]).astype(BF))
                n = r * PAIRS + p
                prod = state_of(s_ref, d, r, p).astype(F32) * state_of(a_ref, d, r, p).astype(F32)
                throughs[d].append(th_ref[d, n : n + 1, :] * jnp.sum(prod, axis=0, keepdims=True))
    heads = per_head((32, 2 * D))
    for d in range(2):
        before = ((i0 < i1) if d == 0 else (i0 > i1)).astype(BF)
        total = nt(heads, jnp.concatenate(tails[d], axis=1))
        through = jnp.broadcast_to(jnp.concatenate(throughs[d], axis=1), (8, 2 * D)).astype(BF)
        through = nt(heads, through)[: 2 * HEADS, 0:1]
        gd_ref[d] = gdp_ref[d] + nn(total.astype(BF), before)[: 2 * HEADS] + through


def weight_early_kernel(
    xk_ref, xr_ref, xck_ref, xcr_ref, dq_ref, dqr_ref, dc_ref, dcr_ref, nk_ref, nr_ref, g_ref, gr_ref, out_ref
):
    x = jnp.concatenate([xk_ref[...], xr_ref[...], xck_ref[...], xcr_ref[...]], axis=1)

    def put(value, start):
        out_ref[:, :, start : start + value.shape[1]] = value.astype(BF).reshape(8, 48, -1)

    for start in range(0, D, 384):
        cols = slice(start, start + 384)
        d = [dq_ref[:, cols], dqr_ref[:, cols], dc_ref[:, cols], dcr_ref[:, cols]]
        put(nn(x, jnp.concatenate(d, axis=0)), start)
    normed = jnp.concatenate([nk_ref[0 : D // 2, :], nr_ref[0 : D // 2, :]], axis=1)
    gain_terms = jnp.concatenate([nk_ref[D // 2 : D, :], nr_ref[D // 2 : D, :]], axis=1)
    for start in range(0, D, 384):
        d = jnp.concatenate([g_ref[:, start : start + 384], gr_ref[:, start : start + 384]], axis=0)
        put(nn(normed, d), D + start)
    put(nn(gain_terms, jnp.ones((2 * TOK, 128), BF)), 2 * D)


def weight_late_kernel(
    xk_ref, xr_ref, xck_ref, xcr_ref, dkv_ref, dkvr_ref, dc_ref, dcr_ref, early_ref, out_ref
):
    x = jnp.concatenate([xk_ref[...], xr_ref[...], xck_ref[...], xcr_ref[...]], axis=1)
    out_ref[:, :, 2 * D :] = early_ref[...]
    for start in range(0, 2 * D, 384):
        cols, far = slice(start, start + 384), slice(D + start, D + start + 384)
        d = [dkv_ref[:, cols], dkvr_ref[:, cols], dc_ref[:, far], dcr_ref[:, far]]
        out_ref[:, :, cols] = nn(x, jnp.concatenate(d, axis=0)).astype(BF).reshape(8, 48, 384)


def token_kernel(dq_ref, dkv_ref, w_ref, rx_ref, out_ref):
    total = nt(dq_ref[...], w_ref[:, :D]) + nt(dkv_ref[...], w_ref[:, D:])
    out_ref[...] = (total + from_slab(rx_ref[...])).astype(BF)


def exchange(x, axis, groups=None):
    return lax.all_to_all(x, axis, 0, 0, tiled=True, axis_index_groups=groups)


def swap(x):
    return lax.ppermute(x, "row", CORE_SWAP)


def after(value, *others):
    return lax.optimization_barrier((value, *others))[0]


def per_device(
    tokens, grad_out, w_qkv, w_out, gain, log_decay_rows, log_decay_cols, border_cols, border_rows
):
    place = lax.axis_index("col")
    at = place.astype(jnp.int32).reshape(1)
    core = (lax.axis_index("row") % 2).astype(jnp.int32).reshape(1)
    x = tokens.reshape(TOK, D)
    g = grad_out.reshape(TOK, D)
    gain = gain.reshape(1, D)
    half = (D // 2, TOK)
    load = ((8, LOAD, 128), BF)
    wide = pltpu.VMEM((2, STATE, 128), F32)
    narrow = pltpu.VMEM((2, LOAD, 128), BF)

    def slab(a):
        return a.reshape(ROWS, 16, CD, D).swapaxes(0, 1).reshape(16, ROWS * CD, D)

    rx = exchange(jnp.concatenate([slab(tokens), slab(grad_out)], axis=1), "row")

    ldr = log_decay_rows.transpose(2, 0, 1, 3)
    ldc = log_decay_cols.swapaxes(2, 3).reshape(2, HEADS, TOK)
    tiles = jnp.concatenate([border_cols, jnp.zeros((COLS,), jnp.int32)]).reshape(9, COLS)
    bc = lax.dynamic_slice_in_dim(tiles, place, 2)
    br = jnp.broadcast_to(border_rows[:, None], (GRID_H, CD)).reshape(1, TOK)
    fac, th, kv, update = call(
        summary_kernel, 4.6,
        [((4, ROWS, COLS, HEADS), F32), ((2, 16, 128), F32), ((TOK, 2 * D), BF), load],
        at, ldr, bc, x, w_qkv, smem=(0,), scratch=[narrow],
    )
    wr, wc = call(
        mask_kernel, 4.3,
        [((UNITS, 2 * COLS, COLS), BF), ((PAIRS, 2 * TOK, TOK), BF)],
        ldr, ldc, bc, br, th,
    )
    states = exchange(after(update, rx, wr), "col")
    q, dn, x_keep, x_send, inside, probs = call(
        row_inside_kernel, 5.7,
        [((TOK, D), BF), ((TOK, D), BF), (half, BF), (half, BF), ((TOK, D), F32), ((UNITS, 2 * COLS, COLS), BF)],
        core, x, g, w_qkv, w_out, kv, wr, smem=(0,),
    )
    x_far, g_far = swap(x_send), swap(g)
    qkv_c, dn_c, col_out, probs_c, xc_keep, xc_send = call(
        col_forward_kernel, 6.8,
        [((TOK, F), BF), ((TOK, D), BF), ((TOK, D), BF), ((PAIRS, 2 * TOK, TOK), BF), (half, BF), (half, BF)],
        core, rx, w_qkv, w_out, wc, smem=(0,),
    )
    states = after(states, col_out, q)
    row_out, out_swap, entering = call(
        row_join_kernel, 5.0,
        [((TOK, D), F32), ((16, 32, D), BF), ((2, STATE, 128), BF)],
        at, q, states, fac, inside, col_out, smem=(0,), scratch=[wide],
    )
    xc_far = swap(xc_send)
    rx2 = exchange(out_swap, "row")
    rx2, x_far, g_far, xc_far = lax.optimization_barrier((rx2, x_far, g_far, xc_far))
    dm, adj = call(
        row_middle_kernel, 4.5,
        [((TOK, D), BF), load],
        at, rx2, row_out, dn, gain, q, fac, th, smem=(0,), scratch=[narrow],
    )
    adj = exchange(adj, "col")
    dq, part, gd_part, n_keep, n_send = call(
        row_local_kernel, 8.9,
        [((TOK, D), BF), ((TOK, 2 * D), F32), ((2, 2 * HEADS, COLS), F32), ((D, TOK), BF), ((D, TOK), BF)],
        core, rx2, row_out, dn, gain, q, kv, dm, entering, wr, probs, fac, smem=(0,),
    )
    n_far, dq_far = swap(n_send), swap(dq)
    dqkv_c, gdc, tok_c = call(
        col_backward_kernel, 9.7,
        [((TOK, F), BF), ((2, HEADS, TOK), F32), ((TOK, D), BF)],
        after(rx2, dm), col_out, dn_c, gain, qkv_c, wc, probs_c, w_qkv,
    )
    dqkv_c_far = swap(dqkv_c)
    adj, n_far, dq_far, tok_c = lax.optimization_barrier((adj, n_far, dq_far, tok_c))
    rx3 = exchange(tok_c.reshape(16, 16, D), "row")
    dkv, gdr = call(
        row_finish_kernel, 5.5,
        [((TOK, 2 * D), BF), ((2, 2 * HEADS, COLS), F32)],
        at, kv, entering, adj, fac, th, part, gd_part,
        smem=(0,), scratch=[wide, pltpu.VMEM((2, STATE, 128), BF)],
    )
    dkv_far = swap(dkv)
    (early,) = call(
        weight_early_kernel, 5.0,
        [((8, 48, 2 * D + 128), BF)],
        x_keep, x_far, xc_keep, xc_far, after(dq, dkv), dq_far, dqkv_c, dqkv_c_far, n_keep, n_far, g, g_far,
    )
    (wg,) = call(
        weight_late_kernel, 6.0,
        [((8, 48, WIDE), BF)],
        x_keep, x_far, xc_keep, xc_far, dkv, dkv_far, dqkv_c, dqkv_c_far, early,
    )
    wg = exchange(after(wg, rx3), "row", EVEN_ODD)
    wg = jnp.sum(wg.astype(F32), axis=0).astype(BF).reshape(8, 6, WIDE)
    wg = exchange(wg, "col")
    wg = jnp.sum(wg.astype(F32), axis=0) * (32768.0 ** (-0.5))
    (grad_tokens,) = call(token_kernel, 4.0, [((TOK, D), BF)], dq, dkv, w_qkv, rx3)
    gdr = gdr.reshape(2, ROWS, HEADS, COLS).swapaxes(1, 2)
    return (
        grad_tokens.reshape(ROWS, COLS, D),
        jnp.concatenate([wg[:, 2 * D : 3 * D], wg[:, : 2 * D]], axis=1),
        wg[:, F : F + D],
        wg[:, F + D],
        gdr.astype(BF),
        gdc.astype(BF).reshape(2, HEADS, GRID_H, CD).swapaxes(2, 3),
    )


def solution(mesh):
    in_specs = (
        P("row", "col", None),
        P("row", "col", None),
        P(),
        P(),
        P(),
        P(None, None, "row", "col"),
        P(None, None, ("col", "row"), None),
        P(),
        P(),
    )
    out_specs = (
        P("row", "col", None),
        P(("row", "col"), None),
        P(("row", "col"), None),
        P(("row", "col")),
        P(None, None, "row", "col"),
        P(None, None, ("col", "row"), None),
    )
    return jax.shard_map(
        per_device, mesh=mesh, in_specs=in_specs, out_specs=out_specs, check_vma=False
    )
```

```python
import jax
import jax.numpy as jnp
from jax import lax
from jax.experimental import pallas as pl
from jax.experimental.pallas import tpu as pltpu
from jax.sharding import PartitionSpec as P

EPSILON = 1e-05
HEADS = 12
HEAD_DIM = 64
PAIRS = HEADS // 2
D = 768
F = 3 * D
ROWS = 2
COLS = 128
TOK = ROWS * COLS
GRID_H = 32
CD = 8
SCALE = HEAD_DIM ** (-0.5)
WIDE = F + 128
SPLIT = 512
VMEM_MIB = 20
F32 = jnp.float32
BF = jnp.bfloat16
SAME_CORE = [[r * 8 + c for r in range(core, 16, 2) for c in range(8)] for core in range(2)]
CORE_SWAP = [(i, i ^ 1) for i in range(16)]


UNITS = ROWS * PAIRS
STATE = UNITS * HEAD_DIM
LOAD = STATE + 16


def call(body, us, outs, *args, smem=(), near=(), keep=(), scratch=()):
    specs = [
        pl.BlockSpec(memory_space=pltpu.SMEM if n in smem else pltpu.VMEM) for n in range(len(args))
    ]
    args = [
        a if n in smem or n in near else pltpu.with_memory_space_constraint(a, pltpu.HBM)
        for n, a in enumerate(args)
    ]
    return pl.pallas_call(
        body,
        out_shape=[(pltpu.VMEM if n in keep else pltpu.HBM)(s, t) for n, (s, t) in enumerate(outs)],
        in_specs=specs,
        out_specs=[pl.BlockSpec(memory_space=pltpu.VMEM)] * len(outs),
        scratch_shapes=list(scratch),
        cost_estimate=pl.CostEstimate(
            flops=int(us * 1.1e9), bytes_accessed=int(us * 3.6e6), transcendentals=0
        ),
        compiler_params=pltpu.CompilerParams(vmem_limit_bytes=VMEM_MIB * 1024 * 1024),
    )(*args)


def iota(shape, dim):
    return lax.broadcasted_iota(jnp.int32, shape, dim)


def nn(a, b):
    return lax.dot_general(a, b, (((1,), (0,)), ((), ())), preferred_element_type=F32)


def nt(a, b):
    return lax.dot_general(a, b, (((1,), (1,)), ((), ())), preferred_element_type=F32)


def tn(a, b):
    return lax.dot_general(a, b, (((0,), (0,)), ((), ())), preferred_element_type=F32)


def left_half(shape):
    return iota(shape, len(shape) - 1) < HEAD_DIM


def split_heads(x):
    mask = left_half(x.shape)
    zero = jnp.zeros_like(x)
    return jnp.concatenate([jnp.where(mask, x, zero), jnp.where(mask, zero, x)], axis=0)


def side(x):
    half = x.shape[0] // 2
    return jnp.concatenate([x[:half], x[half:]], axis=1)


def lanes_of(fac, kind, p):
    shape = (fac.shape[0], 128)
    n = kind * HEADS + 2 * p
    return jnp.where(left_half(shape), fac[:, n : n + 1], fac[:, n + 1 : n + 2])


def compact(m):
    return jnp.where(left_half((HEAD_DIM, 128)), m[:HEAD_DIM], m[HEAD_DIM:])


def unit_rows(r, p):
    u = r * PAIRS + p
    return slice(u * HEAD_DIM, (u + 1) * HEAD_DIM)


def spread(both_ref, place, toward_right, out_ref):
    for d in range(8):
        side_of = d > place if toward_right else d < place
        out_ref[d] = both_ref[jnp.where(side_of, 0, 1)]


def gather_states(place, rx_ref, from_left, state_ref):
    state_ref[...] = jnp.zeros_like(state_ref)

    def step(direction, source):
        for u in range(UNITS):
            rows = slice(u * HEAD_DIM, (u + 1) * HEAD_DIM)
            th = rx_ref[source, STATE:LOAD, :].astype(F32)[u : u + 1]
            state_ref[direction, rows, :] = th * state_ref[direction, rows, :] + rx_ref[source, rows, :].astype(F32)

    lax.fori_loop(0, place, lambda n, c: (step(0 if from_left else 1, n), c)[1], 0)
    lax.fori_loop(0, 7 - place, lambda n, c: (step(1 if from_left else 0, 7 - n), c)[1], 0)


def first_feature(n, j, core):
    return 48 * (2 * n + core) + 6 * j


def pick_rows(core):
    m, f = iota((SPLIT, D), 0), iota((SPLIT, D), 1)
    t = m & 7
    return ((f == first_feature(m >> 6, (m >> 3) & 7, core) + t) & (t < 6)).astype(BF)


def pick_thirds(core):
    m, f = iota((D // 2, D), 0), iota((D // 2, D), 1)
    b, d = m >> 7, (m >> 1) & 63
    return (f == first_feature(d >> 3, d & 7, core) + 3 * (m & 1) + b).astype(BF)


def place_thirds():
    m, n = iota((SPLIT, 128), 0), iota((SPLIT, 128), 1)
    return (((m >> 3) == (n >> 1)) & ((m & 7) == 6 + (n & 1))).astype(BF)


def per_head(shape):
    return (iota(shape, 0) == (iota(shape, 1) >> 6)).astype(BF)


def weights(col_r, row_r, col_l, row_l, lower, mask):
    return jnp.exp(jnp.where(lower, col_r - row_r, col_l - row_l)) * mask


def row_masks(bc_ref):
    i0, i1 = iota((COLS, COLS), 0), iota((COLS, COLS), 1)
    le, ge = (i0 <= i1).astype(BF), (i0 >= i1).astype(BF)
    b = bc_ref[...].astype(F32)
    b8 = jnp.broadcast_to(b[0:1], (8, COLS)).astype(BF)
    seg_row = nn(b8, le)[0:1]
    seg_col = nt(ge, b8)[:, 0:1]
    return i0, i1, le, ge, seg_row, seg_col, b[1:2, 0:1]


def layout_kernel(x_ref, g_ref, out_ref):
    for n, ref in enumerate((x_ref, g_ref)):
        wide = ref[...].astype(F32).reshape(2, 16, 8, D).swapaxes(0, 1).reshape(16, 16, D)
        out_ref[:, n * 16 : (n + 1) * 16, :] = wide.astype(BF)


def summary_kernel(place_ref, ldr_ref, bc_ref, x_ref, w_ref, fac_ref, th_ref, kv_ref, u_ref, both_ref):
    i0, i1, le, ge, seg_row, seg_col, following = row_masks(bc_ref)
    first, last = seg_row[:, 0:1], seg_row[:, COLS - 1 : COLS]
    after = last + following
    th_ref[...] = jnp.zeros_like(th_ref)
    for r in range(ROWS):
        lr, ll = ldr_ref[r, 0], ldr_ref[r, 1]
        row_r, row_l = nn(lr, le), nn(ll, ge)
        col_r, col_l = nt(ge, lr), nt(le, ll)
        fac_ref[r] = jnp.concatenate(
            [
                jnp.where(seg_col == 0.0, jnp.exp(col_r), 0.0) * SCALE,
                jnp.where(seg_col == after, jnp.exp(col_l), 0.0) * SCALE,
                jnp.where(seg_col == last, jnp.exp(col_r[COLS - 1 : COLS] - col_r), 0.0),
                jnp.where(seg_col == first, jnp.exp(col_l[0:1] - col_l), 0.0),
            ],
            axis=1,
        )
        th_r = jnp.where(last == 0.0, jnp.exp(row_r[:, COLS - 1 : COLS]), 0.0)
        th_l = jnp.where(after == first, jnp.exp(row_l[:, 0:1]), 0.0)
        for direction, th in enumerate((th_r, th_l)):
            for p in range(PAIRS):
                n = r * PAIRS + p
                both = jnp.where(left_half((1, 128)), th[2 * p : 2 * p + 1], th[2 * p + 1 : 2 * p + 2])
                th_ref[direction, n : n + 1, :] = both
    kv_ref[...] = nn(x_ref[...], w_ref[:, D:]).astype(BF)
    for r in range(ROWS):
        rows = slice(r * COLS, (r + 1) * COLS)
        for p in range(PAIRS):
            k = kv_ref[rows, p * 128 : (p + 1) * 128]
            v = kv_ref[rows, D + p * 128 : D + (p + 1) * 128].astype(F32)
            for direction in range(2):
                tv = (lanes_of(fac_ref[r], 2 + direction, p) * v).astype(BF)
                both_ref[direction, unit_rows(r, p), :] = compact(tn(k, tv)).astype(BF)
    both_ref[:, STATE:LOAD, :] = th_ref[...].astype(BF)
    spread(both_ref, place_ref[0], True, u_ref)


def mask_kernel(ldr_ref, ldc_ref, bc_ref, br_ref, dep_ref, wr_ref, wc_ref):
    i0, i1, le, ge, seg_row, seg_col, _ = row_masks(bc_ref)
    lower = i0 >= i1
    mask = jnp.where(seg_col == seg_row, jnp.where(i0 == i1, 2.0 * SCALE, SCALE), 0.0)
    for r in range(ROWS):
        lr, ll = ldr_ref[r, 0], ldr_ref[r, 1]
        row_r, row_l = nn(lr, le), nn(ll, ge)
        col_r, col_l = nt(ge, lr), nt(le, ll)
        for h in range(HEADS):
            w = weights(col_r[:, h : h + 1], row_r[h : h + 1], col_l[:, h : h + 1], row_l[h : h + 1], lower, mask)
            wr_ref[r * PAIRS + h // 2, (h % 2) * COLS : (h % 2 + 1) * COLS, :] = w.astype(BF)
    j0, j1 = iota((TOK, TOK), 0), iota((TOK, TOK), 1)
    same = (j0 & 7) == (j1 & 7)
    below = (j0 >> 3) >= (j1 >> 3)
    cle = (same & ((j0 >> 3) <= (j1 >> 3))).astype(BF)
    cge = (same & below).astype(BF)
    r8 = jnp.broadcast_to(br_ref[...].astype(F32), (8, TOK)).astype(BF)
    seg_row = nn(r8, cle)[0:1]
    seg_col = nt(cge, r8)[:, 0:1]
    mask = jnp.where(same & (seg_col == seg_row), jnp.where(j0 == j1, 2.0 * SCALE, SCALE), 0.0)
    lr, ll = ldc_ref[0], ldc_ref[1]
    row_r, row_l = nn(lr, cle), nn(ll, cge)
    col_r, col_l = nt(cge, lr), nt(cle, ll)
    for h in range(HEADS):
        w = weights(col_r[:, h : h + 1], row_r[h : h + 1], col_l[:, h : h + 1], row_l[h : h + 1], below, mask)
        wc_ref[h // 2, (h % 2) * TOK : (h % 2 + 1) * TOK, :] = w.astype(BF)


def row_inside_kernel(
    core_ref, x_ref, g_ref, w_ref, wo_ref, kv_ref, wr_ref, q_ref, dn_ref, keep_ref, send_ref, out_ref, probs_ref
):
    core = core_ref[0]
    send_ref[...] = nt(pick_rows(1 - core), x_ref[...]).astype(BF)
    keep_ref[...] = nt(pick_rows(core), x_ref[...]).astype(BF)
    q_ref[...] = nn(x_ref[...], w_ref[:, :D]).astype(BF)
    dn_ref[...] = nt(g_ref[...], wo_ref[...]).astype(BF)
    for r in range(ROWS):
        rows = slice(r * COLS, (r + 1) * COLS)
        for p in range(PAIRS):
            lanes = slice(p * 128, (p + 1) * 128)
            k = kv_ref[rows, lanes]
            v = kv_ref[rows, D + p * 128 : D + (p + 1) * 128]
            n = r * PAIRS + p
            probs = (nt(split_heads(q_ref[rows, lanes]), k) * wr_ref[n].astype(F32)).astype(BF)
            probs_ref[n] = probs
            out_ref[rows, lanes] = nn(side(probs), split_heads(v))


def col_forward_kernel(
    core_ref, rx_ref, w_ref, wo_ref, wc_ref, qkv_ref, dn_ref, out_ref, probs_ref, keep_ref, send_ref
):
    x = rx_ref[:, 0:16, :].reshape(TOK, D)
    g = rx_ref[:, 16:32, :].reshape(TOK, D)
    qkv_ref[...] = nn(x, w_ref[...]).astype(BF)
    for p in range(PAIRS):
        q = qkv_ref[:, p * 128 : (p + 1) * 128]
        k = qkv_ref[:, D + p * 128 : D + (p + 1) * 128]
        v = qkv_ref[:, 2 * D + p * 128 : 2 * D + (p + 1) * 128]
        probs = (nt(split_heads(q), k) * wc_ref[p].astype(F32)).astype(BF)
        probs_ref[p] = probs
        out_ref[:, p * 128 : (p + 1) * 128] = nn(side(probs), split_heads(v)).astype(BF)
    dn_ref[...] = nt(g, wo_ref[...]).astype(BF)
    core = core_ref[0]
    keep_ref[...] = nt(pick_rows(core), x).astype(BF)
    send_ref[...] = nt(pick_rows(1 - core), x).astype(BF)


def state_of(s_ref, direction, r, p):
    return s_ref[direction, unit_rows(r, p), :]


def both_states(s_ref, r, p):
    return jnp.concatenate([split_heads(state_of(s_ref, d, r, p)) for d in range(2)], axis=1)


def row_join_kernel(place_ref, q_ref, rs_ref, fac_ref, inside_ref, col_ref, out_ref, xch_ref, s_ref, wide_ref):
    gather_states(place_ref[0], rs_ref, True, wide_ref)
    s_ref[...] = wide_ref[...].astype(BF)
    xch_ref[:, 0:16, :] = col_ref[...].reshape(16, 16, D)
    for r in range(ROWS):
        rows = slice(r * COLS, (r + 1) * COLS)
        for p in range(PAIRS):
            lanes = slice(p * 128, (p + 1) * 128)
            carried = nn(q_ref[rows, lanes], both_states(s_ref, r, p))
            out = inside_ref[rows, lanes]
            out = out + lanes_of(fac_ref[r], 0, p) * carried[:, :128]
            out = out + lanes_of(fac_ref[r], 1, p) * carried[:, 128:]
            out_ref[rows, lanes] = out
    slab = out_ref[...].reshape(2, 16, 8, D).swapaxes(0, 1).reshape(16, 16, D)
    xch_ref[:, 16:32, :] = slab.astype(BF)


def norm_backward(mixed, dn, gain):
    inv = lax.rsqrt(jnp.mean(mixed * mixed, axis=-1, keepdims=True) + EPSILON)
    unit = mixed * inv
    scaled = dn * gain
    d_mixed = inv * (scaled - unit * jnp.mean(scaled * unit, axis=-1, keepdims=True))
    return unit, d_mixed


def from_slab(x):
    return x.astype(F32).reshape(16, 2, 8, D).swapaxes(0, 1).reshape(TOK, D)


def row_middle_kernel(
    place_ref, rx_ref, row_ref, dn_ref, gain_ref, q_ref, fac_ref, th_ref, dm_ref, g_ref, both_ref
):
    mixed = row_ref[...] + from_slab(rx_ref[:, 0:16, :])
    _, d_mixed = norm_backward(mixed, dn_ref[...].astype(F32), gain_ref[...])
    dm_ref[...] = d_mixed.astype(BF)
    for r in range(ROWS):
        rows = slice(r * COLS, (r + 1) * COLS)
        for p in range(PAIRS):
            q = q_ref[rows, p * 128 : (p + 1) * 128]
            do = d_mixed[rows, p * 128 : (p + 1) * 128]
            for direction in range(2):
                eo = (lanes_of(fac_ref[r], direction, p) * do).astype(BF)
                both_ref[direction, unit_rows(r, p), :] = compact(tn(q, eo)).astype(BF)
    both_ref[:, STATE:LOAD, :] = th_ref[...].astype(BF)
    spread(both_ref, place_ref[0], False, g_ref)


def local_backward(q, k, v, do, w, probs):
    q2, do2 = split_heads(q), split_heads(do)
    dp = nt(do2, v)
    dw = (dp * w.astype(F32)).astype(BF)
    both = (dp * probs.astype(F32)).astype(BF)
    dq = nn(side(dw), split_heads(k))
    dk = tn(dw, q2)
    dv = tn(probs, do2)
    return dq, dk, dv, both


def col_backward_kernel(
    rx_ref, col_ref, dn_ref, gain_ref, qkv_ref, wc_ref, probs_ref, w_ref, dqkv_ref, gd_ref, tok_ref
):
    mixed = rx_ref[:, 16:32, :].reshape(TOK, D).astype(F32) + col_ref[...].astype(F32)
    _, d_mixed = norm_backward(mixed, dn_ref[...].astype(F32), gain_ref[...])
    d_mixed = d_mixed.astype(BF)
    j0, j1 = iota((TOK, TOK), 0), iota((TOK, TOK), 1)
    same = (j0 & 7) == (j1 & 7)
    k0, k1 = j0 >> 3, j1 >> 3
    before, behind = (same & (k0 < k1)).astype(BF), (same & (k0 > k1)).astype(BF)
    table = jnp.concatenate([before, behind], axis=1)
    for p in range(PAIRS):
        lanes = slice(p * 128, (p + 1) * 128)
        q = qkv_ref[:, p * 128 : (p + 1) * 128]
        k = qkv_ref[:, D + p * 128 : D + (p + 1) * 128]
        v = qkv_ref[:, 2 * D + p * 128 : 2 * D + (p + 1) * 128]
        dq, dk, dv, both = local_backward(q, k, v, d_mixed[:, lanes], wc_ref[p], probs_ref[p])
        dqkv_ref[:, p * 128 : (p + 1) * 128] = dq.astype(BF)
        dqkv_ref[:, D + p * 128 : D + (p + 1) * 128] = dk.astype(BF)
        dqkv_ref[:, 2 * D + p * 128 : 2 * D + (p + 1) * 128] = dv.astype(BF)
        sums = nn(both, table)
        for half in range(2):
            part = sums[half * TOK : (half + 1) * TOK]
            h = 2 * p + half
            gd_ref[0, h : h + 1, :] = jnp.sum(jnp.where(k0 >= k1, part[:, :TOK], 0.0), axis=0, keepdims=True)
            gd_ref[1, h : h + 1, :] = jnp.sum(jnp.where(k0 <= k1, part[:, TOK:], 0.0), axis=0, keepdims=True)
    tok_ref[...] = nt(dqkv_ref[...], w_ref[...]).astype(BF)


def row_local_kernel(
    core_ref, rx_ref, row_ref, dn_ref, gain_ref, q_ref, kv_ref, dm_ref, s_ref, wr_ref, probs_ref, fac_ref,
    dq_ref, part_ref, gd_ref, keep_ref, send_ref,
):
    mixed = row_ref[...] + from_slab(rx_ref[:, 0:16, :])
    unit = mixed * lax.rsqrt(jnp.mean(mixed * mixed, axis=-1, keepdims=True) + EPSILON)
    normed = (unit * gain_ref[...]).astype(BF)
    gain_terms = (dn_ref[...].astype(F32) * unit).astype(BF)
    core = core_ref[0]
    for ref, c in ((keep_ref, core), (send_ref, 1 - core)):
        ref[0:SPLIT, :] = nt(pick_rows(c), gain_terms).astype(BF)
        ref[SPLIT : SPLIT + D // 2, :] = nt(pick_thirds(c), normed).astype(BF)
    i0, i1 = iota((COLS, COLS), 0), iota((COLS, COLS), 1)
    table = jnp.concatenate([(i0 < i1).astype(BF), (i0 > i1).astype(BF)], axis=1)
    entries = [[], []]
    for r in range(ROWS):
        rows = slice(r * COLS, (r + 1) * COLS)
        for p in range(PAIRS):
            lanes = slice(p * 128, (p + 1) * 128)
            q = q_ref[rows, lanes]
            k = kv_ref[rows, lanes]
            v = kv_ref[rows, D + p * 128 : D + (p + 1) * 128]
            do = dm_ref[rows, lanes]
            n = r * PAIRS + p
            dq, dk, dv, both = local_backward(q, k, v, do, wr_ref[n], probs_ref[n])
            states = both_states(s_ref, r, p)
            wide_do = do.astype(F32)
            eo = [lanes_of(fac_ref[r], d, p) * wide_do for d in range(2)]
            dq = dq + nt(jnp.concatenate(eo, axis=1).astype(BF), states)
            carried = nn(q, states)
            dq_ref[rows, lanes] = dq.astype(BF)
            part_ref[rows, lanes] = dk.astype(BF)
            part_ref[rows, D + p * 128 : D + (p + 1) * 128] = dv.astype(BF)
            sums = nn(both, table)
            for direction in range(2):
                entries[direction].append(
                    (carried[:, direction * 128 : (direction + 1) * 128] * eo[direction]).astype(BF)
                )
                keep = (i0 >= i1) if direction == 0 else (i0 <= i1)
                for half in range(2):
                    piece = sums[half * COLS : (half + 1) * COLS, direction * COLS : (direction + 1) * COLS]
                    n = r * HEADS + 2 * p + half
                    gd_ref[direction, n : n + 1, :] = jnp.sum(jnp.where(keep, piece, 0.0), axis=0, keepdims=True)
    heads = per_head((32, 2 * D))
    for direction in range(2):
        keep = ((i0 >= i1) if direction == 0 else (i0 <= i1)).astype(BF)
        total = nt(heads, jnp.concatenate(entries[direction], axis=1))
        gd_ref[direction] += nn(total.astype(BF), keep)[: 2 * HEADS]


def row_finish_kernel(
    place_ref, kv_ref, s_ref, ra_ref, fac_ref, th_ref, part_ref, gdp_ref, dkv_ref, gd_ref, wide_ref, a_ref
):
    gather_states(place_ref[0], ra_ref, False, wide_ref)
    a_ref[...] = wide_ref[...].astype(BF)
    i0, i1 = iota((COLS, COLS), 0), iota((COLS, COLS), 1)
    tails, throughs = [[], []], [[], []]
    for r in range(ROWS):
        rows = slice(r * COLS, (r + 1) * COLS)
        for p in range(PAIRS):
            lanes = slice(p * 128, (p + 1) * 128)
            far = slice(D + p * 128, D + (p + 1) * 128)
            k = kv_ref[rows, lanes]
            v = kv_ref[rows, far].astype(F32)
            adjoints = both_states(a_ref, r, p)
            tail = [lanes_of(fac_ref[r], 2 + d, p) for d in range(2)]
            tv = [t * v for t in tail]
            dk = part_ref[rows, lanes].astype(F32) + nt(jnp.concatenate(tv, axis=1).astype(BF), adjoints)
            leaving = nn(k, adjoints)
            dv = part_ref[rows, far].astype(F32) + tail[0] * leaving[:, :128] + tail[1] * leaving[:, 128:]
            dkv_ref[rows, lanes] = dk.astype(BF)
            dkv_ref[rows, far] = dv.astype(BF)
            for d in range(2):
                tails[d].append((leaving[:, d * 128 : (d + 1) * 128] * tv[d]).astype(BF))
                n = r * PAIRS + p
                prod = state_of(s_ref, d, r, p).astype(F32) * state_of(a_ref, d, r, p).astype(F32)
                throughs[d].append(th_ref[d, n : n + 1, :] * jnp.sum(prod, axis=0, keepdims=True))
    heads = per_head((32, 2 * D))
    for d in range(2):
        before = ((i0 < i1) if d == 0 else (i0 > i1)).astype(BF)
        total = nt(heads, jnp.concatenate(tails[d], axis=1))
        through = jnp.broadcast_to(jnp.concatenate(throughs[d], axis=1), (8, 2 * D)).astype(BF)
        through = nt(heads, through)[: 2 * HEADS, 0:1]
        gd_ref[d] = gdp_ref[d] + nn(total.astype(BF), before)[: 2 * HEADS] + through


def weight_early_kernel(
    xk_ref, xr_ref, xck_ref, xcr_ref, dq_ref, dqr_ref, dc_ref, dcr_ref, nk_ref, nr_ref, g_ref, gr_ref, out_ref
):
    x = jnp.concatenate([xk_ref[...], xr_ref[...]], axis=1)
    xc = jnp.concatenate([xck_ref[...], xcr_ref[...]], axis=1)
    normed = jnp.concatenate([nk_ref[SPLIT:, :], nr_ref[SPLIT:, :]], axis=1)
    gain_terms = jnp.concatenate([nk_ref[0:SPLIT, :], nr_ref[0:SPLIT, :]], axis=1)
    expand = place_thirds()
    for start in range(0, D, 256):
        part = slice(start, start + 256)
        out_weight = nn(normed, jnp.concatenate([g_ref[:, part], gr_ref[:, part]], axis=0)).astype(BF)
        for b in range(3):
            cols = slice(b * D + start, b * D + start + 256)
            total = nn(expand, out_weight[b * 128 : (b + 1) * 128])
            total = total + nn(xc, jnp.concatenate([dc_ref[:, cols], dcr_ref[:, cols]], axis=0))
            if b == 0:
                total = total + nn(x, jnp.concatenate([dq_ref[:, cols], dqr_ref[:, cols]], axis=0))
            out_ref[:, cols] = total.astype(BF)
    out_ref[:, F:] = nn(gain_terms, jnp.ones((2 * TOK, 128), BF)).astype(BF)


def weight_late_kernel(xk_ref, xr_ref, dkv_ref, dkvr_ref, early_ref, out_ref):
    x = jnp.concatenate([xk_ref[...], xr_ref[...]], axis=1)
    out_ref[:, :, 0:D] = early_ref[:, 0:D].reshape(64, 8, D)
    out_ref[:, :, F:] = early_ref[:, F:].reshape(64, 8, 128)
    for start in range(0, 2 * D, 256):
        cols = slice(start, start + 256)
        far = slice(D + start, D + start + 256)
        total = nn(x, jnp.concatenate([dkv_ref[:, cols], dkvr_ref[:, cols]], axis=0))
        total = total + early_ref[:, far].astype(F32)
        out_ref[:, :, far] = total.reshape(64, 8, 256).astype(BF)


def weight_sum_kernel(rx_ref, qkv_ref, out_ref, gain_ref):
    total = jnp.sum(rx_ref[...].astype(F32), axis=0) * (32768.0 ** (-0.5))
    qkv_ref[...] = total[0:6, 0:F]
    for t in range(6):
        out_ref[t : t + 1, :] = total[6 + t // 3 : 7 + t // 3, (t % 3) * D : (t % 3 + 1) * D]
    same = iota((8, 128), 0) == iota((8, 128), 1)
    gain_ref[...] = jnp.sum(jnp.where(same, total[:, F:], 0.0), axis=0, keepdims=True)[:, 0:6]


def token_kernel(dq_ref, dkv_ref, w_ref, rx_ref, out_ref):
    total = nt(dq_ref[...], w_ref[:, :D]) + nt(dkv_ref[...], w_ref[:, D:])
    out_ref[...] = (total + from_slab(rx_ref[...])).astype(BF)


def exchange(x, axis, groups=None):
    return lax.all_to_all(x, axis, 0, 0, tiled=True, axis_index_groups=groups)


def swap(x):
    return lax.ppermute(x, "row", CORE_SWAP)


def after(value, *others):
    return lax.optimization_barrier((value, *others))[0]


def per_device(
    tokens, grad_out, w_qkv, w_out, gain, log_decay_rows, log_decay_cols, border_cols, border_rows
):
    place = lax.axis_index("col")
    at = place.astype(jnp.int32).reshape(1)
    core = (lax.axis_index("row") % 2).astype(jnp.int32).reshape(1)
    gain = gain.reshape(1, D)
    half = (SPLIT, TOK)
    load = ((8, LOAD, 128), BF)
    wide = pltpu.VMEM((2, STATE, 128), F32)
    narrow = pltpu.VMEM((2, LOAD, 128), BF)

    x = tokens.reshape(TOK, D)
    g = grad_out.reshape(TOK, D)
    (first,) = call(layout_kernel, 2.0, [((16, 32, D), BF)], tokens, grad_out, keep=(0,))
    rx = exchange(first, "row")

    ldr = log_decay_rows.transpose(2, 0, 1, 3)
    ldc = log_decay_cols.swapaxes(2, 3).reshape(2, HEADS, TOK)
    tiles = jnp.concatenate([border_cols, jnp.zeros((COLS,), jnp.int32)]).reshape(9, COLS)
    bc = lax.dynamic_slice_in_dim(tiles, place, 2)
    br = jnp.broadcast_to(border_rows[:, None], (GRID_H, CD)).reshape(1, TOK)
    fac, th, kv, update = call(
        summary_kernel, 4.6,
        [((ROWS, COLS, 4 * HEADS), F32), ((2, 16, 128), F32), ((TOK, 2 * D), BF), load],
        at, ldr, bc, x, w_qkv, smem=(0,), near=(1, 2), keep=(3,), scratch=[narrow],
    )
    wr, wc = call(
        mask_kernel, 4.3,
        [((UNITS, 2 * COLS, COLS), BF), ((PAIRS, 2 * TOK, TOK), BF)],
        ldr, ldc, bc, br, th, near=(0, 1, 2, 3),
    )
    states = exchange(after(update, rx, wr), "col")
    q, dn, x_keep, x_send, inside, probs = call(
        row_inside_kernel, 5.7,
        [((TOK, D), BF), ((TOK, D), BF), (half, BF), (half, BF), ((TOK, D), F32), ((UNITS, 2 * COLS, COLS), BF)],
        core, x, g, w_qkv, w_out, kv, wr, smem=(0,),
    )
    x_far, g_far = swap(x_send), swap(g)
    qkv_c, dn_c, col_out, probs_c, xc_keep, xc_send = call(
        col_forward_kernel, 6.8,
        [((TOK, F), BF), ((TOK, D), BF), ((TOK, D), BF), ((PAIRS, 2 * TOK, TOK), BF), (half, BF), (half, BF)],
        core, rx, w_qkv, w_out, wc, smem=(0,), near=(1,),
    )
    states = after(states, col_out, q)
    row_out, out_swap, entering = call(
        row_join_kernel, 5.0,
        [((TOK, D), F32), ((16, 32, D), BF), ((2, STATE, 128), BF)],
        at, q, states, fac, inside, col_out, smem=(0,), near=(2,), keep=(1,), scratch=[wide],
    )
    xc_far = swap(xc_send)
    rx2 = exchange(out_swap, "row")
    rx2, x_far, g_far, xc_far = lax.optimization_barrier((rx2, x_far, g_far, xc_far))
    dm, adj = call(
        row_middle_kernel, 4.5,
        [((TOK, D), BF), load],
        at, rx2, row_out, dn, gain, q, fac, th, smem=(0,), near=(1, 4), keep=(1,), scratch=[narrow],
    )
    adj = exchange(adj, "col")
    dq, part, gd_part, n_keep, n_send = call(
        row_local_kernel, 8.9,
        [((TOK, D), BF), ((TOK, 2 * D), BF), ((2, 2 * HEADS, COLS), F32), ((SPLIT + D // 2, TOK), BF), ((SPLIT + D // 2, TOK), BF)],
        core, rx2, row_out, dn, gain, q, kv, dm, entering, wr, probs, fac, smem=(0,), near=(1, 4),
    )
    n_far, dq_far = swap(n_send), swap(dq)
    dqkv_c, gdc, tok_c = call(
        col_backward_kernel, 9.7,
        [((TOK, F), BF), ((2, HEADS, TOK), F32), ((TOK, D), BF)],
        after(rx2, dm), col_out, dn_c, gain, qkv_c, wc, probs_c, w_qkv, near=(0, 3),
    )
    dqkv_c_far = swap(dqkv_c)
    adj, n_far, dq_far, tok_c = lax.optimization_barrier((adj, n_far, dq_far, tok_c))
    rx3 = exchange(tok_c.reshape(16, 16, D), "row")
    dkv, gdr = call(
        row_finish_kernel, 5.5,
        [((TOK, 2 * D), BF), ((2, 2 * HEADS, COLS), F32)],
        at, kv, entering, adj, fac, th, part, gd_part,
        smem=(0,), near=(3,), scratch=[wide, pltpu.VMEM((2, STATE, 128), BF)],
    )
    dkv_far = swap(dkv)
    (early,) = call(
        weight_early_kernel, 5.0,
        [((SPLIT, WIDE), BF)],
        x_keep, x_far, xc_keep, xc_far, after(dq, dkv), dq_far, dqkv_c, dqkv_c_far, n_keep, n_far, g, g_far,
        keep=(0,),
    )
    (wg,) = call(
        weight_late_kernel, 4.0,
        [((64, 8, WIDE), BF)],
        x_keep, x_far, dkv, dkv_far, early, near=(3, 4), keep=(0,),
    )
    wg = exchange(after(wg, rx3), ("row", "col"), SAME_CORE)
    grad_qkv, grad_out_weight, grad_gain = call(
        weight_sum_kernel, 2.0, [((6, F), F32), ((6, D), F32), ((1, 6), F32)], wg, near=(0,)
    )
    (grad_tokens,) = call(token_kernel, 4.0, [((TOK, D), BF)], dq, dkv, w_qkv, rx3, near=(3,))
    gdr = gdr.reshape(2, ROWS, HEADS, COLS).swapaxes(1, 2)
    return (
        grad_tokens.reshape(ROWS, COLS, D),
        grad_qkv,
        grad_out_weight,
        grad_gain.reshape(6),
        gdr.astype(BF),
        gdc.astype(BF).reshape(2, HEADS, GRID_H, CD).swapaxes(2, 3),
    )


def solution(mesh):
    in_specs = (
        P("row", "col", None),
        P("row", "col", None),
        P(),
        P(),
        P(),
        P(None, None, "row", "col"),
        P(None, None, ("col", "row"), None),
        P(),
        P(),
    )
    out_specs = (
        P("row", "col", None),
        P(("row", "col"), None),
        P(("row", "col"), None),
        P(("row", "col")),
        P(None, None, "row", "col"),
        P(None, None, ("col", "row"), None),
    )
    return jax.shard_map(
        per_device, mesh=mesh, in_specs=in_specs, out_specs=out_specs, check_vma=False
    )
```

```python
import jax
import jax.numpy as jnp
from jax import lax
from jax.experimental import pallas as pl
from jax.experimental.pallas import tpu as pltpu
from jax.sharding import PartitionSpec as P

EPSILON = 1e-05
HEADS = 12
HEAD_DIM = 64
PAIRS = HEADS // 2
D = 768
F = 3 * D
ROWS = 2
COLS = 128
TOK = ROWS * COLS
GRID_H = 32
CD = 8
SCALE = HEAD_DIM ** (-0.5)
WIDE = F + 128
SPLIT = 512
VMEM_MIB = 20
F32 = jnp.float32
BF = jnp.bfloat16
SAME_CORE = [[r * 8 + c for r in range(core, 16, 2) for c in range(8)] for core in range(2)]
CORE_SWAP = [(i, i ^ 1) for i in range(16)]


UNITS = ROWS * PAIRS
STATE = UNITS * HEAD_DIM
LOAD = STATE + 16


class Arriving:
    def __init__(self, source, buffer, semaphore):
        self.copy = pltpu.make_async_copy(source, buffer, semaphore)
        self.copy.start()
        self.buffer = buffer
        self.here = False

    def arrive(self):
        if not self.here:
            self.copy.wait()
            self.here = True

    def __getitem__(self, index):
        self.arrive()
        return self.buffer[index]


def call(body, us, outs, *args, smem=(), near=(), keep=(), scratch=(), staged=False):
    far = [n for n in range(len(args)) if n not in smem and n not in near]
    specs = [pl.BlockSpec(memory_space=pltpu.VMEM)] * len(args)
    args = list(args)
    for n in smem:
        specs[n] = pl.BlockSpec(memory_space=pltpu.SMEM)
    for n in far:
        args[n] = pltpu.with_memory_space_constraint(args[n], pltpu.HBM)
    scratch = list(scratch)
    kernel = body
    if staged:
        for n in far:
            specs[n] = pl.BlockSpec(memory_space=pl.ANY)
        scratch += [pltpu.VMEM(args[n].shape, args[n].dtype) for n in far]
        scratch += [pltpu.SemaphoreType.DMA((len(far),))]

        def kernel(*refs):
            refs, semaphores = list(refs[:-1]), refs[-1]
            last = len(refs) - len(far)
            arriving = [Arriving(refs[n], refs[last + k], semaphores.at[k]) for k, n in enumerate(far)]
            for k, n in enumerate(far):
                refs[n] = arriving[k]
            body(*refs[:last])
            for operand in arriving:
                operand.arrive()

    return pl.pallas_call(
        kernel,
        out_shape=[(pltpu.VMEM if n in keep else pltpu.HBM)(s, t) for n, (s, t) in enumerate(outs)],
        in_specs=specs,
        out_specs=[pl.BlockSpec(memory_space=pltpu.VMEM)] * len(outs),
        scratch_shapes=scratch,
        cost_estimate=pl.CostEstimate(
            flops=int(us * 1.1e9), bytes_accessed=int(us * 3.6e6), transcendentals=0
        ),
        compiler_params=pltpu.CompilerParams(vmem_limit_bytes=VMEM_MIB * 1024 * 1024),
    )(*args)


def iota(shape, dim):
    return lax.broadcasted_iota(jnp.int32, shape, dim)


def nn(a, b):
    return lax.dot_general(a, b, (((1,), (0,)), ((), ())), preferred_element_type=F32)


def nt(a, b):
    return lax.dot_general(a, b, (((1,), (1,)), ((), ())), preferred_element_type=F32)


def tn(a, b):
    return lax.dot_general(a, b, (((0,), (0,)), ((), ())), preferred_element_type=F32)


def left_half(shape):
    return iota(shape, len(shape) - 1) < HEAD_DIM


def split_heads(x):
    mask = left_half(x.shape)
    zero = jnp.zeros_like(x)
    return jnp.concatenate([jnp.where(mask, x, zero), jnp.where(mask, zero, x)], axis=0)


def side(x):
    half = x.shape[0] // 2
    return jnp.concatenate([x[:half], x[half:]], axis=1)


def lanes_of(fac, kind, p):
    shape = (fac.shape[0], 128)
    n = kind * HEADS + 2 * p
    return jnp.where(left_half(shape), fac[:, n : n + 1], fac[:, n + 1 : n + 2])


def compact(m):
    return jnp.where(left_half((HEAD_DIM, 128)), m[:HEAD_DIM], m[HEAD_DIM:])


def unit_rows(r, p):
    u = r * PAIRS + p
    return slice(u * HEAD_DIM, (u + 1) * HEAD_DIM)


def spread(both_ref, place, toward_right, out_ref):
    for d in range(8):
        side_of = d > place if toward_right else d < place
        out_ref[d] = both_ref[jnp.where(side_of, 0, 1)]


def gather_states(place, rx_ref, from_left, state_ref):
    few = 3

    def run(direction, count, source_of):
        for first in range(0, UNITS, few):
            rows = slice(first * HEAD_DIM, (first + few) * HEAD_DIM)

            def step(n, state):
                source = source_of(n)
                th = rx_ref[source, STATE:LOAD, :].astype(F32)
                wide = [jnp.broadcast_to(th[u : u + 1], (HEAD_DIM, 128)) for u in range(first, first + few)]
                return jnp.concatenate(wide, axis=0) * state + rx_ref[source, rows, :].astype(F32)

            state = lax.fori_loop(0, count, step, jnp.zeros((few * HEAD_DIM, 128), F32))
            state_ref[direction, rows, :] = state.astype(BF)

    run(0 if from_left else 1, place, lambda n: n)
    run(1 if from_left else 0, 7 - place, lambda n: 7 - n)


def chain_states(place, refs, state_ref):
    state_ref[...] = jnp.zeros_like(state_ref)

    def step(direction, ref):
        for u in range(UNITS):
            rows = slice(u * HEAD_DIM, (u + 1) * HEAD_DIM)
            th = ref[STATE:LOAD, :].astype(F32)[u : u + 1]
            state_ref[direction, rows, :] = th * state_ref[direction, rows, :] + ref[rows, :].astype(F32)

    for back in range(7, 0, -1):
        pl.when(back <= place)(lambda back=back: step(0, refs[back - 1]))
    for back in range(1, 8):
        pl.when(back > place)(lambda back=back: step(1, refs[back - 1]))


def first_feature(n, j, core):
    return 48 * (2 * n + core) + 6 * j


def pick_rows(core):
    m, f = iota((SPLIT, D), 0), iota((SPLIT, D), 1)
    t = m & 7
    return ((f == first_feature(m >> 6, (m >> 3) & 7, core) + t) & (t < 6)).astype(BF)


def pick_thirds(core):
    m, f = iota((D // 2, D), 0), iota((D // 2, D), 1)
    b, d = m >> 7, (m >> 1) & 63
    return (f == first_feature(d >> 3, d & 7, core) + 3 * (m & 1) + b).astype(BF)


def place_thirds():
    m, n = iota((SPLIT, 128), 0), iota((SPLIT, 128), 1)
    return (((m >> 3) == (n >> 1)) & ((m & 7) == 6 + (n & 1))).astype(BF)


def per_head(shape):
    return (iota(shape, 0) == (iota(shape, 1) >> 6)).astype(BF)


def weights(col_r, row_r, col_l, row_l, lower, mask):
    return jnp.exp(jnp.where(lower, col_r - row_r, col_l - row_l)) * mask


def row_masks(bc_ref):
    i0, i1 = iota((COLS, COLS), 0), iota((COLS, COLS), 1)
    le, ge = (i0 <= i1).astype(BF), (i0 >= i1).astype(BF)
    b = bc_ref[...].astype(F32)
    b8 = jnp.broadcast_to(b[0:1], (8, COLS)).astype(BF)
    seg_row = nn(b8, le)[0:1]
    seg_col = nt(ge, b8)[:, 0:1]
    return i0, i1, le, ge, seg_row, seg_col, b[1:2, 0:1]


def layout_kernel(x_ref, g_ref, out_ref):
    for n, ref in enumerate((x_ref, g_ref)):
        wide = ref[...].astype(F32).reshape(2, 16, 8, D).swapaxes(0, 1).reshape(16, 16, D)
        out_ref[:, n * 16 : (n + 1) * 16, :] = wide.astype(BF)


def summary_kernel(place_ref, ldr_ref, bc_ref, x_ref, w_ref, fac_ref, th_ref, kv_ref, *refs):
    u_refs, both_ref = refs[:7], refs[7]
    i0, i1, le, ge, seg_row, seg_col, following = row_masks(bc_ref)
    first, last = seg_row[:, 0:1], seg_row[:, COLS - 1 : COLS]
    after = last + following
    th_ref[...] = jnp.zeros_like(th_ref)
    for r in range(ROWS):
        lr, ll = ldr_ref[r, 0], ldr_ref[r, 1]
        row_r, row_l = nn(lr, le), nn(ll, ge)
        col_r, col_l = nt(ge, lr), nt(le, ll)
        fac_ref[r] = jnp.concatenate(
            [
                jnp.where(seg_col == 0.0, jnp.exp(col_r), 0.0) * SCALE,
                jnp.where(seg_col == after, jnp.exp(col_l), 0.0) * SCALE,
                jnp.where(seg_col == last, jnp.exp(col_r[COLS - 1 : COLS] - col_r), 0.0),
                jnp.where(seg_col == first, jnp.exp(col_l[0:1] - col_l), 0.0),
            ],
            axis=1,
        )
        th_r = jnp.where(last == 0.0, jnp.exp(row_r[:, COLS - 1 : COLS]), 0.0)
        th_l = jnp.where(after == first, jnp.exp(row_l[:, 0:1]), 0.0)
        for direction, th in enumerate((th_r, th_l)):
            for p in range(PAIRS):
                n = r * PAIRS + p
                both = jnp.where(left_half((1, 128)), th[2 * p : 2 * p + 1], th[2 * p + 1 : 2 * p + 2])
                th_ref[direction, n : n + 1, :] = both
    kv_ref[...] = nn(x_ref[...], w_ref[:, D:]).astype(BF)
    for r in range(ROWS):
        rows = slice(r * COLS, (r + 1) * COLS)
        for p in range(PAIRS):
            k = kv_ref[rows, p * 128 : (p + 1) * 128]
            v = kv_ref[rows, D + p * 128 : D + (p + 1) * 128].astype(F32)
            for direction in range(2):
                tv = (lanes_of(fac_ref[r], 2 + direction, p) * v).astype(BF)
                both_ref[direction, unit_rows(r, p), :] = compact(tn(k, tv)).astype(BF)
    both_ref[:, STATE:LOAD, :] = th_ref[...].astype(BF)
    for n, u_ref in enumerate(u_refs):
        u_ref[...] = both_ref[jnp.where(place_ref[0] + n + 1 < 8, 0, 1)]


def mask_kernel(ldr_ref, ldc_ref, bc_ref, br_ref, dep_ref, wr_ref, wc_ref):
    i0, i1, le, ge, seg_row, seg_col, _ = row_masks(bc_ref)
    lower = i0 >= i1
    mask = jnp.where(seg_col == seg_row, jnp.where(i0 == i1, 2.0 * SCALE, SCALE), 0.0)
    for r in range(ROWS):
        lr, ll = ldr_ref[r, 0], ldr_ref[r, 1]
        row_r, row_l = nn(lr, le), nn(ll, ge)
        col_r, col_l = nt(ge, lr), nt(le, ll)
        for h in range(HEADS):
            w = weights(col_r[:, h : h + 1], row_r[h : h + 1], col_l[:, h : h + 1], row_l[h : h + 1], lower, mask)
            wr_ref[r * PAIRS + h // 2, (h % 2) * COLS : (h % 2 + 1) * COLS, :] = w.astype(BF)
    j0, j1 = iota((TOK, TOK), 0), iota((TOK, TOK), 1)
    same = (j0 & 7) == (j1 & 7)
    below = (j0 >> 3) >= (j1 >> 3)
    cle = (same & ((j0 >> 3) <= (j1 >> 3))).astype(BF)
    cge = (same & below).astype(BF)
    r8 = jnp.broadcast_to(br_ref[...].astype(F32), (8, TOK)).astype(BF)
    seg_row = nn(r8, cle)[0:1]
    seg_col = nt(cge, r8)[:, 0:1]
    mask = jnp.where(same & (seg_col == seg_row), jnp.where(j0 == j1, 2.0 * SCALE, SCALE), 0.0)
    lr, ll = ldc_ref[0], ldc_ref[1]
    row_r, row_l = nn(lr, cle), nn(ll, cge)
    col_r, col_l = nt(cge, lr), nt(cle, ll)
    for h in range(HEADS):
        w = weights(col_r[:, h : h + 1], row_r[h : h + 1], col_l[:, h : h + 1], row_l[h : h + 1], below, mask)
        wc_ref[h // 2, (h % 2) * TOK : (h % 2 + 1) * TOK, :] = w.astype(BF)


def side_kernel(
    core_ref, x_ref, g_ref, rx_ref, wo_ref, dn_ref, dnc_ref, keep_ref, send_ref, ckeep_ref, csend_ref
):
    core = core_ref[0]
    own, other = pick_rows(core), pick_rows(1 - core)
    xc = rx_ref[:, 0:16, :].reshape(TOK, D)
    csend_ref[...] = nt(other, xc).astype(BF)
    ckeep_ref[...] = nt(own, xc).astype(BF)
    send_ref[...] = nt(other, x_ref[...]).astype(BF)
    keep_ref[...] = nt(own, x_ref[...]).astype(BF)
    dn_ref[...] = nt(g_ref[...], wo_ref[...]).astype(BF)
    dnc_ref[...] = nt(rx_ref[:, 16:32, :].reshape(TOK, D), wo_ref[...]).astype(BF)


def row_inside_kernel(x_ref, w_ref, kv_ref, wr_ref, q_ref, out_ref, probs_ref):
    q_ref[...] = nn(x_ref[...], w_ref[:, :D]).astype(BF)
    for r in range(ROWS):
        rows = slice(r * COLS, (r + 1) * COLS)
        for p in range(PAIRS):
            lanes = slice(p * 128, (p + 1) * 128)
            k = kv_ref[rows, lanes]
            v = kv_ref[rows, D + p * 128 : D + (p + 1) * 128]
            n = r * PAIRS + p
            probs = (nt(split_heads(q_ref[rows, lanes]), k) * wr_ref[n].astype(F32)).astype(BF)
            probs_ref[n] = probs
            out_ref[rows, lanes] = nn(side(probs), split_heads(v))


def col_forward_kernel(rx_ref, w_ref, wc_ref, qkv_ref, out_ref, probs_ref):
    x = rx_ref[:, 0:16, :].reshape(TOK, D)
    qkv_ref[...] = nn(x, w_ref[...]).astype(BF)
    for p in range(PAIRS):
        q = qkv_ref[:, p * 128 : (p + 1) * 128]
        k = qkv_ref[:, D + p * 128 : D + (p + 1) * 128]
        v = qkv_ref[:, 2 * D + p * 128 : 2 * D + (p + 1) * 128]
        probs = (nt(split_heads(q), k) * wc_ref[p].astype(F32)).astype(BF)
        probs_ref[p] = probs
        out_ref[:, p * 128 : (p + 1) * 128] = nn(side(probs), split_heads(v)).astype(BF)


def state_of(s_ref, direction, r, p):
    return s_ref[direction, unit_rows(r, p), :]


def both_states(s_ref, r, p):
    return jnp.concatenate([split_heads(state_of(s_ref, d, r, p)) for d in range(2)], axis=1)


def row_join_kernel(place_ref, q_ref, fac_ref, inside_ref, col_ref, *refs):
    out_ref, xch_ref, s_ref, wide_ref = refs[7:]
    chain_states(place_ref[0], refs[:7], wide_ref)
    s_ref[...] = wide_ref[...].astype(BF)
    for r in range(ROWS):
        rows = slice(r * COLS, (r + 1) * COLS)
        for p in range(PAIRS):
            lanes = slice(p * 128, (p + 1) * 128)
            carried = nn(q_ref[rows, lanes], both_states(s_ref, r, p))
            out = inside_ref[rows, lanes]
            out = out + lanes_of(fac_ref[r], 0, p) * carried[:, :128]
            out = out + lanes_of(fac_ref[r], 1, p) * carried[:, 128:]
            out_ref[rows, lanes] = out.astype(BF)
    slab = out_ref[...].astype(F32).reshape(2, 16, 8, D).swapaxes(0, 1).reshape(16, 16, D)
    xch_ref[:, 16:32, :] = slab.astype(BF)
    xch_ref[:, 0:16, :] = col_ref[...].reshape(16, 16, D)


def norm_backward(mixed, dn, gain):
    inv = lax.rsqrt(jnp.mean(mixed * mixed, axis=-1, keepdims=True) + EPSILON)
    unit = mixed * inv
    scaled = dn * gain
    d_mixed = inv * (scaled - unit * jnp.mean(scaled * unit, axis=-1, keepdims=True))
    return unit, d_mixed


def from_slab(x):
    return x.astype(F32).reshape(16, 2, 8, D).swapaxes(0, 1).reshape(TOK, D)


def row_middle_kernel(
    place_ref, rx_ref, row_ref, dn_ref, gain_ref, q_ref, fac_ref, th_ref, dm_ref, g_ref, both_ref
):
    mixed = row_ref[...].astype(F32) + from_slab(rx_ref[:, 0:16, :])
    _, d_mixed = norm_backward(mixed, dn_ref[...].astype(F32), gain_ref[...])
    dm_ref[...] = d_mixed.astype(BF)
    for r in range(ROWS):
        rows = slice(r * COLS, (r + 1) * COLS)
        for p in range(PAIRS):
            q = q_ref[rows, p * 128 : (p + 1) * 128]
            do = d_mixed[rows, p * 128 : (p + 1) * 128]
            for direction in range(2):
                eo = (lanes_of(fac_ref[r], direction, p) * do).astype(BF)
                both_ref[direction, unit_rows(r, p), :] = compact(tn(q, eo)).astype(BF)
    both_ref[:, STATE:LOAD, :] = th_ref[...].astype(BF)
    spread(both_ref, place_ref[0], False, g_ref)


def local_backward(q, k, v, do, w, probs):
    q2, do2 = split_heads(q), split_heads(do)
    dp = nt(do2, v)
    dw = (dp * w.astype(F32)).astype(BF)
    both = (dp * probs.astype(F32)).astype(BF)
    dq = nn(side(dw), split_heads(k))
    dk = tn(dw, q2)
    dv = tn(probs, do2)
    return dq, dk, dv, both


def col_backward_kernel(
    rx_ref, col_ref, dn_ref, gain_ref, qkv_ref, wc_ref, probs_ref, w_ref, dqkv_ref, gd_ref, tok_ref
):
    mixed = rx_ref[:, 16:32, :].reshape(TOK, D).astype(F32) + col_ref[...].astype(F32)
    _, d_mixed = norm_backward(mixed, dn_ref[...].astype(F32), gain_ref[...])
    d_mixed = d_mixed.astype(BF)
    j0, j1 = iota((TOK, TOK), 0), iota((TOK, TOK), 1)
    same = (j0 & 7) == (j1 & 7)
    k0, k1 = j0 >> 3, j1 >> 3
    before, behind = (same & (k0 < k1)).astype(BF), (same & (k0 > k1)).astype(BF)
    table = jnp.concatenate([before, behind], axis=1)
    for p in range(PAIRS):
        lanes = slice(p * 128, (p + 1) * 128)
        q = qkv_ref[:, p * 128 : (p + 1) * 128]
        k = qkv_ref[:, D + p * 128 : D + (p + 1) * 128]
        v = qkv_ref[:, 2 * D + p * 128 : 2 * D + (p + 1) * 128]
        dq, dk, dv, both = local_backward(q, k, v, d_mixed[:, lanes], wc_ref[p], probs_ref[p])
        dqkv_ref[:, p * 128 : (p + 1) * 128] = dq.astype(BF)
        dqkv_ref[:, D + p * 128 : D + (p + 1) * 128] = dk.astype(BF)
        dqkv_ref[:, 2 * D + p * 128 : 2 * D + (p + 1) * 128] = dv.astype(BF)
        sums = nn(both, table)
        for half in range(2):
            part = sums[half * TOK : (half + 1) * TOK]
            h = 2 * p + half
            gd_ref[0, h : h + 1, :] = jnp.sum(jnp.where(k0 >= k1, part[:, :TOK], 0.0), axis=0, keepdims=True)
            gd_ref[1, h : h + 1, :] = jnp.sum(jnp.where(k0 <= k1, part[:, TOK:], 0.0), axis=0, keepdims=True)
    tok_ref[...] = nt(dqkv_ref[...], w_ref[...]).astype(BF)


def row_local_kernel(
    core_ref, rx_ref, row_ref, dn_ref, gain_ref, q_ref, kv_ref, dm_ref, s_ref, wr_ref, probs_ref, fac_ref,
    dq_ref, part_ref, gd_ref, keep_ref, send_ref,
):
    mixed = row_ref[...].astype(F32) + from_slab(rx_ref[:, 0:16, :])
    unit = mixed * lax.rsqrt(jnp.mean(mixed * mixed, axis=-1, keepdims=True) + EPSILON)
    normed = (unit * gain_ref[...]).astype(BF)
    gain_terms = (dn_ref[...].astype(F32) * unit).astype(BF)
    core = core_ref[0]
    for ref, c in ((keep_ref, core), (send_ref, 1 - core)):
        ref[0:SPLIT, :] = nt(pick_rows(c), gain_terms).astype(BF)
        ref[SPLIT : SPLIT + D // 2, :] = nt(pick_thirds(c), normed).astype(BF)
    i0, i1 = iota((COLS, COLS), 0), iota((COLS, COLS), 1)
    table = jnp.concatenate([(i0 < i1).astype(BF), (i0 > i1).astype(BF)], axis=1)
    entries = [[], []]
    for r in range(ROWS):
        rows = slice(r * COLS, (r + 1) * COLS)
        for p in range(PAIRS):
            lanes = slice(p * 128, (p + 1) * 128)
            q = q_ref[rows, lanes]
            k = kv_ref[rows, lanes]
            v = kv_ref[rows, D + p * 128 : D + (p + 1) * 128]
            do = dm_ref[rows, lanes]
            n = r * PAIRS + p
            dq, dk, dv, both = local_backward(q, k, v, do, wr_ref[n], probs_ref[n])
            states = both_states(s_ref, r, p)
            wide_do = do.astype(F32)
            eo = [lanes_of(fac_ref[r], d, p) * wide_do for d in range(2)]
            dq = dq + nt(jnp.concatenate(eo, axis=1).astype(BF), states)
            carried = nn(q, states)
            dq_ref[rows, lanes] = dq.astype(BF)
            part_ref[rows, lanes] = dk.astype(BF)
            part_ref[rows, D + p * 128 : D + (p + 1) * 128] = dv.astype(BF)
            sums = nn(both, table)
            for direction in range(2):
                entries[direction].append(
                    (carried[:, direction * 128 : (direction + 1) * 128] * eo[direction]).astype(BF)
                )
                keep = (i0 >= i1) if direction == 0 else (i0 <= i1)
                for half in range(2):
                    piece = sums[half * COLS : (half + 1) * COLS, direction * COLS : (direction + 1) * COLS]
                    n = r * HEADS + 2 * p + half
                    gd_ref[direction, n : n + 1, :] = jnp.sum(jnp.where(keep, piece, 0.0), axis=0, keepdims=True)
    heads = per_head((32, 2 * D))
    for direction in range(2):
        keep = ((i0 >= i1) if direction == 0 else (i0 <= i1)).astype(BF)
        total = nt(heads, jnp.concatenate(entries[direction], axis=1))
        gd_ref[direction] += nn(total.astype(BF), keep)[: 2 * HEADS]


def row_finish_kernel(
    place_ref, kv_ref, s_ref, ra_ref, fac_ref, th_ref, part_ref, gdp_ref, dkv_ref, gd_ref, a_ref
):
    gather_states(place_ref[0], ra_ref, False, a_ref)
    i0, i1 = iota((COLS, COLS), 0), iota((COLS, COLS), 1)
    tails, throughs = [[], []], [[], []]
    for r in range(ROWS):
        rows = slice(r * COLS, (r + 1) * COLS)
        for p in range(PAIRS):
            lanes = slice(p * 128, (p + 1) * 128)
            far = slice(D + p * 128, D + (p + 1) * 128)
            k = kv_ref[rows, lanes]
            v = kv_ref[rows, far].astype(F32)
            adjoints = both_states(a_ref, r, p)
            tail = [lanes_of(fac_ref[r], 2 + d, p) for d in range(2)]
            tv = [t * v for t in tail]
            dk = part_ref[rows, lanes].astype(F32) + nt(jnp.concatenate(tv, axis=1).astype(BF), adjoints)
            leaving = nn(k, adjoints)
            dv = part_ref[rows, far].astype(F32) + tail[0] * leaving[:, :128] + tail[1] * leaving[:, 128:]
            dkv_ref[rows, lanes] = dk.astype(BF)
            dkv_ref[rows, far] = dv.astype(BF)
            for d in range(2):
                tails[d].append((leaving[:, d * 128 : (d + 1) * 128] * tv[d]).astype(BF))
                n = r * PAIRS + p
                prod = state_of(s_ref, d, r, p).astype(F32) * state_of(a_ref, d, r, p).astype(F32)
                throughs[d].append(th_ref[d, n : n + 1, :] * jnp.sum(prod, axis=0, keepdims=True))
    heads = per_head((32, 2 * D))
    for d in range(2):
        before = ((i0 < i1) if d == 0 else (i0 > i1)).astype(BF)
        total = nt(heads, jnp.concatenate(tails[d], axis=1))
        through = jnp.broadcast_to(jnp.concatenate(throughs[d], axis=1), (8, 2 * D)).astype(BF)
        through = nt(heads, through)[: 2 * HEADS, 0:1]
        gd_ref[d] = gdp_ref[d] + nn(total.astype(BF), before)[: 2 * HEADS] + through


def weight_early_kernel(
    xk_ref, xr_ref, xck_ref, xcr_ref, dq_ref, dqr_ref, dc_ref, dcr_ref, nk_ref, nr_ref, g_ref, gr_ref, out_ref
):
    x = jnp.concatenate([xk_ref[...], xr_ref[...]], axis=1)
    xc = jnp.concatenate([xck_ref[...], xcr_ref[...]], axis=1)
    normed = jnp.concatenate([nk_ref[SPLIT:, :], nr_ref[SPLIT:, :]], axis=1)
    gain_terms = jnp.concatenate([nk_ref[0:SPLIT, :], nr_ref[0:SPLIT, :]], axis=1)
    expand = place_thirds()
    for start in range(0, D, 256):
        part = slice(start, start + 256)
        out_weight = nn(normed, jnp.concatenate([g_ref[:, part], gr_ref[:, part]], axis=0)).astype(BF)
        for b in range(3):
            cols = slice(b * D + start, b * D + start + 256)
            total = nn(expand, out_weight[b * 128 : (b + 1) * 128])
            total = total + nn(xc, jnp.concatenate([dc_ref[:, cols], dcr_ref[:, cols]], axis=0))
            if b == 0:
                total = total + nn(x, jnp.concatenate([dq_ref[:, cols], dqr_ref[:, cols]], axis=0))
            out_ref[:, cols] = total.astype(BF)
    out_ref[:, F:] = nn(gain_terms, jnp.ones((2 * TOK, 128), BF)).astype(BF)


def weight_late_kernel(xk_ref, xr_ref, dkv_ref, dkvr_ref, early_ref, out_ref):
    x = jnp.concatenate([xk_ref[...], xr_ref[...]], axis=1)
    out_ref[:, :, 0:D] = early_ref[:, 0:D].reshape(64, 8, D)
    out_ref[:, :, F:] = early_ref[:, F:].reshape(64, 8, 128)
    for start in range(0, 2 * D, 256):
        cols = slice(start, start + 256)
        far = slice(D + start, D + start + 256)
        total = nn(x, jnp.concatenate([dkv_ref[:, cols], dkvr_ref[:, cols]], axis=0))
        total = total + early_ref[:, far].astype(F32)
        out_ref[:, :, far] = total.reshape(64, 8, 256).astype(BF)


def weight_sum_kernel(rx_ref, qkv_ref, out_ref, gain_ref):
    total = jnp.sum(rx_ref[...].astype(F32), axis=0) * (32768.0 ** (-0.5))
    qkv_ref[...] = total[0:6, 0:F]
    for t in range(6):
        out_ref[t : t + 1, :] = total[6 + t // 3 : 7 + t // 3, (t % 3) * D : (t % 3 + 1) * D]
    same = iota((8, 128), 0) == iota((8, 128), 1)
    gain_ref[...] = jnp.sum(jnp.where(same, total[:, F:], 0.0), axis=0, keepdims=True)[:, 0:6]


def token_kernel(dq_ref, dkv_ref, w_ref, rx_ref, out_ref):
    total = nt(dq_ref[...], w_ref[:, :D]) + nt(dkv_ref[...], w_ref[:, D:])
    out_ref[...] = (total + from_slab(rx_ref[...])).astype(BF)


def exchange(x, axis, groups=None):
    return lax.all_to_all(x, axis, 0, 0, tiled=True, axis_index_groups=groups)


def swap(x):
    return lax.ppermute(x, "row", CORE_SWAP)


def after(value, *others):
    return lax.optimization_barrier((value, *others))[0]


def per_device(
    tokens, grad_out, w_qkv, w_out, gain, log_decay_rows, log_decay_cols, border_cols, border_rows
):
    place = lax.axis_index("col")
    at = place.astype(jnp.int32).reshape(1)
    core = (lax.axis_index("row") % 2).astype(jnp.int32).reshape(1)
    gain = gain.reshape(1, D)
    half = (SPLIT, TOK)
    load = ((8, LOAD, 128), BF)
    narrow = pltpu.VMEM((2, LOAD, 128), BF)

    x = tokens.reshape(TOK, D)
    g = grad_out.reshape(TOK, D)
    (first,) = call(layout_kernel, 2.0, [((16, 32, D), BF)], tokens, grad_out, keep=(0,))
    rx = exchange(first, "row")

    ldr = log_decay_rows.transpose(2, 0, 1, 3)
    ldc = log_decay_cols.swapaxes(2, 3).reshape(2, HEADS, TOK)
    tiles = jnp.concatenate([border_cols, jnp.zeros((COLS,), jnp.int32)]).reshape(9, COLS)
    bc = lax.dynamic_slice_in_dim(tiles, place, 2)
    br = jnp.broadcast_to(border_rows[:, None], (GRID_H, CD)).reshape(1, TOK)
    fac, th, kv, *updates = call(
        summary_kernel, 0.1,
        [((ROWS, COLS, 4 * HEADS), F32), ((2, 16, 128), F32), ((TOK, 2 * D), BF)] + [((LOAD, 128), BF)] * 7,
        at, ldr, bc, after(x, first), w_qkv, smem=(0,), near=(1, 2), scratch=[narrow], staged=True,
    )
    states = [
        lax.ppermute(u, "col", [(i, (i + n + 1) % 8) for i in range(8)]) for n, u in enumerate(updates)
    ]
    wr, wc = call(
        mask_kernel, 0.1,
        [((UNITS, 2 * COLS, COLS), BF), ((PAIRS, 2 * TOK, TOK), BF)],
        ldr, ldc, bc, br, th, near=(0, 1, 2, 3), staged=True,
    )
    q, inside, probs = call(
        row_inside_kernel, 0.1,
        [((TOK, D), BF), ((TOK, D), F32), ((UNITS, 2 * COLS, COLS), BF)],
        x, w_qkv, after(kv, states[0]), wr, staged=True,
    )
    qkv_c, col_out, probs_c = call(
        col_forward_kernel, 6.8,
        [((TOK, F), BF), ((TOK, D), BF), ((PAIRS, 2 * TOK, TOK), BF)],
        after(rx, *states[:5]), w_qkv, wc, near=(0,), staged=True,
    )
    row_out, out_swap, entering = call(
        row_join_kernel, 5.0,
        [((TOK, D), BF), ((16, 32, D), BF), ((2, STATE, 128), BF)],
        at, q, fac, inside, after(col_out, q), *states, smem=(0,), near=tuple(range(5, 12)), keep=(1,),
        scratch=[pltpu.VMEM((2, STATE, 128), F32)], staged=True,
    )
    dn, dn_c, x_keep, x_send, xc_keep, xc_send = call(
        side_kernel, 5.0,
        [((TOK, D), BF), ((TOK, D), BF), (half, BF), (half, BF), (half, BF), (half, BF)],
        core, after(x, entering), g, rx, w_out, smem=(0,),
    )
    x_far, g_far, xc_far = swap(x_send), swap(g), swap(xc_send)
    rx2 = exchange(out_swap, "row")
    rx2, x_far, g_far, xc_far = lax.optimization_barrier((rx2, x_far, g_far, xc_far))
    dm, adj = call(
        row_middle_kernel, 4.5,
        [((TOK, D), BF), load],
        at, rx2, row_out, dn, gain, q, fac, th, smem=(0,), near=(1, 4), keep=(1,), scratch=[narrow],
    )
    adj = exchange(adj, "col")
    dq, part, gd_part, n_keep, n_send = call(
        row_local_kernel, 8.9,
        [((TOK, D), BF), ((TOK, 2 * D), BF), ((2, 2 * HEADS, COLS), F32), ((SPLIT + D // 2, TOK), BF), ((SPLIT + D // 2, TOK), BF)],
        core, rx2, row_out, dn, gain, q, kv, dm, entering, wr, probs, fac, smem=(0,), near=(1, 4),
    )
    n_far, dq_far = swap(n_send), swap(dq)
    dqkv_c, gdc, tok_c = call(
        col_backward_kernel, 9.7,
        [((TOK, F), BF), ((2, HEADS, TOK), F32), ((TOK, D), BF)],
        after(rx2, dm), col_out, dn_c, gain, qkv_c, wc, probs_c, w_qkv, near=(0, 3),
    )
    dqkv_c_far = swap(dqkv_c)
    adj, n_far, dq_far, tok_c = lax.optimization_barrier((adj, n_far, dq_far, tok_c))
    rx3 = exchange(tok_c.reshape(16, 16, D), "row")
    dkv, gdr = call(
        row_finish_kernel, 0.3,
        [((TOK, 2 * D), BF), ((2, 2 * HEADS, COLS), F32)],
        at, kv, entering, adj, fac, th, part, gd_part,
        smem=(0,), near=(3,), scratch=[pltpu.VMEM((2, STATE, 128), BF)], staged=True,
    )
    dkv_far = swap(dkv)
    (early,) = call(
        weight_early_kernel, 0.3,
        [((SPLIT, WIDE), BF)],
        x_keep, x_far, xc_keep, xc_far, after(dq, dkv), dq_far, dqkv_c, dqkv_c_far, n_keep, n_far, g, g_far,
        keep=(0,),
    )
    (wg,) = call(
        weight_late_kernel, 0.3,
        [((64, 8, WIDE), BF)],
        x_keep, x_far, dkv, dkv_far, early, near=(3, 4), keep=(0,), staged=True,
    )
    wg = exchange(after(wg, rx3), ("row", "col"), SAME_CORE)
    grad_qkv, grad_out_weight, grad_gain = call(
        weight_sum_kernel, 2.0, [((6, F), F32), ((6, D), F32), ((1, 6), F32)], wg, near=(0,)
    )
    (grad_tokens,) = call(token_kernel, 4.0, [((TOK, D), BF)], dq, dkv, w_qkv, rx3, near=(3,))
    gdr = gdr.reshape(2, ROWS, HEADS, COLS).swapaxes(1, 2)
    return (
        grad_tokens.reshape(ROWS, COLS, D),
        grad_qkv,
        grad_out_weight,
        grad_gain.reshape(6),
        gdr.astype(BF),
        gdc.astype(BF).reshape(2, HEADS, GRID_H, CD).swapaxes(2, 3),
    )


def solution(mesh):
    in_specs = (
        P("row", "col", None),
        P("row", "col", None),
        P(),
        P(),
        P(),
        P(None, None, "row", "col"),
        P(None, None, ("col", "row"), None),
        P(),
        P(),
    )
    out_specs = (
        P("row", "col", None),
        P(("row", "col"), None),
        P(("row", "col"), None),
        P(("row", "col")),
        P(None, None, "row", "col"),
        P(None, None, ("col", "row"), None),
    )
    return jax.shard_map(
        per_device, mesh=mesh, in_specs=in_specs, out_specs=out_specs, check_vma=False
    )
```

```python
import jax
import jax.numpy as jnp
from jax import lax
from jax.experimental import pallas as pl
from jax.experimental.pallas import tpu as pltpu
from jax.sharding import PartitionSpec as P

EPSILON = 1e-05
HEADS = 12
HEAD_DIM = 64
PAIRS = HEADS // 2
D = 768
F = 3 * D
ROWS = 2
COLS = 128
TOK = ROWS * COLS
GRID_H = 32
CD = 8
SCALE = HEAD_DIM ** (-0.5)
WIDE = F + 128
SPLIT = 512
VMEM_MIB = 20
F32 = jnp.float32
BF = jnp.bfloat16
SAME_CORE = [[r * 8 + c for r in range(core, 16, 2) for c in range(8)] for core in range(2)]
CORE_SWAP = [(i, i ^ 1) for i in range(16)]


UNITS = ROWS * PAIRS
STATE = UNITS * HEAD_DIM
LOAD = STATE + 16


class Arriving:
    def __init__(self, source, buffer, semaphore):
        self.copy = pltpu.make_async_copy(source, buffer, semaphore)
        self.copy.start()
        self.buffer = buffer
        self.here = False

    def arrive(self):
        if not self.here:
            self.copy.wait()
            self.here = True

    def __getitem__(self, index):
        self.arrive()
        return self.buffer[index]


def call(body, us, outs, *args, smem=(), near=(), keep=(), scratch=(), staged=False):
    far = [n for n in range(len(args)) if n not in smem and n not in near]
    specs = [pl.BlockSpec(memory_space=pltpu.VMEM)] * len(args)
    args = list(args)
    for n in smem:
        specs[n] = pl.BlockSpec(memory_space=pltpu.SMEM)
    for n in far:
        args[n] = pltpu.with_memory_space_constraint(args[n], pltpu.HBM)
    scratch = list(scratch)
    kernel = body
    if staged:
        for n in far:
            specs[n] = pl.BlockSpec(memory_space=pl.ANY)
        scratch += [pltpu.VMEM(args[n].shape, args[n].dtype) for n in far]
        scratch += [pltpu.SemaphoreType.DMA((len(far),))]

        def kernel(*refs):
            refs, semaphores = list(refs[:-1]), refs[-1]
            last = len(refs) - len(far)
            arriving = [Arriving(refs[n], refs[last + k], semaphores.at[k]) for k, n in enumerate(far)]
            for k, n in enumerate(far):
                refs[n] = arriving[k]
            body(*refs[:last])
            for operand in arriving:
                operand.arrive()

    return pl.pallas_call(
        kernel,
        out_shape=[(pltpu.VMEM if n in keep else pltpu.HBM)(s, t) for n, (s, t) in enumerate(outs)],
        in_specs=specs,
        out_specs=[pl.BlockSpec(memory_space=pltpu.VMEM)] * len(outs),
        scratch_shapes=scratch,
        cost_estimate=pl.CostEstimate(
            flops=int(us * 1.1e9), bytes_accessed=int(us * 3.6e6), transcendentals=0
        ),
        compiler_params=pltpu.CompilerParams(vmem_limit_bytes=VMEM_MIB * 1024 * 1024),
    )(*args)


def iota(shape, dim):
    return lax.broadcasted_iota(jnp.int32, shape, dim)


def nn(a, b):
    return lax.dot_general(a, b, (((1,), (0,)), ((), ())), preferred_element_type=F32)


def nt(a, b):
    return lax.dot_general(a, b, (((1,), (1,)), ((), ())), preferred_element_type=F32)


def tn(a, b):
    return lax.dot_general(a, b, (((0,), (0,)), ((), ())), preferred_element_type=F32)


def left_half(shape):
    return iota(shape, len(shape) - 1) < HEAD_DIM


def split_heads(x):
    mask = left_half(x.shape)
    zero = jnp.zeros_like(x)
    return jnp.concatenate([jnp.where(mask, x, zero), jnp.where(mask, zero, x)], axis=0)


def side(x):
    half = x.shape[0] // 2
    return jnp.concatenate([x[:half], x[half:]], axis=1)


def lanes_of(fac, kind, p):
    shape = (fac.shape[0], 128)
    n = kind * HEADS + 2 * p
    return jnp.where(left_half(shape), fac[:, n : n + 1], fac[:, n + 1 : n + 2])


def compact(m):
    return jnp.where(left_half((HEAD_DIM, 128)), m[:HEAD_DIM], m[HEAD_DIM:])


def unit_rows(r, p):
    u = r * PAIRS + p
    return slice(u * HEAD_DIM, (u + 1) * HEAD_DIM)


def spread(both_ref, place, toward_right, out_ref):
    for d in range(8):
        side_of = d > place if toward_right else d < place
        out_ref[d] = both_ref[jnp.where(side_of, 0, 1)]


def gather_states(place, rx_ref, from_left, state_ref):
    few = 3

    def run(direction, count, source_of):
        for first in range(0, UNITS, few):
            rows = slice(first * HEAD_DIM, (first + few) * HEAD_DIM)

            def step(n, state):
                source = source_of(n)
                th = rx_ref[source, STATE:LOAD, :].astype(F32)
                wide = [jnp.broadcast_to(th[u : u + 1], (HEAD_DIM, 128)) for u in range(first, first + few)]
                return jnp.concatenate(wide, axis=0) * state + rx_ref[source, rows, :].astype(F32)

            state = lax.fori_loop(0, count, step, jnp.zeros((few * HEAD_DIM, 128), F32))
            state_ref[direction, rows, :] = state.astype(BF)

    run(0 if from_left else 1, place, lambda n: n)
    run(1 if from_left else 0, 7 - place, lambda n: 7 - n)


def chain_states(place, refs, state_ref):
    state_ref[...] = jnp.zeros_like(state_ref)

    def step(direction, ref):
        for u in range(UNITS):
            rows = slice(u * HEAD_DIM, (u + 1) * HEAD_DIM)
            th = ref[STATE:LOAD, :].astype(F32)[u : u + 1]
            state_ref[direction, rows, :] = th * state_ref[direction, rows, :] + ref[rows, :].astype(F32)

    for back in range(7, 0, -1):
        pl.when(back <= place)(lambda back=back: step(0, refs[back - 1]))
    for back in range(1, 8):
        pl.when(back > place)(lambda back=back: step(1, refs[back - 1]))


def first_feature(n, j, core):
    return 48 * (2 * n + core) + 6 * j


def pick_rows(core):
    m, f = iota((SPLIT, D), 0), iota((SPLIT, D), 1)
    t = m & 7
    return ((f == first_feature(m >> 6, (m >> 3) & 7, core) + t) & (t < 6)).astype(BF)


def pick_thirds(core):
    m, f = iota((D // 2, D), 0), iota((D // 2, D), 1)
    b, d = m >> 7, (m >> 1) & 63
    return (f == first_feature(d >> 3, d & 7, core) + 3 * (m & 1) + b).astype(BF)


def place_thirds():
    m, n = iota((SPLIT, 128), 0), iota((SPLIT, 128), 1)
    return (((m >> 3) == (n >> 1)) & ((m & 7) == 6 + (n & 1))).astype(BF)


def per_head(shape):
    return (iota(shape, 0) == (iota(shape, 1) >> 6)).astype(BF)


def weights(col_r, row_r, col_l, row_l, lower, mask):
    return jnp.exp(jnp.where(lower, col_r - row_r, col_l - row_l)) * mask


def row_masks(bc_ref):
    i0, i1 = iota((COLS, COLS), 0), iota((COLS, COLS), 1)
    le, ge = (i0 <= i1).astype(BF), (i0 >= i1).astype(BF)
    b = bc_ref[...].astype(F32)
    b8 = jnp.broadcast_to(b[0:1], (8, COLS)).astype(BF)
    seg_row = nn(b8, le)[0:1]
    seg_col = nt(ge, b8)[:, 0:1]
    return i0, i1, le, ge, seg_row, seg_col, b[1:2, 0:1]


def layout_kernel(x_ref, g_ref, out_ref):
    for n, ref in enumerate((x_ref, g_ref)):
        wide = ref[...].astype(F32).reshape(2, 16, 8, D).swapaxes(0, 1).reshape(16, 16, D)
        out_ref[:, n * 16 : (n + 1) * 16, :] = wide.astype(BF)


def summary_kernel(place_ref, ldr_ref, bc_ref, x_ref, w_ref, fac_ref, th_ref, kv_ref, *refs):
    u_refs, both_ref = refs[:7], refs[7]
    i0, i1, le, ge, seg_row, seg_col, following = row_masks(bc_ref)
    first, last = seg_row[:, 0:1], seg_row[:, COLS - 1 : COLS]
    after = last + following
    th_ref[...] = jnp.zeros_like(th_ref)
    for r in range(ROWS):
        lr, ll = ldr_ref[r, 0], ldr_ref[r, 1]
        row_r, row_l = nn(lr, le), nn(ll, ge)
        col_r, col_l = nt(ge, lr), nt(le, ll)
        fac_ref[r] = jnp.concatenate(
            [
                jnp.where(seg_col == 0.0, jnp.exp(col_r), 0.0) * SCALE,
                jnp.where(seg_col == after, jnp.exp(col_l), 0.0) * SCALE,
                jnp.where(seg_col == last, jnp.exp(col_r[COLS - 1 : COLS] - col_r), 0.0),
                jnp.where(seg_col == first, jnp.exp(col_l[0:1] - col_l), 0.0),
            ],
            axis=1,
        )
        th_r = jnp.where(last == 0.0, jnp.exp(row_r[:, COLS - 1 : COLS]), 0.0)
        th_l = jnp.where(after == first, jnp.exp(row_l[:, 0:1]), 0.0)
        for direction, th in enumerate((th_r, th_l)):
            for p in range(PAIRS):
                n = r * PAIRS + p
                both = jnp.where(left_half((1, 128)), th[2 * p : 2 * p + 1], th[2 * p + 1 : 2 * p + 2])
                th_ref[direction, n : n + 1, :] = both
    kv_ref[...] = nn(x_ref[...], w_ref[:, D:]).astype(BF)
    for r in range(ROWS):
        rows = slice(r * COLS, (r + 1) * COLS)
        for p in range(PAIRS):
            k = kv_ref[rows, p * 128 : (p + 1) * 128]
            v = kv_ref[rows, D + p * 128 : D + (p + 1) * 128].astype(F32)
            for direction in range(2):
                tv = (lanes_of(fac_ref[r], 2 + direction, p) * v).astype(BF)
                both_ref[direction, unit_rows(r, p), :] = compact(tn(k, tv)).astype(BF)
    both_ref[:, STATE:LOAD, :] = th_ref[...].astype(BF)
    for n, u_ref in enumerate(u_refs):
        u_ref[...] = both_ref[jnp.where(place_ref[0] + n + 1 < 8, 0, 1)]


def mask_kernel(ldr_ref, ldc_ref, bc_ref, br_ref, dep_ref, wr_ref, wc_ref):
    i0, i1, le, ge, seg_row, seg_col, _ = row_masks(bc_ref)
    lower = i0 >= i1
    mask = jnp.where(seg_col == seg_row, jnp.where(i0 == i1, 2.0 * SCALE, SCALE), 0.0)
    for r in range(ROWS):
        lr, ll = ldr_ref[r, 0], ldr_ref[r, 1]
        row_r, row_l = nn(lr, le), nn(ll, ge)
        col_r, col_l = nt(ge, lr), nt(le, ll)
        for h in range(HEADS):
            w = weights(col_r[:, h : h + 1], row_r[h : h + 1], col_l[:, h : h + 1], row_l[h : h + 1], lower, mask)
            wr_ref[r * PAIRS + h // 2, (h % 2) * COLS : (h % 2 + 1) * COLS, :] = w.astype(BF)
    j0, j1 = iota((TOK, TOK), 0), iota((TOK, TOK), 1)
    same = (j0 & 7) == (j1 & 7)
    below = (j0 >> 3) >= (j1 >> 3)
    cle = (same & ((j0 >> 3) <= (j1 >> 3))).astype(BF)
    cge = (same & below).astype(BF)
    r8 = jnp.broadcast_to(br_ref[...].astype(F32), (8, TOK)).astype(BF)
    seg_row = nn(r8, cle)[0:1]
    seg_col = nt(cge, r8)[:, 0:1]
    mask = jnp.where(same & (seg_col == seg_row), jnp.where(j0 == j1, 2.0 * SCALE, SCALE), 0.0)
    lr, ll = ldc_ref[0], ldc_ref[1]
    row_r, row_l = nn(lr, cle), nn(ll, cge)
    col_r, col_l = nt(cge, lr), nt(cle, ll)
    for h in range(HEADS):
        w = weights(col_r[:, h : h + 1], row_r[h : h + 1], col_l[:, h : h + 1], row_l[h : h + 1], below, mask)
        wc_ref[h // 2, (h % 2) * TOK : (h % 2 + 1) * TOK, :] = w.astype(BF)


def side_kernel(
    core_ref, x_ref, g_ref, rx_ref, wo_ref, dn_ref, dnc_ref, keep_ref, send_ref, ckeep_ref, csend_ref
):
    core = core_ref[0]
    own, other = pick_rows(core), pick_rows(1 - core)
    xc = rx_ref[:, 0:16, :].reshape(TOK, D)
    csend_ref[...] = nt(other, xc).astype(BF)
    ckeep_ref[...] = nt(own, xc).astype(BF)
    send_ref[...] = nt(other, x_ref[...]).astype(BF)
    keep_ref[...] = nt(own, x_ref[...]).astype(BF)
    dn_ref[...] = nt(g_ref[...], wo_ref[...]).astype(BF)
    dnc_ref[...] = nt(rx_ref[:, 16:32, :].reshape(TOK, D), wo_ref[...]).astype(BF)


def row_inside_kernel(x_ref, w_ref, kv_ref, wr_ref, q_ref, out_ref, probs_ref):
    q_ref[...] = nn(x_ref[...], w_ref[:, :D]).astype(BF)
    for r in range(ROWS):
        rows = slice(r * COLS, (r + 1) * COLS)
        for p in range(PAIRS):
            lanes = slice(p * 128, (p + 1) * 128)
            k = kv_ref[rows, lanes]
            v = kv_ref[rows, D + p * 128 : D + (p + 1) * 128]
            n = r * PAIRS + p
            probs = (nt(split_heads(q_ref[rows, lanes]), k) * wr_ref[n].astype(F32)).astype(BF)
            probs_ref[n] = probs
            out_ref[rows, lanes] = nn(side(probs), split_heads(v))


def col_forward_kernel(rx_ref, w_ref, wc_ref, qkv_ref, out_ref, probs_ref):
    x = rx_ref[:, 0:16, :].reshape(TOK, D)
    qkv_ref[...] = nn(x, w_ref[...]).astype(BF)
    for p in range(PAIRS):
        q = qkv_ref[:, p * 128 : (p + 1) * 128]
        k = qkv_ref[:, D + p * 128 : D + (p + 1) * 128]
        v = qkv_ref[:, 2 * D + p * 128 : 2 * D + (p + 1) * 128]
        probs = (nt(split_heads(q), k) * wc_ref[p].astype(F32)).astype(BF)
        probs_ref[p] = probs
        out_ref[:, p * 128 : (p + 1) * 128] = nn(side(probs), split_heads(v)).astype(BF)


def state_of(s_ref, direction, r, p):
    return s_ref[direction, unit_rows(r, p), :]


def both_states(s_ref, r, p):
    return jnp.concatenate([split_heads(state_of(s_ref, d, r, p)) for d in range(2)], axis=1)


def row_join_kernel(place_ref, q_ref, fac_ref, inside_ref, col_ref, *refs):
    out_ref, xch_ref, s_ref, wide_ref = refs[7:]
    chain_states(place_ref[0], refs[:7], wide_ref)
    s_ref[...] = wide_ref[...].astype(BF)
    for r in range(ROWS):
        rows = slice(r * COLS, (r + 1) * COLS)
        for p in range(PAIRS):
            lanes = slice(p * 128, (p + 1) * 128)
            carried = nn(q_ref[rows, lanes], both_states(s_ref, r, p))
            out = inside_ref[rows, lanes]
            out = out + lanes_of(fac_ref[r], 0, p) * carried[:, :128]
            out = out + lanes_of(fac_ref[r], 1, p) * carried[:, 128:]
            out_ref[rows, lanes] = out.astype(BF)
    slab = out_ref[...].astype(F32).reshape(2, 16, 8, D).swapaxes(0, 1).reshape(16, 16, D)
    xch_ref[:, 16:32, :] = slab.astype(BF)
    xch_ref[:, 0:16, :] = col_ref[...].reshape(16, 16, D)


def norm_backward(mixed, dn, gain):
    inv = lax.rsqrt(jnp.mean(mixed * mixed, axis=-1, keepdims=True) + EPSILON)
    unit = mixed * inv
    scaled = dn * gain
    d_mixed = inv * (scaled - unit * jnp.mean(scaled * unit, axis=-1, keepdims=True))
    return unit, d_mixed


def from_slab(x):
    return x.astype(F32).reshape(16, 2, 8, D).swapaxes(0, 1).reshape(TOK, D)


def row_middle_kernel(
    place_ref, rx_ref, row_ref, dn_ref, gain_ref, q_ref, fac_ref, th_ref, dm_ref, g_ref, both_ref
):
    mixed = row_ref[...].astype(F32) + from_slab(rx_ref[:, 0:16, :])
    _, d_mixed = norm_backward(mixed, dn_ref[...].astype(F32), gain_ref[...])
    dm_ref[...] = d_mixed.astype(BF)
    for r in range(ROWS):
        rows = slice(r * COLS, (r + 1) * COLS)
        for p in range(PAIRS):
            q = q_ref[rows, p * 128 : (p + 1) * 128]
            do = d_mixed[rows, p * 128 : (p + 1) * 128]
            for direction in range(2):
                eo = (lanes_of(fac_ref[r], direction, p) * do).astype(BF)
                both_ref[direction, unit_rows(r, p), :] = compact(tn(q, eo)).astype(BF)
    both_ref[:, STATE:LOAD, :] = th_ref[...].astype(BF)
    spread(both_ref, place_ref[0], False, g_ref)


def local_backward(q, k, v, do, w, probs):
    q2, do2 = split_heads(q), split_heads(do)
    dp = nt(do2, v)
    dw = (dp * w.astype(F32)).astype(BF)
    both = (dp * probs.astype(F32)).astype(BF)
    dq = nn(side(dw), split_heads(k))
    dk = tn(dw, q2)
    dv = tn(probs, do2)
    return dq, dk, dv, both


def col_backward_kernel(
    rx_ref, col_ref, dn_ref, gain_ref, qkv_ref, wc_ref, probs_ref, w_ref, dqkv_ref, gd_ref, tok_ref
):
    mixed = rx_ref[:, 16:32, :].reshape(TOK, D).astype(F32) + col_ref[...].astype(F32)
    _, d_mixed = norm_backward(mixed, dn_ref[...].astype(F32), gain_ref[...])
    d_mixed = d_mixed.astype(BF)
    j0, j1 = iota((TOK, TOK), 0), iota((TOK, TOK), 1)
    same = (j0 & 7) == (j1 & 7)
    k0, k1 = j0 >> 3, j1 >> 3
    before, behind = (same & (k0 < k1)).astype(BF), (same & (k0 > k1)).astype(BF)
    table = jnp.concatenate([before, behind], axis=1)
    for p in range(PAIRS):
        lanes = slice(p * 128, (p + 1) * 128)
        q = qkv_ref[:, p * 128 : (p + 1) * 128]
        k = qkv_ref[:, D + p * 128 : D + (p + 1) * 128]
        v = qkv_ref[:, 2 * D + p * 128 : 2 * D + (p + 1) * 128]
        dq, dk, dv, both = local_backward(q, k, v, d_mixed[:, lanes], wc_ref[p], probs_ref[p])
        dqkv_ref[:, p * 128 : (p + 1) * 128] = dq.astype(BF)
        dqkv_ref[:, D + p * 128 : D + (p + 1) * 128] = dk.astype(BF)
        dqkv_ref[:, 2 * D + p * 128 : 2 * D + (p + 1) * 128] = dv.astype(BF)
        sums = nn(both, table)
        for half in range(2):
            part = sums[half * TOK : (half + 1) * TOK]
            h = 2 * p + half
            gd_ref[0, h : h + 1, :] = jnp.sum(jnp.where(k0 >= k1, part[:, :TOK], 0.0), axis=0, keepdims=True)
            gd_ref[1, h : h + 1, :] = jnp.sum(jnp.where(k0 <= k1, part[:, TOK:], 0.0), axis=0, keepdims=True)
    tok_ref[...] = nt(dqkv_ref[...], w_ref[...]).astype(BF)


def row_local_kernel(
    core_ref, rx_ref, row_ref, dn_ref, gain_ref, q_ref, kv_ref, dm_ref, s_ref, wr_ref, probs_ref, fac_ref,
    dq_ref, part_ref, gd_ref, keep_ref, send_ref,
):
    mixed = row_ref[...].astype(F32) + from_slab(rx_ref[:, 0:16, :])
    unit = mixed * lax.rsqrt(jnp.mean(mixed * mixed, axis=-1, keepdims=True) + EPSILON)
    normed = (unit * gain_ref[...]).astype(BF)
    gain_terms = (dn_ref[...].astype(F32) * unit).astype(BF)
    core = core_ref[0]
    for ref, c in ((keep_ref, core), (send_ref, 1 - core)):
        ref[0:SPLIT, :] = nt(pick_rows(c), gain_terms).astype(BF)
        ref[SPLIT : SPLIT + D // 2, :] = nt(pick_thirds(c), normed).astype(BF)
    i0, i1 = iota((COLS, COLS), 0), iota((COLS, COLS), 1)
    table = jnp.concatenate([(i0 < i1).astype(BF), (i0 > i1).astype(BF)], axis=1)
    entries = [[], []]
    for r in range(ROWS):
        rows = slice(r * COLS, (r + 1) * COLS)
        for p in range(PAIRS):
            lanes = slice(p * 128, (p + 1) * 128)
            q = q_ref[rows, lanes]
            k = kv_ref[rows, lanes]
            v = kv_ref[rows, D + p * 128 : D + (p + 1) * 128]
            do = dm_ref[rows, lanes]
            n = r * PAIRS + p
            dq, dk, dv, both = local_backward(q, k, v, do, wr_ref[n], probs_ref[n])
            states = both_states(s_ref, r, p)
            wide_do = do.astype(F32)
            eo = [lanes_of(fac_ref[r], d, p) * wide_do for d in range(2)]
            dq = dq + nt(jnp.concatenate(eo, axis=1).astype(BF), states)
            carried = nn(q, states)
            dq_ref[rows, lanes] = dq.astype(BF)
            part_ref[rows, lanes] = dk.astype(BF)
            part_ref[rows, D + p * 128 : D + (p + 1) * 128] = dv.astype(BF)
            sums = nn(both, table)
            for direction in range(2):
                entries[direction].append(
                    (carried[:, direction * 128 : (direction + 1) * 128] * eo[direction]).astype(BF)
                )
                keep = (i0 >= i1) if direction == 0 else (i0 <= i1)
                for half in range(2):
                    piece = sums[half * COLS : (half + 1) * COLS, direction * COLS : (direction + 1) * COLS]
                    n = r * HEADS + 2 * p + half
                    gd_ref[direction, n : n + 1, :] = jnp.sum(jnp.where(keep, piece, 0.0), axis=0, keepdims=True)
    heads = per_head((32, 2 * D))
    for direction in range(2):
        keep = ((i0 >= i1) if direction == 0 else (i0 <= i1)).astype(BF)
        total = nt(heads, jnp.concatenate(entries[direction], axis=1))
        gd_ref[direction] += nn(total.astype(BF), keep)[: 2 * HEADS]


def row_finish_kernel(
    place_ref, kv_ref, s_ref, ra_ref, fac_ref, th_ref, part_ref, gdp_ref, dkv_ref, gd_ref, a_ref
):
    gather_states(place_ref[0], ra_ref, False, a_ref)
    i0, i1 = iota((COLS, COLS), 0), iota((COLS, COLS), 1)
    tails, throughs = [[], []], [[], []]
    for r in range(ROWS):
        rows = slice(r * COLS, (r + 1) * COLS)
        for p in range(PAIRS):
            lanes = slice(p * 128, (p + 1) * 128)
            far = slice(D + p * 128, D + (p + 1) * 128)
            k = kv_ref[rows, lanes]
            v = kv_ref[rows, far].astype(F32)
            adjoints = both_states(a_ref, r, p)
            tail = [lanes_of(fac_ref[r], 2 + d, p) for d in range(2)]
            tv = [t * v for t in tail]
            dk = part_ref[rows, lanes].astype(F32) + nt(jnp.concatenate(tv, axis=1).astype(BF), adjoints)
            leaving = nn(k, adjoints)
            dv = part_ref[rows, far].astype(F32) + tail[0] * leaving[:, :128] + tail[1] * leaving[:, 128:]
            dkv_ref[rows, lanes] = dk.astype(BF)
            dkv_ref[rows, far] = dv.astype(BF)
            for d in range(2):
                tails[d].append((leaving[:, d * 128 : (d + 1) * 128] * tv[d]).astype(BF))
                n = r * PAIRS + p
                prod = state_of(s_ref, d, r, p).astype(F32) * state_of(a_ref, d, r, p).astype(F32)
                throughs[d].append(th_ref[d, n : n + 1, :] * jnp.sum(prod, axis=0, keepdims=True))
    heads = per_head((32, 2 * D))
    for d in range(2):
        before = ((i0 < i1) if d == 0 else (i0 > i1)).astype(BF)
        total = nt(heads, jnp.concatenate(tails[d], axis=1))
        through = jnp.broadcast_to(jnp.concatenate(throughs[d], axis=1), (8, 2 * D)).astype(BF)
        through = nt(heads, through)[: 2 * HEADS, 0:1]
        gd_ref[d] = gdp_ref[d] + nn(total.astype(BF), before)[: 2 * HEADS] + through


def weight_early_kernel(
    xk_ref, xr_ref, xck_ref, xcr_ref, dq_ref, dqr_ref, dc_ref, dcr_ref, nk_ref, nr_ref, g_ref, gr_ref, out_ref
):
    x = jnp.concatenate([xk_ref[...], xr_ref[...]], axis=1)
    xc = jnp.concatenate([xck_ref[...], xcr_ref[...]], axis=1)
    normed = jnp.concatenate([nk_ref[SPLIT:, :], nr_ref[SPLIT:, :]], axis=1)
    gain_terms = jnp.concatenate([nk_ref[0:SPLIT, :], nr_ref[0:SPLIT, :]], axis=1)
    expand = place_thirds()
    for start in range(0, D, 256):
        part = slice(start, start + 256)
        out_weight = nn(normed, jnp.concatenate([g_ref[:, part], gr_ref[:, part]], axis=0)).astype(BF)
        for b in range(3):
            cols = slice(b * D + start, b * D + start + 256)
            total = nn(expand, out_weight[b * 128 : (b + 1) * 128])
            total = total + nn(xc, jnp.concatenate([dc_ref[:, cols], dcr_ref[:, cols]], axis=0))
            if b == 0:
                total = total + nn(x, jnp.concatenate([dq_ref[:, cols], dqr_ref[:, cols]], axis=0))
            out_ref[:, cols] = total.astype(BF)
    out_ref[:, F:] = nn(gain_terms, jnp.ones((2 * TOK, 128), BF)).astype(BF)


def weight_late_kernel(xk_ref, xr_ref, dkv_ref, dkvr_ref, early_ref, out_ref):
    x = jnp.concatenate([xk_ref[...], xr_ref[...]], axis=1)
    out_ref[:, :, 0:D] = early_ref[:, 0:D].reshape(64, 8, D)
    out_ref[:, :, F:] = early_ref[:, F:].reshape(64, 8, 128)
    for start in range(0, 2 * D, 256):
        cols = slice(start, start + 256)
        far = slice(D + start, D + start + 256)
        total = nn(x, jnp.concatenate([dkv_ref[:, cols], dkvr_ref[:, cols]], axis=0))
        total = total + early_ref[:, far].astype(F32)
        out_ref[:, :, far] = total.reshape(64, 8, 256).astype(BF)


def weight_sum_kernel(rx_ref, qkv_ref, out_ref, gain_ref):
    total = jnp.sum(rx_ref[...].astype(F32), axis=0) * (32768.0 ** (-0.5))
    qkv_ref[...] = total[0:6, 0:F]
    for t in range(6):
        out_ref[t : t + 1, :] = total[6 + t // 3 : 7 + t // 3, (t % 3) * D : (t % 3 + 1) * D]
    same = iota((8, 128), 0) == iota((8, 128), 1)
    gain_ref[...] = jnp.sum(jnp.where(same, total[:, F:], 0.0), axis=0, keepdims=True)[:, 0:6]


def token_kernel(dq_ref, dkv_ref, w_ref, rx_ref, out_ref):
    total = nt(dq_ref[...], w_ref[:, :D]) + nt(dkv_ref[...], w_ref[:, D:])
    out_ref[...] = (total + from_slab(rx_ref[...])).astype(BF)


def exchange(x, axis, groups=None):
    return lax.all_to_all(x, axis, 0, 0, tiled=True, axis_index_groups=groups)


def swap(x):
    return lax.ppermute(x, "row", CORE_SWAP)


def after(value, *others):
    return lax.optimization_barrier((value, *others))[0]


def per_device(
    tokens, grad_out, w_qkv, w_out, gain, log_decay_rows, log_decay_cols, border_cols, border_rows
):
    place = lax.axis_index("col")
    at = place.astype(jnp.int32).reshape(1)
    core = (lax.axis_index("row") % 2).astype(jnp.int32).reshape(1)
    gain = gain.reshape(1, D)
    half = (SPLIT, TOK)
    load = ((8, LOAD, 128), BF)
    narrow = pltpu.VMEM((2, LOAD, 128), BF)

    x = tokens.reshape(TOK, D)
    g = grad_out.reshape(TOK, D)
    (first,) = call(layout_kernel, 2.0, [((16, 32, D), BF)], tokens, grad_out, keep=(0,))
    rx = exchange(first, "row")

    ldr = log_decay_rows.transpose(2, 0, 1, 3)
    ldc = log_decay_cols.swapaxes(2, 3).reshape(2, HEADS, TOK)
    tiles = jnp.concatenate([border_cols, jnp.zeros((COLS,), jnp.int32)]).reshape(9, COLS)
    bc = lax.dynamic_slice_in_dim(tiles, place, 2)
    br = jnp.broadcast_to(border_rows[:, None], (GRID_H, CD)).reshape(1, TOK)
    fac, th, kv, *updates = call(
        summary_kernel, 0.1,
        [((ROWS, COLS, 4 * HEADS), F32), ((2, 16, 128), F32), ((TOK, 2 * D), BF)] + [((LOAD, 128), BF)] * 7,
        at, ldr, bc, after(x, first), w_qkv, smem=(0,), near=(1, 2), scratch=[narrow], staged=True,
    )
    states = [
        lax.ppermute(u, "col", [(i, (i + n + 1) % 8) for i in range(8)]) for n, u in enumerate(updates)
    ]
    wr, wc = call(
        mask_kernel, 0.1,
        [((UNITS, 2 * COLS, COLS), BF), ((PAIRS, 2 * TOK, TOK), BF)],
        ldr, ldc, bc, br, th, near=(0, 1, 2, 3), staged=True,
    )
    q, inside, probs = call(
        row_inside_kernel, 0.1,
        [((TOK, D), BF), ((TOK, D), F32), ((UNITS, 2 * COLS, COLS), BF)],
        x, w_qkv, after(kv, states[0]), wr, staged=True,
    )
    qkv_c, col_out, probs_c = call(
        col_forward_kernel, 6.8,
        [((TOK, F), BF), ((TOK, D), BF), ((PAIRS, 2 * TOK, TOK), BF)],
        after(rx, states[0], states[1]), w_qkv, wc, near=(0,), staged=True,
    )
    row_out, out_swap, entering = call(
        row_join_kernel, 5.0,
        [((TOK, D), BF), ((16, 32, D), BF), ((2, STATE, 128), BF)],
        at, q, fac, inside, after(col_out, q), *states, smem=(0,), near=tuple(range(5, 12)), keep=(1,),
        scratch=[pltpu.VMEM((2, STATE, 128), F32)], staged=True,
    )
    dn, dn_c, x_keep, x_send, xc_keep, xc_send = call(
        side_kernel, 5.0,
        [((TOK, D), BF), ((TOK, D), BF), (half, BF), (half, BF), (half, BF), (half, BF)],
        core, after(x, entering), g, rx, w_out, smem=(0,),
    )
    x_far, g_far, xc_far = swap(x_send), swap(g), swap(xc_send)
    rx2 = exchange(out_swap, "row")
    rx2, x_far, g_far, xc_far = lax.optimization_barrier((rx2, x_far, g_far, xc_far))
    dm, adj = call(
        row_middle_kernel, 4.5,
        [((TOK, D), BF), load],
        at, rx2, row_out, dn, gain, q, fac, th, smem=(0,), near=(1, 4), keep=(1,), scratch=[narrow],
    )
    adj = exchange(adj, "col")
    dq, part, gd_part, n_keep, n_send = call(
        row_local_kernel, 8.9,
        [((TOK, D), BF), ((TOK, 2 * D), BF), ((2, 2 * HEADS, COLS), F32), ((SPLIT + D // 2, TOK), BF), ((SPLIT + D // 2, TOK), BF)],
        core, rx2, row_out, dn, gain, q, kv, dm, entering, wr, probs, fac, smem=(0,), near=(1, 4),
    )
    n_far, dq_far = swap(n_send), swap(dq)
    dqkv_c, gdc, tok_c = call(
        col_backward_kernel, 9.7,
        [((TOK, F), BF), ((2, HEADS, TOK), F32), ((TOK, D), BF)],
        after(rx2, dm), col_out, dn_c, gain, qkv_c, wc, probs_c, w_qkv, near=(0, 3),
    )
    dqkv_c_far = swap(dqkv_c)
    adj, n_far, dq_far, tok_c = lax.optimization_barrier((adj, n_far, dq_far, tok_c))
    rx3 = exchange(tok_c.reshape(16, 16, D), "row")
    dkv, gdr = call(
        row_finish_kernel, 0.3,
        [((TOK, 2 * D), BF), ((2, 2 * HEADS, COLS), F32)],
        at, kv, entering, adj, fac, th, part, gd_part,
        smem=(0,), near=(3,), scratch=[pltpu.VMEM((2, STATE, 128), BF)], staged=True,
    )
    dkv_far = swap(dkv)
    (early,) = call(
        weight_early_kernel, 0.3,
        [((SPLIT, WIDE), BF)],
        x_keep, x_far, xc_keep, xc_far, after(dq, dkv), dq_far, dqkv_c, dqkv_c_far, n_keep, n_far, g, g_far,
        keep=(0,),
    )
    (wg,) = call(
        weight_late_kernel, 0.3,
        [((64, 8, WIDE), BF)],
        x_keep, x_far, dkv, dkv_far, early, near=(3, 4), keep=(0,), staged=True,
    )
    wg = exchange(after(wg, rx3), ("row", "col"), SAME_CORE)
    grad_qkv, grad_out_weight, grad_gain = call(
        weight_sum_kernel, 2.0, [((6, F), F32), ((6, D), F32), ((1, 6), F32)], wg, near=(0,)
    )
    (grad_tokens,) = call(token_kernel, 4.0, [((TOK, D), BF)], dq, dkv, w_qkv, rx3, near=(3,))
    gdr = gdr.reshape(2, ROWS, HEADS, COLS).swapaxes(1, 2)
    return (
        grad_tokens.reshape(ROWS, COLS, D),
        grad_qkv,
        grad_out_weight,
        grad_gain.reshape(6),
        gdr.astype(BF),
        gdc.astype(BF).reshape(2, HEADS, GRID_H, CD).swapaxes(2, 3),
    )


def solution(mesh):
    in_specs = (
        P("row", "col", None),
        P("row", "col", None),
        P(),
        P(),
        P(),
        P(None, None, "row", "col"),
        P(None, None, ("col", "row"), None),
        P(),
        P(),
    )
    out_specs = (
        P("row", "col", None),
        P(("row", "col"), None),
        P(("row", "col"), None),
        P(("row", "col")),
        P(None, None, "row", "col"),
        P(None, None, ("col", "row"), None),
    )
    return jax.shard_map(
        per_device, mesh=mesh, in_specs=in_specs, out_specs=out_specs, check_vma=False
    )
```

```python
import jax
import jax.numpy as jnp
from jax import lax
from jax.experimental import pallas as pl
from jax.experimental.pallas import tpu as pltpu
from jax.sharding import PartitionSpec as P

EPSILON = 1e-05
HEADS = 12
HEAD_DIM = 64
PAIRS = HEADS // 2
D = 768
F = 3 * D
ROWS = 2
COLS = 128
TOK = ROWS * COLS
GRID_H = 32
CD = 8
SCALE = HEAD_DIM ** (-0.5)
WIDE = F + 128
SPLIT = 512
VMEM_MIB = 20
F32 = jnp.float32
BF = jnp.bfloat16
SAME_CORE = [[r * 8 + c for r in range(core, 16, 2) for c in range(8)] for core in range(2)]
CORE_SWAP = [(i, i ^ 1) for i in range(16)]


UNITS = ROWS * PAIRS
STATE = UNITS * HEAD_DIM
LOAD = STATE + 16


class Arriving:
    def __init__(self, source, buffer, semaphore):
        self.copy = pltpu.make_async_copy(source, buffer, semaphore)
        self.copy.start()
        self.buffer = buffer
        self.here = False

    def arrive(self):
        if not self.here:
            self.copy.wait()
            self.here = True

    def __getitem__(self, index):
        self.arrive()
        return self.buffer[index]


def call(body, us, outs, *args, smem=(), near=(), keep=(), scratch=(), staged=False):
    far = [n for n in range(len(args)) if n not in smem and n not in near]
    specs = [pl.BlockSpec(memory_space=pltpu.VMEM)] * len(args)
    args = list(args)
    for n in smem:
        specs[n] = pl.BlockSpec(memory_space=pltpu.SMEM)
    for n in far:
        args[n] = pltpu.with_memory_space_constraint(args[n], pltpu.HBM)
    scratch = list(scratch)
    kernel = body
    if staged:
        for n in far:
            specs[n] = pl.BlockSpec(memory_space=pl.ANY)
        scratch += [pltpu.VMEM(args[n].shape, args[n].dtype) for n in far]
        scratch += [pltpu.SemaphoreType.DMA((len(far),))]

        def kernel(*refs):
            refs, semaphores = list(refs[:-1]), refs[-1]
            last = len(refs) - len(far)
            arriving = [Arriving(refs[n], refs[last + k], semaphores.at[k]) for k, n in enumerate(far)]
            for k, n in enumerate(far):
                refs[n] = arriving[k]
            body(*refs[:last])
            for operand in arriving:
                operand.arrive()

    return pl.pallas_call(
        kernel,
        out_shape=[(pltpu.VMEM if n in keep else pltpu.HBM)(s, t) for n, (s, t) in enumerate(outs)],
        in_specs=specs,
        out_specs=[pl.BlockSpec(memory_space=pltpu.VMEM)] * len(outs),
        scratch_shapes=scratch,
        cost_estimate=pl.CostEstimate(
            flops=int(us * 1.1e9), bytes_accessed=int(us * 3.6e6), transcendentals=0
        ),
        compiler_params=pltpu.CompilerParams(vmem_limit_bytes=VMEM_MIB * 1024 * 1024),
    )(*args)


def iota(shape, dim):
    return lax.broadcasted_iota(jnp.int32, shape, dim)


def nn(a, b):
    return lax.dot_general(a, b, (((1,), (0,)), ((), ())), preferred_element_type=F32)


def nt(a, b):
    return lax.dot_general(a, b, (((1,), (1,)), ((), ())), preferred_element_type=F32)


def tn(a, b):
    return lax.dot_general(a, b, (((0,), (0,)), ((), ())), preferred_element_type=F32)


def left_half(shape):
    return iota(shape, len(shape) - 1) < HEAD_DIM


def split_heads(x):
    mask = left_half(x.shape)
    zero = jnp.zeros_like(x)
    return jnp.concatenate([jnp.where(mask, x, zero), jnp.where(mask, zero, x)], axis=0)


def side(x):
    half = x.shape[0] // 2
    return jnp.concatenate([x[:half], x[half:]], axis=1)


def lanes_of(fac, kind, p):
    shape = (fac.shape[0], 128)
    n = kind * HEADS + 2 * p
    return jnp.where(left_half(shape), fac[:, n : n + 1], fac[:, n + 1 : n + 2])


def compact(m):
    return jnp.where(left_half((HEAD_DIM, 128)), m[:HEAD_DIM], m[HEAD_DIM:])


def unit_rows(r, p):
    u = r * PAIRS + p
    return slice(u * HEAD_DIM, (u + 1) * HEAD_DIM)


def spread(both_ref, place, toward_right, out_ref):
    for d in range(8):
        side_of = d > place if toward_right else d < place
        out_ref[d] = both_ref[jnp.where(side_of, 0, 1)]


def gather_states(place, rx_ref, from_left, state_ref):
    few = 3

    def run(direction, count, source_of):
        for first in range(0, UNITS, few):
            rows = slice(first * HEAD_DIM, (first + few) * HEAD_DIM)

            def step(n, state):
                source = source_of(n)
                th = rx_ref[source, STATE:LOAD, :].astype(F32)
                wide = [jnp.broadcast_to(th[u : u + 1], (HEAD_DIM, 128)) for u in range(first, first + few)]
                return jnp.concatenate(wide, axis=0) * state + rx_ref[source, rows, :].astype(F32)

            state = lax.fori_loop(0, count, step, jnp.zeros((few * HEAD_DIM, 128), F32))
            state_ref[direction, rows, :] = state.astype(BF)

    run(0 if from_left else 1, place, lambda n: n)
    run(1 if from_left else 0, 7 - place, lambda n: 7 - n)


def chain_states(place, refs, state_ref):
    state_ref[...] = jnp.zeros_like(state_ref)

    def step(direction, ref):
        for u in range(UNITS):
            rows = slice(u * HEAD_DIM, (u + 1) * HEAD_DIM)
            th = ref[STATE:LOAD, :].astype(F32)[u : u + 1]
            state_ref[direction, rows, :] = th * state_ref[direction, rows, :] + ref[rows, :].astype(F32)

    for back in range(7, 0, -1):
        pl.when(back <= place)(lambda back=back: step(0, refs[back - 1]))
    for back in range(1, 8):
        pl.when(back > place)(lambda back=back: step(1, refs[back - 1]))


def first_feature(n, j, core):
    return 48 * (2 * n + core) + 6 * j


def pick_rows(core):
    m, f = iota((SPLIT, D), 0), iota((SPLIT, D), 1)
    t = m & 7
    return ((f == first_feature(m >> 6, (m >> 3) & 7, core) + t) & (t < 6)).astype(BF)


def pick_thirds(core):
    m, f = iota((D // 2, D), 0), iota((D // 2, D), 1)
    b, d = m >> 7, (m >> 1) & 63
    return (f == first_feature(d >> 3, d & 7, core) + 3 * (m & 1) + b).astype(BF)


def place_thirds():
    m, n = iota((SPLIT, 128), 0), iota((SPLIT, 128), 1)
    return (((m >> 3) == (n >> 1)) & ((m & 7) == 6 + (n & 1))).astype(BF)


def per_head(shape):
    return (iota(shape, 0) == (iota(shape, 1) >> 6)).astype(BF)


def weights(col_r, row_r, col_l, row_l, lower, mask):
    return jnp.exp(jnp.where(lower, col_r - row_r, col_l - row_l)) * mask


def row_masks(bc_ref):
    i0, i1 = iota((COLS, COLS), 0), iota((COLS, COLS), 1)
    le, ge = (i0 <= i1).astype(BF), (i0 >= i1).astype(BF)
    b = bc_ref[...].astype(F32)
    b8 = jnp.broadcast_to(b[0:1], (8, COLS)).astype(BF)
    seg_row = nn(b8, le)[0:1]
    seg_col = nt(ge, b8)[:, 0:1]
    return i0, i1, le, ge, seg_row, seg_col, b[1:2, 0:1]


def layout_kernel(x_ref, g_ref, out_ref):
    for n, ref in enumerate((x_ref, g_ref)):
        wide = ref[...].astype(F32).reshape(2, 16, 8, D).swapaxes(0, 1).reshape(16, 16, D)
        out_ref[:, n * 16 : (n + 1) * 16, :] = wide.astype(BF)


def summary_kernel(place_ref, ldr_ref, bc_ref, x_ref, w_ref, fac_ref, th_ref, kv_ref, *refs):
    u_refs, both_ref = refs[:7], refs[7]
    i0, i1, le, ge, seg_row, seg_col, following = row_masks(bc_ref)
    first, last = seg_row[:, 0:1], seg_row[:, COLS - 1 : COLS]
    after = last + following
    th_ref[...] = jnp.zeros_like(th_ref)
    for r in range(ROWS):
        lr, ll = ldr_ref[r, 0], ldr_ref[r, 1]
        row_r, row_l = nn(lr, le), nn(ll, ge)
        col_r, col_l = nt(ge, lr), nt(le, ll)
        fac_ref[r] = jnp.concatenate(
            [
                jnp.where(seg_col == 0.0, jnp.exp(col_r), 0.0) * SCALE,
                jnp.where(seg_col == after, jnp.exp(col_l), 0.0) * SCALE,
                jnp.where(seg_col == last, jnp.exp(col_r[COLS - 1 : COLS] - col_r), 0.0),
                jnp.where(seg_col == first, jnp.exp(col_l[0:1] - col_l), 0.0),
            ],
            axis=1,
        )
        th_r = jnp.where(last == 0.0, jnp.exp(row_r[:, COLS - 1 : COLS]), 0.0)
        th_l = jnp.where(after == first, jnp.exp(row_l[:, 0:1]), 0.0)
        for direction, th in enumerate((th_r, th_l)):
            for p in range(PAIRS):
                n = r * PAIRS + p
                both = jnp.where(left_half((1, 128)), th[2 * p : 2 * p + 1], th[2 * p + 1 : 2 * p + 2])
                th_ref[direction, n : n + 1, :] = both
    kv_ref[...] = nn(x_ref[...], w_ref[:, D:]).astype(BF)
    for r in range(ROWS):
        rows = slice(r * COLS, (r + 1) * COLS)
        for p in range(PAIRS):
            k = kv_ref[rows, p * 128 : (p + 1) * 128]
            v = kv_ref[rows, D + p * 128 : D + (p + 1) * 128].astype(F32)
            for direction in range(2):
                tv = (lanes_of(fac_ref[r], 2 + direction, p) * v).astype(BF)
                both_ref[direction, unit_rows(r, p), :] = compact(tn(k, tv)).astype(BF)
    both_ref[:, STATE:LOAD, :] = th_ref[...].astype(BF)
    for n, u_ref in enumerate(u_refs):
        u_ref[...] = both_ref[jnp.where(place_ref[0] + n + 1 < 8, 0, 1)]


def mask_kernel(ldr_ref, ldc_ref, bc_ref, br_ref, dep_ref, wr_ref, wc_ref):
    i0, i1, le, ge, seg_row, seg_col, _ = row_masks(bc_ref)
    lower = i0 >= i1
    mask = jnp.where(seg_col == seg_row, jnp.where(i0 == i1, 2.0 * SCALE, SCALE), 0.0)
    for r in range(ROWS):
        lr, ll = ldr_ref[r, 0], ldr_ref[r, 1]
        row_r, row_l = nn(lr, le), nn(ll, ge)
        col_r, col_l = nt(ge, lr), nt(le, ll)
        for h in range(HEADS):
            w = weights(col_r[:, h : h + 1], row_r[h : h + 1], col_l[:, h : h + 1], row_l[h : h + 1], lower, mask)
            wr_ref[r * PAIRS + h // 2, (h % 2) * COLS : (h % 2 + 1) * COLS, :] = w.astype(BF)
    j0, j1 = iota((TOK, TOK), 0), iota((TOK, TOK), 1)
    same = (j0 & 7) == (j1 & 7)
    below = (j0 >> 3) >= (j1 >> 3)
    cle = (same & ((j0 >> 3) <= (j1 >> 3))).astype(BF)
    cge = (same & below).astype(BF)
    r8 = jnp.broadcast_to(br_ref[...].astype(F32), (8, TOK)).astype(BF)
    seg_row = nn(r8, cle)[0:1]
    seg_col = nt(cge, r8)[:, 0:1]
    mask = jnp.where(same & (seg_col == seg_row), jnp.where(j0 == j1, 2.0 * SCALE, SCALE), 0.0)
    lr, ll = ldc_ref[0], ldc_ref[1]
    row_r, row_l = nn(lr, cle), nn(ll, cge)
    col_r, col_l = nt(cge, lr), nt(cle, ll)
    for h in range(HEADS):
        w = weights(col_r[:, h : h + 1], row_r[h : h + 1], col_l[:, h : h + 1], row_l[h : h + 1], below, mask)
        wc_ref[h // 2, (h % 2) * TOK : (h % 2 + 1) * TOK, :] = w.astype(BF)


def side_kernel(
    core_ref, x_ref, g_ref, rx_ref, wo_ref, dn_ref, dnc_ref, keep_ref, send_ref, ckeep_ref, csend_ref
):
    core = core_ref[0]
    own, other = pick_rows(core), pick_rows(1 - core)
    xc = rx_ref[:, 0:16, :].reshape(TOK, D)
    csend_ref[...] = nt(other, xc).astype(BF)
    ckeep_ref[...] = nt(own, xc).astype(BF)
    send_ref[...] = nt(other, x_ref[...]).astype(BF)
    keep_ref[...] = nt(own, x_ref[...]).astype(BF)
    dn_ref[...] = nt(g_ref[...], wo_ref[...]).astype(BF)
    dnc_ref[...] = nt(rx_ref[:, 16:32, :].reshape(TOK, D), wo_ref[...]).astype(BF)


def row_inside_kernel(x_ref, w_ref, kv_ref, wr_ref, q_ref, out_ref, probs_ref):
    q_ref[...] = nn(x_ref[...], w_ref[:, :D]).astype(BF)
    for r in range(ROWS):
        rows = slice(r * COLS, (r + 1) * COLS)
        for p in range(PAIRS):
            lanes = slice(p * 128, (p + 1) * 128)
            k = kv_ref[rows, lanes]
            v = kv_ref[rows, D + p * 128 : D + (p + 1) * 128]
            n = r * PAIRS + p
            probs = (nt(split_heads(q_ref[rows, lanes]), k) * wr_ref[n].astype(F32)).astype(BF)
            probs_ref[n] = probs
            out_ref[rows, lanes] = nn(side(probs), split_heads(v))


def col_forward_kernel(rx_ref, w_ref, wc_ref, qkv_ref, out_ref, probs_ref):
    x = rx_ref[:, 0:16, :].reshape(TOK, D)
    qkv_ref[...] = nn(x, w_ref[...]).astype(BF)
    for p in range(PAIRS):
        q = qkv_ref[:, p * 128 : (p + 1) * 128]
        k = qkv_ref[:, D + p * 128 : D + (p + 1) * 128]
        v = qkv_ref[:, 2 * D + p * 128 : 2 * D + (p + 1) * 128]
        probs = (nt(split_heads(q), k) * wc_ref[p].astype(F32)).astype(BF)
        probs_ref[p] = probs
        out_ref[:, p * 128 : (p + 1) * 128] = nn(side(probs), split_heads(v)).astype(BF)


def state_of(s_ref, direction, r, p):
    return s_ref[direction, unit_rows(r, p), :]


def both_states(s_ref, r, p):
    return jnp.concatenate([split_heads(state_of(s_ref, d, r, p)) for d in range(2)], axis=1)


def row_join_kernel(place_ref, q_ref, fac_ref, inside_ref, col_ref, *refs):
    out_ref, xch_ref, s_ref, wide_ref = refs[7:]
    chain_states(place_ref[0], refs[:7], wide_ref)
    s_ref[...] = wide_ref[...].astype(BF)
    for r in range(ROWS):
        rows = slice(r * COLS, (r + 1) * COLS)
        for p in range(PAIRS):
            lanes = slice(p * 128, (p + 1) * 128)
            carried = nn(q_ref[rows, lanes], both_states(s_ref, r, p))
            out = inside_ref[rows, lanes]
            out = out + lanes_of(fac_ref[r], 0, p) * carried[:, :128]
            out = out + lanes_of(fac_ref[r], 1, p) * carried[:, 128:]
            out_ref[rows, lanes] = out.astype(BF)
    slab = out_ref[...].astype(F32).reshape(2, 16, 8, D).swapaxes(0, 1).reshape(16, 16, D)
    xch_ref[:, 16:32, :] = slab.astype(BF)
    xch_ref[:, 0:16, :] = col_ref[...].reshape(16, 16, D)


def norm_backward(mixed, dn, gain):
    inv = lax.rsqrt(jnp.mean(mixed * mixed, axis=-1, keepdims=True) + EPSILON)
    unit = mixed * inv
    scaled = dn * gain
    d_mixed = inv * (scaled - unit * jnp.mean(scaled * unit, axis=-1, keepdims=True))
    return unit, d_mixed


def from_slab(x):
    return x.astype(F32).reshape(16, 2, 8, D).swapaxes(0, 1).reshape(TOK, D)


def row_middle_kernel(
    place_ref, rx_ref, row_ref, dn_ref, gain_ref, q_ref, fac_ref, th_ref, dm_ref, g_ref, both_ref
):
    mixed = row_ref[...].astype(F32) + from_slab(rx_ref[:, 0:16, :])
    _, d_mixed = norm_backward(mixed, dn_ref[...].astype(F32), gain_ref[...])
    dm_ref[...] = d_mixed.astype(BF)
    for r in range(ROWS):
        rows = slice(r * COLS, (r + 1) * COLS)
        for p in range(PAIRS):
            q = q_ref[rows, p * 128 : (p + 1) * 128]
            do = d_mixed[rows, p * 128 : (p + 1) * 128]
            for direction in range(2):
                eo = (lanes_of(fac_ref[r], direction, p) * do).astype(BF)
                both_ref[direction, unit_rows(r, p), :] = compact(tn(q, eo)).astype(BF)
    both_ref[:, STATE:LOAD, :] = th_ref[...].astype(BF)
    spread(both_ref, place_ref[0], False, g_ref)


def local_backward(q, k, v, do, w, probs):
    q2, do2 = split_heads(q), split_heads(do)
    dp = nt(do2, v)
    dw = (dp * w.astype(F32)).astype(BF)
    both = (dp * probs.astype(F32)).astype(BF)
    dq = nn(side(dw), split_heads(k))
    dk = tn(dw, q2)
    dv = tn(probs, do2)
    return dq, dk, dv, both


def col_backward_kernel(
    rx_ref, col_ref, dn_ref, gain_ref, qkv_ref, wc_ref, probs_ref, w_ref, dqkv_ref, gd_ref, tok_ref
):
    mixed = rx_ref[:, 16:32, :].reshape(TOK, D).astype(F32) + col_ref[...].astype(F32)
    _, d_mixed = norm_backward(mixed, dn_ref[...].astype(F32), gain_ref[...])
    d_mixed = d_mixed.astype(BF)
    j0, j1 = iota((TOK, TOK), 0), iota((TOK, TOK), 1)
    same = (j0 & 7) == (j1 & 7)
    k0, k1 = j0 >> 3, j1 >> 3
    before, behind = (same & (k0 < k1)).astype(BF), (same & (k0 > k1)).astype(BF)
    table = jnp.concatenate([before, behind], axis=1)
    for p in range(PAIRS):
        lanes = slice(p * 128, (p + 1) * 128)
        q = qkv_ref[:, p * 128 : (p + 1) * 128]
        k = qkv_ref[:, D + p * 128 : D + (p + 1) * 128]
        v = qkv_ref[:, 2 * D + p * 128 : 2 * D + (p + 1) * 128]
        dq, dk, dv, both = local_backward(q, k, v, d_mixed[:, lanes], wc_ref[p], probs_ref[p])
        dqkv_ref[:, p * 128 : (p + 1) * 128] = dq.astype(BF)
        dqkv_ref[:, D + p * 128 : D + (p + 1) * 128] = dk.astype(BF)
        dqkv_ref[:, 2 * D + p * 128 : 2 * D + (p + 1) * 128] = dv.astype(BF)
        sums = nn(both, table)
        for half in range(2):
            part = sums[half * TOK : (half + 1) * TOK]
            h = 2 * p + half
            gd_ref[0, h : h + 1, :] = jnp.sum(jnp.where(k0 >= k1, part[:, :TOK], 0.0), axis=0, keepdims=True)
            gd_ref[1, h : h + 1, :] = jnp.sum(jnp.where(k0 <= k1, part[:, TOK:], 0.0), axis=0, keepdims=True)
    tok_ref[...] = nt(dqkv_ref[...], w_ref[...]).astype(BF)


def row_local_kernel(
    core_ref, rx_ref, row_ref, dn_ref, gain_ref, q_ref, kv_ref, dm_ref, s_ref, wr_ref, probs_ref, fac_ref,
    dq_ref, part_ref, gd_ref, keep_ref, send_ref,
):
    mixed = row_ref[...].astype(F32) + from_slab(rx_ref[:, 0:16, :])
    unit = mixed * lax.rsqrt(jnp.mean(mixed * mixed, axis=-1, keepdims=True) + EPSILON)
    normed = (unit * gain_ref[...]).astype(BF)
    gain_terms = (dn_ref[...].astype(F32) * unit).astype(BF)
    core = core_ref[0]
    for ref, c in ((keep_ref, core), (send_ref, 1 - core)):
        ref[0:SPLIT, :] = nt(pick_rows(c), gain_terms).astype(BF)
        ref[SPLIT : SPLIT + D // 2, :] = nt(pick_thirds(c), normed).astype(BF)
    i0, i1 = iota((COLS, COLS), 0), iota((COLS, COLS), 1)
    table = jnp.concatenate([(i0 < i1).astype(BF), (i0 > i1).astype(BF)], axis=1)
    entries = [[], []]
    for r in range(ROWS):
        rows = slice(r * COLS, (r + 1) * COLS)
        for p in range(PAIRS):
            lanes = slice(p * 128, (p + 1) * 128)
            q = q_ref[rows, lanes]
            k = kv_ref[rows, lanes]
            v = kv_ref[rows, D + p * 128 : D + (p + 1) * 128]
            do = dm_ref[rows, lanes]
            n = r * PAIRS + p
            dq, dk, dv, both = local_backward(q, k, v, do, wr_ref[n], probs_ref[n])
            states = both_states(s_ref, r, p)
            wide_do = do.astype(F32)
            eo = [lanes_of(fac_ref[r], d, p) * wide_do for d in range(2)]
            dq = dq + nt(jnp.concatenate(eo, axis=1).astype(BF), states)
            carried = nn(q, states)
            dq_ref[rows, lanes] = dq.astype(BF)
            part_ref[rows, lanes] = dk.astype(BF)
            part_ref[rows, D + p * 128 : D + (p + 1) * 128] = dv.astype(BF)
            sums = nn(both, table)
            for direction in range(2):
                entries[direction].append(
                    (carried[:, direction * 128 : (direction + 1) * 128] * eo[direction]).astype(BF)
                )
                keep = (i0 >= i1) if direction == 0 else (i0 <= i1)
                for half in range(2):
                    piece = sums[half * COLS : (half + 1) * COLS, direction * COLS : (direction + 1) * COLS]
                    n = r * HEADS + 2 * p + half
                    gd_ref[direction, n : n + 1, :] = jnp.sum(jnp.where(keep, piece, 0.0), axis=0, keepdims=True)
    heads = per_head((32, 2 * D))
    for direction in range(2):
        keep = ((i0 >= i1) if direction == 0 else (i0 <= i1)).astype(BF)
        total = nt(heads, jnp.concatenate(entries[direction], axis=1))
        gd_ref[direction] += nn(total.astype(BF), keep)[: 2 * HEADS]


def row_finish_kernel(
    place_ref, kv_ref, s_ref, ra_ref, fac_ref, th_ref, part_ref, gdp_ref, dkv_ref, gd_ref, a_ref
):
    gather_states(place_ref[0], ra_ref, False, a_ref)
    i0, i1 = iota((COLS, COLS), 0), iota((COLS, COLS), 1)
    tails, throughs = [[], []], [[], []]
    for r in range(ROWS):
        rows = slice(r * COLS, (r + 1) * COLS)
        for p in range(PAIRS):
            lanes = slice(p * 128, (p + 1) * 128)
            far = slice(D + p * 128, D + (p + 1) * 128)
            k = kv_ref[rows, lanes]
            v = kv_ref[rows, far].astype(F32)
            adjoints = both_states(a_ref, r, p)
            tail = [lanes_of(fac_ref[r], 2 + d, p) for d in range(2)]
            tv = [t * v for t in tail]
            dk = part_ref[rows, lanes].astype(F32) + nt(jnp.concatenate(tv, axis=1).astype(BF), adjoints)
            leaving = nn(k, adjoints)
            dv = part_ref[rows, far].astype(F32) + tail[0] * leaving[:, :128] + tail[1] * leaving[:, 128:]
            dkv_ref[rows, lanes] = dk.astype(BF)
            dkv_ref[rows, far] = dv.astype(BF)
            for d in range(2):
                tails[d].append((leaving[:, d * 128 : (d + 1) * 128] * tv[d]).astype(BF))
                n = r * PAIRS + p
                prod = state_of(s_ref, d, r, p).astype(F32) * state_of(a_ref, d, r, p).astype(F32)
                throughs[d].append(th_ref[d, n : n + 1, :] * jnp.sum(prod, axis=0, keepdims=True))
    heads = per_head((32, 2 * D))
    for d in range(2):
        before = ((i0 < i1) if d == 0 else (i0 > i1)).astype(BF)
        total = nt(heads, jnp.concatenate(tails[d], axis=1))
        through = jnp.broadcast_to(jnp.concatenate(throughs[d], axis=1), (8, 2 * D)).astype(BF)
        through = nt(heads, through)[: 2 * HEADS, 0:1]
        gd_ref[d] = gdp_ref[d] + nn(total.astype(BF), before)[: 2 * HEADS] + through


def weight_out_kernel(nk_ref, nr_ref, g_ref, gr_ref, out_ref, gain_ref):
    normed = jnp.concatenate([nk_ref[SPLIT:, :], nr_ref[SPLIT:, :]], axis=1)
    gain_terms = jnp.concatenate([nk_ref[0:SPLIT, :], nr_ref[0:SPLIT, :]], axis=1)
    for start in range(0, D, 256):
        part = slice(start, start + 256)
        out_ref[:, part] = nn(normed, jnp.concatenate([g_ref[:, part], gr_ref[:, part]], axis=0)).astype(BF)
    gain_ref[...] = nn(gain_terms, jnp.ones((2 * TOK, 128), BF)).astype(BF)


def weight_early_kernel(
    xk_ref, xr_ref, xck_ref, xcr_ref, dq_ref, dqr_ref, dc_ref, dcr_ref, ow_ref, gain_ref, out_ref
):
    x = jnp.concatenate([xk_ref[...], xr_ref[...]], axis=1)
    xc = jnp.concatenate([xck_ref[...], xcr_ref[...]], axis=1)
    expand = place_thirds()
    for start in range(0, F, 256):
        b, part = start // D, slice(start % D, start % D + 256)
        cols = slice(start, start + 256)
        total = nn(expand, ow_ref[b * 128 : (b + 1) * 128, part])
        total = total + nn(xc, jnp.concatenate([dc_ref[:, cols], dcr_ref[:, cols]], axis=0))
        if b == 0:
            total = total + nn(x, jnp.concatenate([dq_ref[:, cols], dqr_ref[:, cols]], axis=0))
        out_ref[:, cols] = total.astype(BF)
    out_ref[:, F:] = gain_ref[...]


def weight_late_kernel(xk_ref, xr_ref, dkv_ref, dkvr_ref, early_ref, out_ref):
    x = jnp.concatenate([xk_ref[...], xr_ref[...]], axis=1)
    out_ref[:, :, 0:D] = early_ref[:, 0:D].reshape(64, 8, D)
    out_ref[:, :, F:] = early_ref[:, F:].reshape(64, 8, 128)
    for start in range(0, 2 * D, 256):
        cols = slice(start, start + 256)
        far = slice(D + start, D + start + 256)
        total = nn(x, jnp.concatenate([dkv_ref[:, cols], dkvr_ref[:, cols]], axis=0))
        total = total + early_ref[:, far].astype(F32)
        out_ref[:, :, far] = total.reshape(64, 8, 256).astype(BF)


def weight_sum_kernel(rx_ref, qkv_ref, out_ref, gain_ref):
    total = jnp.sum(rx_ref[...].astype(F32), axis=0) * (32768.0 ** (-0.5))
    qkv_ref[...] = total[0:6, 0:F]
    for t in range(6):
        out_ref[t : t + 1, :] = total[6 + t // 3 : 7 + t // 3, (t % 3) * D : (t % 3 + 1) * D]
    same = iota((8, 128), 0) == iota((8, 128), 1)
    gain_ref[...] = jnp.sum(jnp.where(same, total[:, F:], 0.0), axis=0, keepdims=True)[:, 0:6]


def token_kernel(dq_ref, dkv_ref, w_ref, rx_ref, out_ref):
    total = nt(dq_ref[...], w_ref[:, :D]) + nt(dkv_ref[...], w_ref[:, D:])
    out_ref[...] = (total + from_slab(rx_ref[...])).astype(BF)


def exchange(x, axis, groups=None):
    return lax.all_to_all(x, axis, 0, 0, tiled=True, axis_index_groups=groups)


def swap(x):
    return lax.ppermute(x, "row", CORE_SWAP)


def after(value, *others):
    return lax.optimization_barrier((value, *others))[0]


def per_device(
    tokens, grad_out, w_qkv, w_out, gain, log_decay_rows, log_decay_cols, border_cols, border_rows
):
    place = lax.axis_index("col")
    at = place.astype(jnp.int32).reshape(1)
    core = (lax.axis_index("row") % 2).astype(jnp.int32).reshape(1)
    gain = gain.reshape(1, D)
    half = (SPLIT, TOK)
    load = ((8, LOAD, 128), BF)
    narrow = pltpu.VMEM((2, LOAD, 128), BF)

    x = tokens.reshape(TOK, D)
    g = grad_out.reshape(TOK, D)
    (first,) = call(layout_kernel, 2.0, [((16, 32, D), BF)], tokens, grad_out, keep=(0,))
    rx = exchange(first, "row")

    ldr = log_decay_rows.transpose(2, 0, 1, 3)
    ldc = log_decay_cols.swapaxes(2, 3).reshape(2, HEADS, TOK)
    tiles = jnp.concatenate([border_cols, jnp.zeros((COLS,), jnp.int32)]).reshape(9, COLS)
    bc = lax.dynamic_slice_in_dim(tiles, place, 2)
    br = jnp.broadcast_to(border_rows[:, None], (GRID_H, CD)).reshape(1, TOK)
    fac, th, kv, *updates = call(
        summary_kernel, 0.1,
        [((ROWS, COLS, 4 * HEADS), F32), ((2, 16, 128), F32), ((TOK, 2 * D), BF)] + [((LOAD, 128), BF)] * 7,
        at, ldr, bc, after(x, first), w_qkv, smem=(0,), near=(1, 2), scratch=[narrow], staged=True,
    )
    states = [
        lax.ppermute(u, "col", [(i, (i + n + 1) % 8) for i in range(8)]) for n, u in enumerate(updates)
    ]
    wr, wc = call(
        mask_kernel, 0.1,
        [((UNITS, 2 * COLS, COLS), BF), ((PAIRS, 2 * TOK, TOK), BF)],
        ldr, ldc, bc, br, th, near=(0, 1, 2, 3), staged=True,
    )
    q, inside, probs = call(
        row_inside_kernel, 0.1,
        [((TOK, D), BF), ((TOK, D), F32), ((UNITS, 2 * COLS, COLS), BF)],
        x, w_qkv, after(kv, states[0]), wr, staged=True,
    )
    qkv_c, col_out, probs_c = call(
        col_forward_kernel, 6.8,
        [((TOK, F), BF), ((TOK, D), BF), ((PAIRS, 2 * TOK, TOK), BF)],
        after(rx, states[0], states[1]), w_qkv, wc, near=(0,), staged=True,
    )
    row_out, out_swap, entering = call(
        row_join_kernel, 5.0,
        [((TOK, D), BF), ((16, 32, D), BF), ((2, STATE, 128), BF)],
        at, q, fac, inside, after(col_out, q), *states, smem=(0,), near=tuple(range(5, 12)), keep=(1,),
        scratch=[pltpu.VMEM((2, STATE, 128), F32)], staged=True,
    )
    dn, dn_c, x_keep, x_send, xc_keep, xc_send = call(
        side_kernel, 5.0,
        [((TOK, D), BF), ((TOK, D), BF), (half, BF), (half, BF), (half, BF), (half, BF)],
        core, after(x, entering), g, rx, w_out, smem=(0,),
    )
    x_far, g_far, xc_far = swap(x_send), swap(g), swap(xc_send)
    rx2 = exchange(out_swap, "row")
    rx2, x_far, g_far, xc_far = lax.optimization_barrier((rx2, x_far, g_far, xc_far))
    dm, adj = call(
        row_middle_kernel, 4.5,
        [((TOK, D), BF), load],
        at, rx2, row_out, dn, gain, q, fac, th, smem=(0,), near=(1, 4), keep=(1,), scratch=[narrow],
    )
    adj = exchange(adj, "col")
    dq, part, gd_part, n_keep, n_send = call(
        row_local_kernel, 8.9,
        [((TOK, D), BF), ((TOK, 2 * D), BF), ((2, 2 * HEADS, COLS), F32), ((SPLIT + D // 2, TOK), BF), ((SPLIT + D // 2, TOK), BF)],
        core, rx2, row_out, dn, gain, q, kv, dm, entering, wr, probs, fac, smem=(0,), near=(1, 4),
    )
    n_far, dq_far = swap(n_send), swap(dq)
    dqkv_c, gdc, tok_c = call(
        col_backward_kernel, 9.7,
        [((TOK, F), BF), ((2, HEADS, TOK), F32), ((TOK, D), BF)],
        after(rx2, dm), col_out, dn_c, gain, qkv_c, wc, probs_c, w_qkv, near=(0, 3),
    )
    dqkv_c_far = swap(dqkv_c)
    out_weight, gain_weight = call(
        weight_out_kernel, 0.1, [((D // 2, D), BF), ((SPLIT, 128), BF)], n_keep, n_far, g, g_far
    )
    adj, out_weight, dq_far = lax.optimization_barrier((adj, out_weight, dq_far))
    rx3 = exchange(tok_c.reshape(16, 16, D), "row")
    dkv, gdr = call(
        row_finish_kernel, 0.3,
        [((TOK, 2 * D), BF), ((2, 2 * HEADS, COLS), F32)],
        at, kv, entering, adj, fac, th, part, gd_part,
        smem=(0,), near=(3,), scratch=[pltpu.VMEM((2, STATE, 128), BF)], staged=True,
    )
    dkv_far = swap(dkv)
    (early,) = call(
        weight_early_kernel, 0.3,
        [((SPLIT, WIDE), BF)],
        x_keep, x_far, xc_keep, xc_far, after(dq, dkv), dq_far, dqkv_c, dqkv_c_far, out_weight, gain_weight,
        keep=(0,),
    )
    (wg,) = call(
        weight_late_kernel, 0.3,
        [((64, 8, WIDE), BF)],
        x_keep, x_far, dkv, dkv_far, early, near=(3, 4), keep=(0,), staged=True,
    )
    wg = exchange(after(wg, rx3), ("row", "col"), SAME_CORE)
    grad_qkv, grad_out_weight, grad_gain = call(
        weight_sum_kernel, 2.0, [((6, F), F32), ((6, D), F32), ((1, 6), F32)], wg, near=(0,)
    )
    (grad_tokens,) = call(token_kernel, 4.0, [((TOK, D), BF)], dq, dkv, w_qkv, rx3, near=(3,))
    gdr = gdr.reshape(2, ROWS, HEADS, COLS).swapaxes(1, 2)
    return (
        grad_tokens.reshape(ROWS, COLS, D),
        grad_qkv,
        grad_out_weight,
        grad_gain.reshape(6),
        gdr.astype(BF),
        gdc.astype(BF).reshape(2, HEADS, GRID_H, CD).swapaxes(2, 3),
    )


def solution(mesh):
    in_specs = (
        P("row", "col", None),
        P("row", "col", None),
        P(),
        P(),
        P(),
        P(None, None, "row", "col"),
        P(None, None, ("col", "row"), None),
        P(),
        P(),
    )
    out_specs = (
        P("row", "col", None),
        P(("row", "col"), None),
        P(("row", "col"), None),
        P(("row", "col")),
        P(None, None, "row", "col"),
        P(None, None, ("col", "row"), None),
    )
    return jax.shard_map(
        per_device, mesh=mesh, in_specs=in_specs, out_specs=out_specs, check_vma=False
    )
```
